32 devices in a mesh: section: 2 (over core), seq: 4 (over z), head: 4 (over y, x).
Axes of the slice: x: 2, y: 2, z: 4, core: 2. Of those that a mesh axis runs over, the one named last changes fastest.
Arguments:
- tokens: bfloat16 [2, 2048, 1536], P(None, 'seq'), may hold values from -6 to 6
- cotangent: bfloat16 [2, 2048, 1536], P(None, 'seq'), may hold values from -6 to 6
- rms_gain: bfloat16 [2, 1536], P('section'), may hold values from 0.5 to 1.5
- proj_gate: bfloat16 [2, 1536, 3072], P('section', None, 'head'), may hold values from -0.15625 to 0.15625
- proj_x: bfloat16 [2, 1536, 3072], P('section', None, 'head'), may hold values from -0.15625 to 0.15625
- proj_bc: bfloat16 [2, 1536, 2, 128], P('section', None, None, 'head'), may hold values from -0.15625 to 0.15625
- proj_step: bfloat16 [2, 1536, 48], P('section', None, 'head'), may hold values from -0.15625 to 0.15625
- conv_x: bfloat16 [2, 4, 3072], P('section', None, 'head'), may hold values from -3 to 3
- conv_x_bias: bfloat16 [2, 3072], P('section', 'head'), may hold values from -0.5 to 0.5
- conv_bc: bfloat16 [2, 4, 2, 128], P('section', None, None, 'head'), may hold values from -3 to 3
- conv_bc_bias: bfloat16 [2, 2, 128], P('section', None, 'head'), may hold values from -0.5 to 0.5
- step_bias: float32 [2, 48], P('section', 'head'), may hold values from -6 to -3
- decay_log: float32 [2, 48], P('section', 'head'), may hold values from -4 to 2
- skip_gain: float32 [2, 48], P('section', 'head'), may hold values from 0.5 to 1.5
- norm_gain: bfloat16 [2, 3072], P('section', 'head'), may hold values from 0.5 to 1.5
- proj_out: bfloat16 [2, 3072, 1536], P('section', 'head'), may hold values from -0.109375 to 0.109375
Outputs:
- hidden_out: float32 [2, 2, 2048, 1536], P('section', None, 'seq', 'head')
- grad_tokens: float32 [2, 2, 2048, 1536], P('section', None, 'seq', 'head')
- grad_rms_gain: float32 [2, 1536], P('section')
- grad_proj_gate: float32 [2, 1536, 3072], P('section', None, 'head')
- grad_proj_x: float32 [2, 1536, 3072], P('section', None, 'head')
- grad_proj_bc: float32 [2, 1536, 2, 128], P('section', None, None, 'head')
- grad_proj_step: float32 [2, 1536, 48], P('section', None, 'head')
- grad_conv_x: float32 [2, 4, 3072], P('section', None, 'head')
- grad_conv_x_bias: float32 [2, 3072], P('section', 'head')
- grad_conv_bc: float32 [2, 4, 2, 128], P('section', None, None, 'head')
- grad_conv_bc_bias: float32 [2, 2, 128], P('section', None, 'head')
- grad_step_bias: float32 [2, 48], P('section', 'head')
- grad_decay_log: float32 [2, 48], P('section', 'head')
- grad_skip_gain: float32 [2, 48], P('section', 'head')
- grad_norm_gain: float32 [2, 3072], P('section', 'head')
- grad_proj_out: float32 [2, 3072, 1536], P('section', 'head')
The draws below stay inside these ranges and needn't reach their ends.
All inputs are finite; a program needn't handle non-finite values.
Results may differ from the reference program's by a relative error of at most 0.04.
Values may be sent and summed in bfloat16 or wider, within the bound.
A program may use at most 256 MiB of HBM per device.

```python
from functools import partial
import jax
import jax.numpy as jnp
from jax import lax

D = 1536
H = 48
HP = 64
NS = 128
KW = 4
BLOCK = 256
PIECES = 2
DI = 3072
PIECE_TOK = 2048
N_SECTION = 2


def block_scale(stream_key, shape, shards, smallest, high):
    level = 1.0
    for dim, shards_of in shards:
        steps = jax.random.uniform(jax.random.fold_in(jax.random.fold_in(stream_key, 6), dim), (shards_of,), jnp.float32, smallest / len(shards), high / len(shards))
        level = level * jnp.repeat(jnp.exp(steps), shape[dim] // shards_of).reshape((-1,) + (1,) * (len(shape) - 1 - dim))
    return level


def normal_values(stream_key, extent, scale, bound, cuts=(), kind=jnp.bfloat16):
    values = jax.random.normal(stream_key, extent, jnp.float32) * scale
    if len(cuts) > 0:
        values = block_scale(stream_key, extent, cuts, -0.22, 0.18) * values
    return jnp.clip(values, min=-bound, max=bound).astype(kind)


def setup_inputs(seed: int = 0) -> dict:
    keys = jax.random.split(jax.random.key(seed), 17)
    tokens = normal_values(keys[0], (PIECES, PIECE_TOK, D), 1.0, 6.0, ((1, 4),))
    cotangent = normal_values(keys[1], (PIECES, PIECE_TOK, D), 1.0, 6.0, ((1, 4),))
    rms_gain = jnp.clip(1.0 + 0.1 * jax.random.normal(keys[2], (N_SECTION, D), jnp.float32), 0.5, 1.5).astype(jnp.bfloat16)
    proj_gate = normal_values(keys[3], (N_SECTION, D, DI), D ** -0.5, 0.15625, ((0, 2), (2, 4)))
    proj_x = normal_values(keys[4], (N_SECTION, D, DI), D ** -0.5, 0.15625, ((0, 2), (2, 4)))
    proj_bc = normal_values(keys[5], (N_SECTION, D, 2, NS), D ** -0.5, 0.15625, ((0, 2), (3, 4)))
    proj_step = normal_values(keys[6], (N_SECTION, D, H), D ** -0.5, 0.15625, ((0, 2), (2, 4)))
    conv_x = normal_values(keys[7], (N_SECTION, KW, DI), KW ** -0.5, 3.0, ((0, 2), (2, 4)))
    conv_x_bias = jnp.clip(jax.random.uniform(keys[8], (N_SECTION, DI), jnp.float32, -0.5, 0.5) * block_scale(keys[8], (N_SECTION, DI), ((0, 2), (1, 4)), -0.4, 0.0), -0.5, 0.5).astype(jnp.bfloat16)
    conv_bc = normal_values(keys[9], (N_SECTION, KW, 2, NS), KW ** -0.5, 3.0, ((0, 2), (3, 4)))
    conv_bc_bias = jnp.clip(jax.random.uniform(keys[10], (N_SECTION, 2, NS), jnp.float32, -0.5, 0.5) * block_scale(keys[10], (N_SECTION, 2, NS), ((0, 2), (2, 4)), -0.4, 0.0), -0.5, 0.5).astype(jnp.bfloat16)
    step_bias = jnp.clip(-6.0 + 3.0 * jax.random.uniform(keys[11], (N_SECTION, H), jnp.float32) ** block_scale(keys[11], (N_SECTION, H), ((0, 2), (1, 4)), -0.2, 0.2), -6.0, -3.0)
    decay_log = jnp.clip(-4.0 + 6.0 * jax.random.uniform(keys[12], (N_SECTION, H), jnp.float32) ** block_scale(keys[12], (N_SECTION, H), ((0, 2), (1, 4)), -0.2, 0.2), -4.0, 2.0)
    skip_gain = jnp.clip(0.5 + 1.0 * jax.random.uniform(keys[13], (N_SECTION, H), jnp.float32) ** block_scale(keys[13], (N_SECTION, H), ((0, 2), (1, 4)), -0.2, 0.2), 0.5, 1.5)
    norm_gain = jnp.clip(1.0 + 0.1 * jax.random.normal(keys[14], (N_SECTION, DI), jnp.float32), 0.5, 1.5).astype(jnp.bfloat16)
    proj_out = normal_values(keys[15], (N_SECTION, DI, D), DI ** -0.5, 0.109375, ((0, 2), (1, 4)))
    return dict(tokens=tokens, cotangent=cotangent, rms_gain=rms_gain, proj_gate=proj_gate, proj_x=proj_x, proj_bc=proj_bc, proj_step=proj_step, conv_x=conv_x, conv_x_bias=conv_x_bias, conv_bc=conv_bc, conv_bc_bias=conv_bc_bias, step_bias=step_bias, decay_log=decay_log, skip_gain=skip_gain, norm_gain=norm_gain, proj_out=proj_out)


EPSILON = 1e-05
PRECISE = lax.Precision.HIGHEST

@jax.custom_vjp
def low(v):
    return lax.optimization_barrier(v.astype(jnp.bfloat16)).astype(jnp.float32)

@jax.custom_vjp
def low_back(v):
    return v

def low_keep(v):
    return (low(v), None)

def low_pass(kept, grad):
    return (grad,)

def back_keep(v):
    return (v, None)

def back_low(kept, grad):
    return (low(grad),)
low.defvjp(low_keep, low_pass)
low_back.defvjp(back_keep, back_low)

def block_step(decay_rate, carry_state, blocks):
    inputs, step_rows, b_rows, c_rows = blocks
    log_decay = jnp.cumsum(step_rows * decay_rate[None, :], axis=0)
    places = jnp.arange(step_rows.shape[0])
    causal = (places[:, None] >= places[None, :])[:, :, None]
    spread = log_decay[:, None, :] - log_decay[None, :, :]
    weights = jnp.where(causal, jnp.exp(jnp.where(causal, spread, 0.0)), 0.0)
    scores = jnp.dot(c_rows, b_rows.T, precision=PRECISE)
    mixing = scores[:, :, None] * weights * step_rows[None, :, :]
    within = jnp.einsum('tsh,shp->thp', mixing, inputs, precision=PRECISE)
    carried = jnp.einsum('tn,hpn->thp', c_rows, carry_state, precision=PRECISE)
    outputs = within + jnp.exp(log_decay)[:, :, None] * carried
    tail_weight = jnp.exp(log_decay[-1][None, :] - log_decay) * step_rows
    update = jnp.einsum('shp,sn->hpn', tail_weight[:, :, None] * inputs, b_rows, precision=PRECISE)
    new_state = jnp.exp(log_decay[-1])[:, None, None] * carry_state + update
    return (new_state, outputs)

def split_blocks(array):
    return array.reshape((array.shape[0] // BLOCK, BLOCK) + array.shape[1:])

def state_space(inputs, step_rows, decay_rate, b_rows, c_rows, start_state):
    stepper = jax.checkpoint(partial(block_step, decay_rate))
    final_state, outputs = lax.scan(stepper, start_state, (split_blocks(inputs), split_blocks(step_rows), split_blocks(b_rows), split_blocks(c_rows)))
    return outputs.reshape(inputs.shape)

def causal_conv(padded, kernel, offset):
    tap_count = kernel.shape[0]
    length = padded.shape[0] - tap_count + 1
    summed = offset
    for tap_index in range(tap_count):
        summed = summed + kernel[tap_index] * padded[tap_index:tap_index + length]
    return jax.nn.silu(summed)

def mixer_layer(residual, rms_gain, proj_gate, proj_x, proj_bc, proj_step, conv_x, conv_x_bias, conv_bc, conv_bc_bias, step_bias, decay_log, skip_gain, norm_gain, proj_out):
    length = residual.shape[0]
    scale_rows = lax.rsqrt(lax.optimization_barrier(jnp.mean(residual * residual, axis=-1, keepdims=True)) + EPSILON)
    normed = low(residual * scale_rows * rms_gain)
    gate_pre = low_back(jnp.dot(normed, proj_gate, precision=PRECISE))
    x_proj = low_back(jnp.dot(normed, proj_x, precision=PRECISE))
    bc_proj = low_back(jnp.einsum('td,dcn->tcn', normed, proj_bc, precision=PRECISE))
    step_proj = low_back(jnp.dot(normed, proj_step, precision=PRECISE))
    x_conv = causal_conv(jnp.concatenate([jnp.zeros((KW - 1, x_proj.shape[1]), jnp.float32), x_proj]), conv_x, conv_x_bias)
    bc_conv = causal_conv(jnp.concatenate([jnp.zeros((KW - 1,) + bc_proj.shape[1:], jnp.float32), bc_proj]), conv_bc, conv_bc_bias)
    step_rows = jax.nn.softplus(step_proj + step_bias)
    decay_rate = -jnp.exp(decay_log)
    inputs = x_conv.reshape(length, H, HP)
    mixed = state_space(inputs, step_rows, decay_rate, bc_conv[:, 0], bc_conv[:, 1], jnp.zeros((H, HP, NS), jnp.float32))
    mixed = (mixed + skip_gain[None, :, None] * inputs).reshape(length, DI)
    gated = mixed * jax.nn.silu(gate_pre)
    normed_out = low(gated * lax.rsqrt(lax.optimization_barrier(jnp.mean(gated * gated, axis=-1, keepdims=True)) + EPSILON) * norm_gain)
    return residual + jnp.dot(normed_out, proj_out, precision=PRECISE)

def reference(tokens, cotangent, rms_gain, proj_gate, proj_x, proj_bc, proj_step, conv_x, conv_x_bias, conv_bc, conv_bc_bias, step_bias, decay_log, skip_gain, norm_gain, proj_out):
    weights = (rms_gain, proj_gate, proj_x, proj_bc, proj_step, conv_x, conv_x_bias, conv_bc, conv_bc_bias, step_bias, decay_log, skip_gain, norm_gain, proj_out)
    residual = tokens.reshape(PIECES * PIECE_TOK, D).astype(jnp.float32)
    results = []
    backers = []
    for section_index in range(N_SECTION):
        params = tuple((weight[section_index].astype(jnp.float32) for weight in weights))
        if section_index > 0:
            residual = low(results[-1])
        result, backer = jax.vjp(mixer_layer, residual, *params)
        results.append(result)
        backers.append(backer)
    upstream = cotangent.reshape(PIECES * PIECE_TOK, D).astype(jnp.float32)
    input_grads = [None] * N_SECTION
    weight_grads = [None] * N_SECTION
    for section_index in reversed(range(N_SECTION)):
        parts = backers[section_index](upstream)
        input_grads[section_index] = parts[0]
        weight_grads[section_index] = parts[1:]
        upstream = low(parts[0])
    shape_out = (N_SECTION, PIECES, PIECE_TOK, D)
    stacked = [jnp.stack([weight_grads[section_index][which] for section_index in range(N_SECTION)]) for which in range(len(weights))]
    return (jnp.stack(results).reshape(shape_out), jnp.stack(input_grads).reshape(shape_out), stacked[0], stacked[1], stacked[2], stacked[3], stacked[4], stacked[5], stacked[6], stacked[7], stacked[8], stacked[9], stacked[10], stacked[11], stacked[12], stacked[13])
```

```python
import functools

import jax
import jax.numpy as jnp
from jax import lax
from jax.experimental import pallas as pl
from jax.experimental.pallas import tpu as pltpu
from jax.sharding import PartitionSpec as P

F32, BF = jnp.float32, jnp.bfloat16
MESH = pl.DeviceIdType.MESH
EPS = 1e-05
Q = 128
LANES = 128
GROUP = 16
NN, NT, TN = ((1,), (0,)), ((1,), (1,)), ((0,), (0,))
VM, HB = pltpu.VMEM, pl.ANY


def dot(a, b, dims=NN):
    return lax.dot_general(a, b, (dims, ((), ())), preferred_element_type=F32)


def iota(shape, dim):
    return lax.broadcasted_iota(jnp.int32, shape, dim)


def split3(v):
    hi = v.astype(BF)
    rest = v - hi.astype(F32)
    mid = rest.astype(BF)
    return hi, mid, (rest - mid.astype(F32)).astype(BF)


def sum3(matrix, v, dims=NN):
    hi, mid, low = split3(v)
    return dot(matrix, hi, dims) + dot(matrix, mid, dims) + dot(matrix, low, dims)


def dot2(a, v, dims=NN):
    hi = v.astype(BF)
    return dot(a, hi, dims) + dot(a, (v - hi.astype(F32)).astype(BF), dims)


def silu_grad(v):
    sg = jax.nn.sigmoid(v)
    return sg * (1.0 + v * (1.0 - sg))


def fold(v):
    total = v[:, :LANES]
    for k in range(1, v.shape[1] // LANES):
        total = total + v[:, k * LANES : (k + 1) * LANES]
    return total


def to_row(v):
    return jnp.sum(jnp.transpose(fold(v)), axis=0, keepdims=True)


def to_col(row):
    return jnp.transpose(jnp.broadcast_to(row, (Q, Q)))[:, :1]


class Lay:
    def __init__(self, mesh_shape, rows, width, model, heads, local_state):
        self.sections, self.seqs, self.parts = mesh_shape
        self.rows, self.width, self.model, self.heads = rows, width, model, heads
        self.nb = rows // Q
        self.share = model // self.parts
        self.ls = local_state
        self.off = 2 * local_state
        self.hp = width // heads
        self.inner = width * self.parts
        self.state = local_state * self.parts

    def place(self):
        self.c = lax.axis_index("section")
        self.z = lax.axis_index("seq")
        self.q = lax.axis_index("head")

    def heads_peers(self):
        return [
            (k, (self.c, self.z, lax.rem(self.q + k, self.parts)))
            for k in range(1, self.parts)
        ]

    def seq_peers(self):
        return [(k, (self.c, lax.rem(self.z + k, self.seqs), self.q)) for k in range(1, self.seqs)]

    def sibling(self):
        return (1 - self.c, self.z, self.q)

    def next_run(self):
        last = self.z == self.seqs - 1
        return (
            jnp.where(last, 1 - self.c, self.c),
            jnp.where(last, 0, self.z + 1),
            self.q,
        )

    def prev_run(self):
        first = self.z == 0
        return (
            jnp.where(first, 1 - self.c, self.c),
            jnp.where(first, self.seqs - 1, self.z - 1),
            self.q,
        )


def meet(targets):
    barrier = pltpu.get_barrier_semaphore()
    for target in targets:
        pl.semaphore_signal(barrier, inc=1, device_id=target, device_id_type=MESH)
    pl.semaphore_wait(barrier, len(targets))


def column_and_heads(lay):
    column = [
        ((lay.c + s) % 2, lax.rem(lay.z + k, lay.seqs), lay.q)
        for s in range(2)
        for k in range(lay.seqs)
        if s or k
    ]
    return column + [target for _, target in lay.heads_peers()]


def remote(src, dst, send, recv, target):
    return pltpu.make_async_remote_copy(
        src_ref=src,
        dst_ref=dst,
        send_sem=send,
        recv_sem=recv,
        device_id=target,
        device_id_type=MESH,
    )


class SeqSum:
    def __init__(self, lay, pieces, sems):
        self.pieces, self.sems = pieces, sems
        z, n = lay.z, lay.seqs
        self.left = z < n // 2
        depth = jnp.where(self.left, z, n - 1 - z)
        self.outer = depth > 0
        self.middle = depth == n // 2 - 1
        self.inside = (lay.c, jnp.where(self.left, z + 1, z - 1), lay.q)
        self.outside = (lay.c, jnp.clip(jnp.where(self.left, z - 1, z + 1), 0, n - 1), lay.q)

    def pass_on(self, k, src):
        own, inner, result, rows = self.pieces[k]
        ssem, asem, tsem, _ = self.sems

        def to_middle():
            remote(src, result.at[rows], ssem.at[k], tsem.at[k], self.inside).start()

        def to_next():
            remote(src, inner.at[rows], ssem.at[k], asem.at[k], self.inside).start()

        pl.when(self.middle)(to_middle)
        pl.when(jnp.logical_not(self.middle))(to_next)

    def inward(self, k):
        own, inner, result, rows = self.pieces[k]
        ssem, asem, tsem, _ = self.sems

        @pl.when(self.outer)
        def _():
            remote(own.at[rows], inner.at[rows], ssem.at[k], asem.at[k], self.inside).wait_recv()
            inner[rows, :] = inner[rows, :] + own[rows, :]
            self.pass_on(k, inner.at[rows])

    def push(self, k):
        @pl.when(jnp.logical_not(self.outer))
        def _():
            own, _, _, rows = self.pieces[k]
            self.pass_on(k, own.at[rows])

    def outward(self, k):
        own, inner, result, rows = self.pieces[k]
        ssem, _, tsem, osem = self.sems

        def arrived():
            remote(own.at[rows], result.at[rows], ssem.at[k], tsem.at[k], self.inside).wait_recv()

        @pl.when(self.outer)
        def _():
            arrived()

            @pl.when(self.middle)
            def _():
                result[rows, :] = result[rows, :] + inner[rows, :]

            remote(result.at[rows], result.at[rows], osem.at[k], tsem.at[k], self.outside).start()

    def ending(self, k):
        own, inner, result, rows = self.pieces[k]
        ssem, _, tsem, _ = self.sems

        @pl.when(jnp.logical_not(self.outer))
        def _():
            remote(own.at[rows], result.at[rows], ssem.at[k], tsem.at[k], self.inside).wait_recv()

            @pl.when(self.middle)
            def _():
                result[rows, :] = result[rows, :] + own[rows, :]

    def finish(self):
        for k, (own, inner, result, rows) in enumerate(self.pieces):
            ssem, _, tsem, osem = self.sems
            remote(own.at[rows], result.at[rows], ssem.at[k], tsem.at[k], self.inside).wait_send()

            @pl.when(self.outer)
            def _():
                remote(
                    result.at[rows], result.at[rows], osem.at[k], tsem.at[k], self.outside
                ).wait_send()


class Pump:
    def __init__(self, seq_sum, done=None):
        self.sum, self.done = seq_sum, done
        self.ready = self.pushed = self.taken = self.given = self.ended = 0

    def end(self, k):
        self.sum.ending(k)
        if self.done is not None:
            self.done(k)

    def plan(self):
        steps = []

        def feed():
            while self.pushed < min(self.ready, self.taken + 2):
                steps.append((self.sum.push, self.pushed))
                self.pushed += 1

        feed()
        if self.taken < self.pushed:
            steps.append((self.sum.inward, self.taken))
            self.taken += 1
            feed()
        if self.given < self.taken - 1:
            steps.append((self.sum.outward, self.given))
            self.given += 1
        if self.ended < self.given - 2:
            steps.append((self.end, self.ended))
            self.ended += 1
        return steps

    def feed(self):
        while self.pushed < min(self.ready, self.taken + 2):
            self.sum.push(self.pushed)
            self.pushed += 1

    def tick(self):
        self.later()()

    def later(self):
        steps = self.plan()

        def act():
            for kind, piece in steps:
                kind(piece)

        return act

    def finish(self):
        while self.taken < self.ready:
            self.tick()
        while self.given < self.taken:
            self.sum.outward(self.given)
            self.given += 1
        while self.ended < self.given:
            self.end(self.ended)
            self.ended += 1
        self.sum.finish()


class Scan:
    def __init__(self, lay, forward, expm, v):
        self.lay, self.expm, self.v = lay, expm, v
        self.steps = max(lay.seqs - 1, 0).bit_length()
        assert 1 << self.steps == lay.seqs
        self.forward = forward
        self.u = lay.z if forward else lay.seqs - 1 - lay.z
        self.first = lay.c == (0 if forward else 1)

    def device(self, u):
        u = jnp.clip(u, 0, self.lay.seqs - 1)
        return (self.lay.c, u if self.forward else self.lay.seqs - 1 - u, self.lay.q)

    def row(self, chosen):
        total = jnp.ones((8, LANES), F32)
        for u in range(self.lay.seqs):
            z = u if self.forward else self.lay.seqs - 1 - u
            total = jnp.where(chosen(u), total * self.v.table[z], total)
        return expand(self.lay, self.expm[...], total)[:1, :]

    def copies(self, s, ahead, only=None):
        v = self.v
        src, dst = (v.main_s, v.main_r) if ahead else (v.back_s, v.back_r)
        send, recv = (v.scan_sem.at[0 if ahead else 2], v.scan_sem.at[1 if ahead else 3])
        out = []
        for t in range(1 << s) if only is None else (only,):
            u = self.u + 1 + t if ahead else self.u - 1 - t
            out.append(
                remote(src, dst.at[s], send.at[(1 << s) - 1 + t], recv.at[s], self.device(u))
            )
        return out

    def gives(self, s, ahead):
        place = self.u if ahead else self.lay.seqs - 1 - self.u
        return lax.rem(place, 2 << s) == (1 << s) - 1

    def takes(self, s, ahead):
        place = self.u if ahead else self.lay.seqs - 1 - self.u
        return lax.rem(place // (1 << s), 2) == 1

    def give(self, s):
        v = self.v

        @pl.when(self.gives(s, True))
        def _():
            own_decay = self.row(lambda u: u == self.u)
            v.main_s[...] = (v.enter[...] * own_decay + v.own_state[...]).astype(BF)
            for copy in self.copies(s, True):
                copy.start()

        @pl.when(self.first & self.gives(s, False))
        def _():
            v.back_s[...] = (v.rest[...] + v.own_state[...] * self.row(lambda u: u > self.u)).astype(BF)
            for copy in self.copies(s, False):
                copy.start()

    def start(self):
        v = self.v
        v.enter[...] = jnp.zeros(v.enter.shape, F32)
        v.rest[...] = jnp.zeros(v.rest.shape, F32)
        if self.steps:
            self.give(0)

    def advance(self, s):
        v = self.v

        @pl.when(self.takes(s, True))
        def _():
            self.copies(s, True, 0)[0].wait_recv()
            begin = (self.u // (1 << s)) * (1 << s)
            between = self.row(lambda u: (u >= begin) & (u < self.u))
            v.enter[...] += between * v.main_r[s].astype(F32)

        @pl.when(self.first & self.takes(s, False))
        def _():
            self.copies(s, False, 0)[0].wait_recv()
            v.rest[...] += v.back_r[s].astype(F32)

        if s + 1 < self.steps:
            self.give(s + 1)

    def hand_over(self):
        v = self.v
        self.total = remote(
            v.total_s, v.total_r, v.total_sem.at[0], v.total_sem.at[1], self.lay.sibling()
        )

        @pl.when(self.first)
        def _():
            own_decay = self.row(lambda u: u == self.u)
            after = self.row(lambda u: u > self.u)
            through = (v.enter[...] * own_decay + v.own_state[...]) * after
            v.total_s[...] = (through + v.rest[...]).astype(BF)
            self.total.start()

    def result(self):
        v = self.v

        @pl.when(jnp.logical_not(self.first))
        def _():
            self.total.wait_recv()
            v.enter[...] += self.row(lambda u: u < self.u) * v.total_r[...].astype(F32)

        pl.when(self.first)(self.total.wait_send)
        for s in range(self.steps):
            for ahead in (True, False):
                gives = self.gives(s, ahead)

                @pl.when(gives if ahead else self.first & gives)
                def _():
                    for copy in self.copies(s, ahead):
                        copy.wait_send()


def scan_scratch(lay, kinds):
    n, w, steps = lay.state, lay.width, max(lay.seqs - 1, 1).bit_length()
    dma = pltpu.SemaphoreType.DMA
    out = dict(
        table=VM((lay.seqs, 8, LANES), F32),
        own_state=VM((n, w), F32),
        enter=VM((n, w), F32),
        rest=VM((n, w), F32),
        main_s=VM((n, w), BF),
        back_s=VM((n, w), BF),
        total_s=VM((n, w), BF),
        table_sem=dma((2, max(lay.seqs - 1, 1))),
    )
    for kind in kinds:
        out[kind + "main_r"] = VM((steps, n, w), BF)
        out[kind + "back_r"] = VM((steps, n, w), BF)
        out[kind + "total_r"] = VM((n, w), BF)
        out[kind + "scan_sem"] = dma((4, max(lay.seqs - 1, 1)))
        out[kind + "total_sem"] = dma((2,))
    return out


def scan_refs(v, kind):
    shared = ["table", "own_state", "enter", "rest", "main_s", "back_s", "total_s"]
    own = ["main_r", "back_r", "total_r", "scan_sem", "total_sem"]
    refs = [getattr(v, name) for name in shared] + [getattr(v, kind + name) for name in own]
    return Names(shared + own, refs)


def share_table(lay, v):
    copies = [
        remote(v.table.at[lay.z], v.table.at[lay.z], v.table_sem.at[0, k - 1], v.table_sem.at[1, k - 1], to)
        for k, to in lay.seq_peers()
    ]
    for copy in copies:
        copy.start()
    return copies


class Names:
    def __init__(self, names, refs):
        assert len(names) == len(refs), (len(names), len(refs))
        self.__dict__.update(zip(names, refs))


def pieces_of(own, inner, result, count):
    size = own.shape[0] // count
    return [(own, inner, result, pl.ds(k * size, size)) for k in range(count)]


def expander(lay):
    lane = iota((LANES, lay.width), 0) - lay.off
    head = iota((LANES, lay.width), 1) // lay.hp
    hit = (lane >= 0) & (lane < 3 * GROUP) & (lax.rem(lane + GROUP * 8, GROUP) == head)
    return jnp.where(hit, 1.0, 0.0).astype(BF)


def expand(lay, exp_matrix, v):
    hi, mid, low = split3(v)
    lane = iota(v.shape, 1) - lay.off
    packed = jnp.where(
        lane < 0,
        0.0,
        jnp.where(
            lane < GROUP,
            hi.astype(F32),
            jnp.where(
                lane < 2 * GROUP, mid.astype(F32), jnp.where(lane < 3 * GROUP, low.astype(F32), 0.0)
            ),
        ),
    )
    return dot(packed.astype(BF), exp_matrix)


def head_sum(exp_matrix, v):
    hi, mid, low = split3(v)
    return dot(hi, exp_matrix, NT) + dot(mid, exp_matrix, NT) + dot(low, exp_matrix, NT)


def selectors(lay):
    shape = (lay.parts * LANES, 2 * lay.state)
    row, col = iota(shape, 0), iota(shape, 1)
    piece, lane = row // LANES, lax.rem(row, LANES)
    kind, n = col // lay.state, lax.rem(col, lay.state)
    want = kind * lay.ls + lax.rem(n, lay.ls)
    same = piece == n // lay.ls
    top = jnp.where(same & (lane == want), 1.0, 0.0).astype(BF)
    bottom = jnp.where(same & (lane == want + LANES // 2), 1.0, 0.0).astype(BF)
    return top, bottom


def tri(kind):
    row, col = iota((Q, Q), 0), iota((Q, Q), 1)
    hit = {"lower": row >= col, "upper": row <= col, "strict": row > col}[kind]
    return jnp.where(hit, 1.0, 0.0).astype(BF)


def block(i, size=Q, base=0):
    return pl.ds(pl.multiple_of(i * size + base, 8), size)


def conv_cat(ref, i):
    return ref[pl.ds(pl.multiple_of(i * Q + 8, 8), Q + 8), :]


def conv_pre(cat, kernel, bias):
    total = bias
    for k in range(4):
        total = total + kernel[k : k + 1, :] * cat[5 + k : 5 + k + Q, :]
    return total


def softplus(v):
    return jnp.maximum(v, 0.0) + jnp.log1p(jnp.exp(-jnp.abs(v)))


def params(lay, pk_ref, layer):
    pk = pk_ref[layer]
    w = lay.width
    out = dict(
        conv_x=pk[0:4, :],
        bias_x=pk[4:5, :],
        gain_out=pk[5:6, :],
        skip=pk[6:7, :],
        gain=jnp.concatenate([pk[7:8, :], pk[8:9, :]], axis=1)
        if lay.model == 2 * w
        else None,
        conv_sm=jnp.concatenate([pk[9:10, k * LANES : (k + 1) * LANES] for k in range(4)], axis=0),
        bias_sm=pk[9:10, 4 * LANES : 5 * LANES],
        step_bias=pk[10:11, 0:LANES],
        rate=pk[10:11, LANES : 2 * LANES],
    )
    return out


def decay_tile(cum, cum_t, lane, causal):
    diff = cum[:, lane : lane + 1] - cum_t[lane : lane + 1, :]
    return jnp.exp(jnp.where(causal, diff, -1e30))


def halves(v):
    lane = iota(v.shape, 1)
    left = lane < LANES // 2
    zero = jnp.zeros_like(v)
    return jnp.where(left, v, zero), jnp.where(left, zero, v)


class Load:
    def __init__(self, own, other, dst, sem, mine):
        self.mine = mine
        self.copies = [pltpu.make_async_copy(src, dst, sem) for src in (own, other)]

    def start(self):
        pl.when(self.mine)(self.copies[0].start)
        pl.when(jnp.logical_not(self.mine))(self.copies[1].start)

    def wait(self):
        self.copies[0].wait()


def forward(lay, v, p, resid, weights, ready, project):
    c, z, q = lay.c, lay.z, lay.q
    nb, w, n = lay.nb, lay.width, lay.state
    wsm, wx, wg = weights
    expm, normed, sm, xp, cums, bc = v.expm, v.normed, v.sm, v.xp, v.cums, v.bc
    scan = Scan(lay, True, expm, scan_refs(v, "f_"))
    counter = iter(range(16))

    def send(src, dst, target):
        at = next(counter)
        copy = remote(src, dst, v.fsend.at[at], v.frecv.at[at], target)
        copy.start()
        return copy

    @pl.loop(0, nb)
    def _(i):
        x = resid[block(i), :].astype(F32)
        scale = lax.rsqrt(jnp.mean(x * x, axis=1, keepdims=True) + EPS)
        normed[block(i), :] = (x * scale * p["gain"]).astype(BF)

    ready(0)
    sm[16:, :] = dot(normed[...], wsm[...])
    v.shs[...] = sm[lay.rows :, :].astype(BF)
    after = lay.next_run()
    halo_s = send(v.shs, v.shr, after)
    tables = run_decays(lay, v, p)
    ready(1)
    step_n = 256

    @pl.loop(0, w // step_n)
    def _(j):
        cols = pl.ds(pl.multiple_of(j * step_n, step_n), step_n)
        xp[16:, cols] = dot(normed[...], wx[:, cols])

    v.xhs[...] = xp[lay.rows :, :].astype(BF)
    halo_x = send(v.xhs, v.xhr, after)
    halo_s.wait()
    inside = jnp.where((c == 0) & (z == 0), 0.0, 1.0)
    sm[:16, :] = v.shr[...].astype(F32) * inside

    half = lay.rows // 2
    conv_rows = []
    for i in range(nb):
        pre = conv_pre(conv_cat(sm, i), p["conv_sm"], p["bias_sm"])
        conv_rows.append(pre * jax.nn.sigmoid(pre))
    top = jnp.concatenate(conv_rows[: nb // 2], axis=0)
    bottom = jnp.concatenate(conv_rows[nb // 2 :], axis=0)
    lane = iota(top.shape, 1)
    v.bcg[q] = jnp.where(lane < LANES // 2, top, pltpu.roll(bottom, LANES // 2, 1)).astype(BF)
    sends = [send(v.bcg.at[q], v.bcg.at[q], target) for _, target in lay.heads_peers()]
    halo_x.wait()
    xp[:16, :] = v.xhr[...].astype(F32) * inside

    @pl.loop(0, nb)
    def _(i):
        pre = conv_pre(conv_cat(xp, i), p["conv_x"], p["bias_x"])
        v.xc[block(i), :] = pre * jax.nn.sigmoid(pre)

    for copy in sends:
        copy.wait()
    pieces = jnp.concatenate([v.bcg[k] for k in range(lay.parts)], axis=1)
    sel_top, sel_bottom = selectors(lay)
    bc[:half, :] = dot(pieces, sel_top).astype(BF)
    bc[half:, :] = dot(pieces, sel_bottom).astype(BF)

    v.local[0] = jnp.zeros((n, w), F32)
    v.dpre[...] = jnp.zeros(v.dpre.shape, F32)
    state = None
    total = jnp.zeros((1, LANES), F32)
    for i in range(nb):
        rows = pl.ds(i * Q, Q)
        cum = cums[1, rows, :]
        last = cum[Q - 1 :, :]
        weight = jnp.exp(last - cum) * cums[0, rows, :]
        xw = (v.xc[rows, :] * expand(lay, expm[...], weight)).astype(BF)
        update = dot(bc[rows, :n], xw, TN)
        dec = expand(lay, expm[...], jnp.broadcast_to(jnp.exp(last), (8, LANES)))[:1, :]
        state = update if i == 0 else state * dec + update
        total = total + last
        if i < nb - 1:
            v.local[i + 1] = state
            v.dpre[8 * (i + 1) : 8 * (i + 2), :] = jnp.broadcast_to(total, (8, LANES))
    v.own_state[...] = state
    for copy in tables:
        copy.wait()
    scan.start()
    ready(2)

    @pl.loop(0, w // step_n)
    def _(j):
        cols = pl.ds(pl.multiple_of(j * step_n, step_n), step_n)
        v.gate[:, cols] = dot(normed[...], wg[:, cols])

    @pl.loop(0, nb)
    def _(i):
        if scan.steps > 1:
            pl.when(i == nb - 1)(functools.partial(scan.advance, 0))
        causal = iota((Q, Q), 0) >= iota((Q, Q), 1)
        cum = cums[1, block(i), :]
        cum_t = jnp.transpose(cum)
        scores = dot(bc[block(i), n:], bc[block(i), :n], NT)
        stepped = (v.xc[block(i), :] * expand(lay, expm[...], cums[0, block(i), :])).astype(BF)
        for pair in range(lay.heads // 2):
            cols = slice(pair * LANES, (pair + 1) * LANES)
            mixes = [
                (scores * decay_tile(cum, cum_t, lay.off + 2 * pair + e, causal)).astype(BF)
                for e in range(2)
            ]
            xl, xr = halves(stepped[:, cols])
            v.ysd[block(i), cols] = dot(
                jnp.concatenate(mixes, axis=1), jnp.concatenate([xl, xr], axis=0)
            )

    @pl.loop(0, nb)
    def _(i):
        v.nt[:, pl.ds(pl.multiple_of(i * Q, Q), Q)] = jnp.transpose(normed[block(i), :])

    for step in range(1 if scan.steps > 1 else 0, scan.steps):
        scan.advance(step)
    scan.hand_over()
    scan.result()
    start = v.enter[...]

    @pl.loop(0, nb)
    def _(i):
        cum = cums[1, block(i), :]
        dec = jnp.exp(v.dpre[pl.ds(pl.multiple_of(8 * i, 8), 8), :])
        full = v.local[i] + expand(lay, expm[...], dec)[:1, :] * start
        v.sin[i] = full
        carried = dot2(bc[block(i), n:], full) * expand(lay, expm[...], jnp.exp(cum))
        y = v.ysd[block(i), :] + carried
        v.ysd[block(i), :] = y
        g = v.gate[block(i), :]
        gated = (y + p["skip"] * v.xc[block(i), :]) * (g * jax.nn.sigmoid(g))
        row = to_row(gated * gated)
        v.sqb[q, pl.ds(pl.multiple_of(8 * i, 8), 8), :] = jnp.broadcast_to(row, (8, Q))
        v.go[block(i), :] = (gated * p["gain_out"]).astype(BF)

    squares = [send(v.sqb.at[q], v.sqb.at[q], target) for _, target in lay.heads_peers()]
    ready(3)
    project()
    for copy in squares:
        copy.wait()
    total_sq = v.sqb[0]
    for k in range(1, lay.parts):
        total_sq = total_sq + v.sqb[k]
    v.sqt[...] = total_sq


def run_decays(lay, v, p):
    lower = tri("lower")
    lasts = []
    for i in range(lay.nb):
        rows = pl.ds(i * Q, Q)
        step = softplus(v.sm[16 + i * Q : 16 + (i + 1) * Q, :] + p["step_bias"])
        v.cums[0, rows, :] = step
        cum = sum3(lower, step * p["rate"])
        v.cums[1, rows, :] = cum
        lasts.append(cum[Q - 1 :, :])
    v.table[lay.z] = jnp.broadcast_to(jnp.exp(sum(lasts)), (8, LANES))
    return share_table(lay, v)


def kept_shapes(lay):
    r, w, m, n = lay.rows, lay.width, lay.model, lay.state
    return dict(
        nt=((m, r), BF),
        gate=((r, w), F32),
        xp=((r + 16, w), F32),
        sm=((r + 16, LANES), F32),
        ysd=((r, w), F32),
        sin=((lay.nb, n, w), F32),
        bc=((r, 2 * n), BF),
        sqt=((8 * lay.nb, Q), F32),
    )


def fwd_scratch(lay):
    r, w = lay.rows, lay.width
    dma = pltpu.SemaphoreType.DMA
    n_sem = 2 + 2 * (lay.parts - 1)
    return dict(
        xhs=VM((16, w), BF),
        xhr=VM((16, w), BF),
        shs=VM((16, LANES), BF),
        shr=VM((16, LANES), BF),
        bcg=VM((lay.parts, r // 2, LANES), BF),
        dpre=VM((8 * lay.nb, LANES), F32),
        sqb=VM((lay.parts, 8 * lay.nb, Q), F32),
        fsend=dma((n_sem,)),
        frecv=dma((n_sem,)),
    )


START_SMALL = ["conv_x", "bias_x", "gain_out", "rms", "conv_sm", "bias_sm"]
START_HEADS = ["step_bias", "decay", "skip"]


def start_ins():
    return ["tokens"] + [f"own{k}" for k in range(4)] + START_SMALL + START_HEADS


def start_outs(lay):
    r, w, m = lay.rows, lay.width, lay.model
    sds = jax.ShapeDtypeStruct
    out = {name: sds(*spec) for name, spec in kept_shapes(lay).items()}
    out.update(
        pk=sds((2, 16, w), F32),
        hid=sds((r, lay.share), F32),
        full=sds((r, m), BF),
        other0=sds((m, w), BF),
        other1=sds((m, w), BF),
        other2=sds((m, LANES), BF),
        other3=sds((w, m), BF),
    )
    return out


def start_scratch(lay):
    r, w, m, n = lay.rows, lay.width, lay.model, lay.state
    dma = pltpu.SemaphoreType.DMA
    peers = lay.parts - 1
    out = dict(
        resid=VM((r, m), BF),
        wg=VM((2, m, w), BF),
        wx=VM((2, m, w), BF),
        wsm=VM((2, m, LANES), BF),
        wo=VM((2, w, m), BF),
        expm=VM((LANES, w), BF),
        normed=VM((r, m), BF),
        xc=VM((r, w), F32),
        cums=VM((2, r, LANES), F32),
        go=VM((r, w), BF),
        local=VM((lay.nb, n, w), F32),
        tmp=VM((16, LANES), F32),
        part=VM((lay.parts, r, lay.share), BF),
        got=VM((peers, r, lay.share), BF),
        wsem=dma((5,)),
        psem=dma((9,)),
        vsem=dma((5,)),
        rs_send=dma((peers, lay.nb)),
        rs_recv=dma((peers, lay.nb)),
        ag_send=dma((peers, lay.nb)),
        ag_recv=dma((peers, lay.nb)),
    )
    out.update(fwd_scratch(lay))
    out.update(scan_scratch(lay, ["f_"]))
    return out


def pack(lay, v):
    c, w, heads, off = lay.c, lay.width, lay.heads, lay.off
    f = lambda ref: ref[...].astype(F32)
    v.tmp[...] = jnp.zeros(v.tmp.shape, F32)
    v.tmp[0:4, :off] = f(v.conv_sm)
    v.tmp[4:5, :off] = f(v.bias_sm)
    v.tmp[8:9, :heads] = v.step_bias[...]
    v.tmp[9:10, :heads] = -jnp.exp(v.decay[...])
    v.tmp[10:11, :heads] = v.skip[...]
    rows = v.tmp[8:16, :]
    groups = rows * 0.0
    for k in range(3):
        groups = groups + pltpu.roll(rows, off + k * GROUP, 1)
    v.pk[c] = jnp.zeros((16, w), F32)
    v.pk[c, 0:4, :] = f(v.conv_x)
    v.pk[c, 4:5, :] = f(v.bias_x)
    v.pk[c, 5:6, :] = f(v.gain_out)
    v.pk[c, 6:7, :] = expand(lay, v.expm[...], groups)[2:3, :]
    rms = f(v.rms)
    for k in range(lay.model // w):
        v.pk[c, 7 + k : 8 + k, :] = rms[:, k * w : (k + 1) * w]
    for k in range(5):
        v.pk[c, 9:10, k * LANES : (k + 1) * LANES] = v.tmp[k : k + 1, :]
    for k in range(2):
        v.pk[c, 10:11, k * LANES : (k + 1) * LANES] = groups[k : k + 1, :]


def start_kernel(lay, *refs):
    v = Names(start_ins() + list(start_outs(lay)) + list(start_scratch(lay)), refs)
    lay.place()
    c, q, nb = lay.c, lay.q, lay.nb
    both, own_w = (v.wg, v.wx, v.wsm, v.wo), (v.own0, v.own1, v.own2, v.own3)
    kept_w = (v.other0, v.other1, v.other2, v.other3)
    order = (2, 1, 0, 3)
    loads = [pltpu.make_async_copy(v.tokens.at[c], v.resid, v.wsem.at[4])]
    loads += [
        pltpu.make_async_copy(own_w[k], both[k].at[c], v.wsem.at[at]) for at, k in enumerate(order)
    ]
    for load in loads:
        load.start()
    v.expm[...] = expander(lay)
    pack(lay, v)
    meet(column_and_heads(lay))
    swaps = [remote(v.pk.at[c], v.pk.at[c], v.psem.at[4], v.vsem.at[4], lay.sibling())]
    swaps += [
        remote(own_w[k], both[k].at[c], v.psem.at[at], v.vsem.at[at], lay.sibling())
        for at, k in enumerate(order)
    ]
    for copy in swaps:
        copy.start()
    keeps = [
        pltpu.make_async_copy(both[k].at[1 - c], kept_w[k], v.psem.at[5 + at])
        for at, k in enumerate(order)
    ]
    wg, wx, wsm, wo = (ref.at[0] for ref in both)
    swaps[0].wait()
    loads[0].wait()

    def ready(at):
        loads[1 + at].wait()
        swaps[1 + at].wait()
        keeps[at].start()

    peers = lay.heads_peers()
    chunks = [[] for _ in range(nb)]

    def project():
        for k, target in peers + [(0, None)]:
            owner = lax.rem(q + k, lay.parts)
            cols = pl.ds(pl.multiple_of(owner * lay.share, LANES), lay.share)
            v.part[k] = dot(v.go[...], wo[:, cols]).astype(BF)
            if k == 0:
                continue
            for i in range(nb):
                rows = pl.ds(i * Q, Q)
                copy = remote(
                    v.part.at[k, rows],
                    v.got.at[k - 1, rows],
                    v.rs_send.at[k - 1, i],
                    v.rs_recv.at[k - 1, i],
                    target,
                )
                copy.start()
                chunks[i].append(copy)

    p = params(lay, v.pk, 0)
    forward(lay, v, p, v.resid, (wsm, wx, wg), ready, project)
    cols = pl.ds(pl.multiple_of(q * lay.share, LANES), lay.share)
    given = []
    for i in range(nb):
        rows = pl.ds(i * Q, Q)
        for copy in chunks[i]:
            copy.wait()
        total = v.part[0, rows, :].astype(F32)
        for k, _ in peers:
            total = total + v.got[k - 1, rows, :].astype(F32)
        row = v.sqt[8 * i : 8 * i + 1, :]
        value = v.resid[rows, cols].astype(F32) + to_col(lax.rsqrt(row / lay.inner + EPS)) * total
        v.hid[rows, :] = value
        v.full[rows, cols] = value.astype(BF)
        for k, target in peers:
            copy = remote(
                v.full.at[rows, cols],
                v.full.at[rows, cols],
                v.ag_send.at[k - 1, i],
                v.ag_recv.at[k - 1, i],
                target,
            )
            copy.start()
            given.append(copy)
    for copy in given + keeps:
        copy.wait()


def start_layer(lay, *args):
    outs, scratch = start_outs(lay), start_scratch(lay)
    vmem, hbm = pl.BlockSpec(memory_space=VM), pl.BlockSpec(memory_space=HB)
    got = pl.pallas_call(
        functools.partial(start_kernel, lay),
        out_shape=tuple(outs.values()),
        in_specs=[hbm] * 5 + [vmem] * (len(args) - 5),
        out_specs=tuple([vmem] * (len(outs) - 4) + [hbm] * 4),
        scratch_shapes=list(scratch.values()),
        compiler_params=pltpu.CompilerParams(
            collective_id=1, has_side_effects=True, vmem_limit_bytes=58 << 20
        ),
        name="mixer_start",
    )(*args)
    return Names(list(outs), got)


EARLIER = ["prev_x", "prev_s", "done_o", "done_g", "done_x", "small", "hid0", "hid1", "gt1"]
EARLIER_HBM = 3
X_EARLY = 2


def back_ins(lay, more):
    weights = [f"own{k}" for k in range(4)] + [f"other{k}" for k in range(4)]
    if more:
        return ["up", "tokens"] + list(kept_shapes(lay)) + weights + ["pk"] + EARLIER
    return ["cotangent", "resid"] + weights + ["pk"]


def back_outs(lay, late, gather, more):
    r, w, m = lay.rows, lay.width, lay.model
    sds = jax.ShapeDtypeStruct
    out = dict(gt=sds((r, lay.share), F32))
    if more:
        out["total"] = sds((16 + 8 * lay.parts, w), F32)
    else:
        out.update(
            sum_o=sds((w // 2, m), BF),
            sum_g=sds((m // 2, w), BF),
            sum_x=sds((m // 2 // N_X * X_EARLY, w), BF),
            rest_x=sds((m // 2 - m // 2 // N_X * X_EARLY, w), BF),
            own_s=sds((m // 2, LANES), BF),
            psm=sds((16, w), F32),
        )
    if gather:
        out["full"] = sds((r, m), BF)
    if late:
        out["hid"] = sds((r, lay.share), F32)
    if more:
        out.update(
            fin_o=sds((w, m), BF),
            fin_g=sds((m, w), BF),
            fin_x=sds((m, w), BF),
            fin_s=sds((m, LANES), BF),
            got_hid=sds((r, lay.share), F32),
            got_gt=sds((r, lay.share), F32),
        )
    return out


N_OUT = N_GATE = N_X = 4


def back_scratch(lay, late, gather, more):
    r, w, m, n, nb = lay.rows, lay.width, lay.model, lay.state, lay.nb
    dma = pltpu.SemaphoreType.DMA
    peers = lay.parts - 1
    n_sem = 2 * peers + 2 + 4 + peers
    n_seq = N_OUT + N_GATE + (2 * (N_X + 1) - X_EARLY if more else X_EARLY)
    out = dict(
        wg=VM((m, w), BF),
        wx=VM((m, w), BF),
        wsm=VM((m, LANES), BF),
        wo=VM((w, m), BF),
        expm=VM((LANES, w), BF),
        xc=VM((r, w), F32),
        dy=VM((r, w), F32),
        dx=VM((r, w), F32),
        cums=VM((2, r, LANES), F32),
        rcs=VM((r, LANES), F32),
        lowg=VM((r, w), BF),
        lowx=VM((r, w), BF),
        lowsm=VM((r, LANES), BF),
        no=VM((r, w), BF),
        rsb=VM((lay.parts, 8 * nb, Q), F32),
        lamloc=VM((nb, n, w), F32),
        dsuf=VM((8 * nb, LANES), F32),
        dbc=VM((r, 2 * n), F32),
        dbs=VM((lay.parts, r // 2, LANES), BF),
        dbr=VM((peers, r // 2, LANES), BF),
        xdp=VM((r + 16, w), F32),
        smdp=VM((r + 16, LANES), F32),
        hxs=VM((16, w), BF),
        hxr=VM((16, w), BF),
        hss=VM((16, LANES), BF),
        hsr=VM((16, LANES), BF),
        dsp=VM((r, LANES), F32),
        gr_g=VM((m // 2, w), BF),
        gr_x=VM((m // 2, w), BF),
        gs_o=VM((w // 2, m), BF),
        gr_o=VM((w // 2, m), BF),
        gs_s=VM((m // 2, LANES), BF),
        gr_s=VM((m // 2, LANES), BF),
        rdacc=VM((r, LANES), F32),
        acch=VM((8, LANES), F32),
        own_o=VM((w // 2, m), BF),
        own_g=VM((m // 2, w), BF),
        in_o=VM((w // 2, m), BF),
        in_g=VM((m // 2, w), BF),
        in_x=VM((m // 2, w), BF),
        dnp=VM((lay.parts, r, lay.share), BF),
        got=VM((peers, r, lay.share), BF),
        rd2=VM((8 * nb, Q), F32),
        got_rows=VM((peers, 8 * nb, Q), F32),
        gains=VM((8, m), F32),
        wsem=dma((5,)),
        ssem=dma((n_sem,)),
        rsem=dma((n_sem,)),
        rs_send=dma((peers, nb)),
        rs_recv=dma((peers, nb)),
        seq1=dma((n_seq,)),
        seq2=dma((n_seq,)),
        seq3=dma((n_seq,)),
        seq4=dma((n_seq,)),
    )
    if gather:
        out.update(ag_send=dma((peers, nb)), ag_recv=dma((peers, nb)))
    out["own_x"] = VM((m // 2, w), BF)
    if more:
        for kind in ("in_s", "in_ps", "own_s", "sum_s", "sum_ps"):
            out[kind] = VM((m // 2, LANES), BF)
        for kind in ("sum_x", "sum_g"):
            out[kind] = VM((m // 2, w), BF)
        for kind in ("in_px", "sum_px"):
            out[kind] = VM((m // 2 - m // 2 // N_X * X_EARLY, w), BF)
        column = 2 * lay.seqs
        out.update(
            sum_o=VM((w // 2, m), BF),
            psm=VM((16, w), F32),
            slots=VM((column, 16, w), F32),
            rest_rows=VM((lay.parts, 8, w), F32),
            fin_sem=dma((3, n_seq + 3)),
            pair_sem=dma((2, 2)),
            slot_sem=dma((2, column - 1)),
            part_sem=dma((2, peers)),
        )
        out["resid"] = VM((r, m), BF)
    out.update(scan_scratch(lay, ["b_"] if more else ["f_", "b_"]))
    if late:
        out.update(
                late_got=VM((peers, r, lay.share), BF),
            late_send=dma((peers,)),
            late_recv=dma((peers,)),
            up=VM((r, m), BF),
        )
        out.update({name: VM(*spec) for name, spec in kept_shapes(lay).items()})
        out.update(fwd_scratch(lay))
    return out


def bwd_kernel(lay, layer, late, gather, more, *refs):
    outs, scratch = back_outs(lay, late, gather, more), back_scratch(lay, late, gather, more)
    v = Names(back_ins(lay, more) + list(outs) + list(scratch), refs)
    lay.place()
    c, z, q = lay.c, lay.z, lay.q
    nb, w, n, m = lay.nb, lay.width, lay.state, lay.model
    half = lay.rows // 2
    own_w, other_w = (v.own0, v.own1, v.own2, v.own3), (v.other0, v.other1, v.other2, v.other3)
    loads = [
        Load(own_w[k], other_w[k], (v.wg, v.wx, v.wsm, v.wo)[k], v.wsem.at[at], c == layer)
        for at, k in enumerate((3, 0, 1, 2) if more else (2, 1, 0, 3))
    ]
    if more:
        rows_in = pltpu.make_async_copy(v.tokens.at[c], v.resid, v.wsem.at[4])
    else:
        rows_in = pltpu.make_async_copy(v.cotangent.at[c], v.up, v.wsem.at[4])
    for load in loads + [rows_in]:
        load.start()
    meet(column_and_heads(lay))
    peers = lay.heads_peers()
    counter = iter(range(64))

    def send(src, dst, target):
        at = next(counter)
        copy = remote(src, dst, v.ssem.at[at], v.rsem.at[at], target)
        copy.start()
        return copy

    out_pieces = pieces_of(v.own_o, v.in_o, v.sum_o, N_OUT)
    gate_pieces = pieces_of(v.own_g, v.in_g, v.sum_g, N_GATE)
    finals = []

    def plan_settling(ref, fin, of, rows, skipped=0):
        size = ref.shape[0] if rows is None else rows.size
        offset = skipped + (0 if rows is None else rows.start)
        at = len(finals)
        into = fin.at[pl.ds(pl.multiple_of(c * (fin.shape[0] // 2) + offset, 16), size)]
        src = ref if rows is None else ref.at[rows]
        here = pltpu.make_async_copy(src, into, v.fin_sem.at[0, at])
        there = remote(src, into, v.fin_sem.at[1, at], v.fin_sem.at[2, at], lay.sibling())
        finals.append((of, here, there))

    def settle(at):
        of, here, there = finals[at]
        pl.when(c == of)(here.start)
        pl.when(c != of)(there.start)

    if more:
        kinds = [(pieces_of(v.prev_x, v.in_px, v.sum_px, N_X - X_EARLY), v.fin_x, 1)]
        kinds += [(pieces_of(v.prev_s, v.in_ps, v.sum_ps, 1), v.fin_s, 1)]
        kinds += [(out_pieces, v.fin_o, 0), (gate_pieces, v.fin_g, 0)]
        kinds += [(pieces_of(v.own_x, v.in_x, v.sum_x, N_X), v.fin_x, 0)]
        kinds += [(pieces_of(v.own_s, v.in_s, v.sum_s, 1), v.fin_s, 0)]
        listed = [(piece, fin, of) for pieces, fin, of in kinds for piece in pieces]

        for (_, _, result, rows), fin, of in listed:
            skipped = m // 2 // N_X * X_EARLY if result is v.sum_px else 0
            plan_settling(result, fin, of, rows, skipped)
        done = settle
        plan_settling(v.done_o, v.fin_o, 1, None)
        plan_settling(v.done_g, v.fin_g, 1, None)
        plan_settling(v.done_x, v.fin_x, 1, None)
        for at in range(len(listed), len(finals)):
            settle(at)
        pairs = [
            [
                remote(src, dst, v.pair_sem.at[0, k], v.pair_sem.at[1, k], lay.sibling())
                for src in srcs
            ]
            for k, (dst, srcs) in enumerate(
                ((v.got_hid, (v.hid1, v.hid0)), (v.got_gt, (v.gt1, v.gt)))
            )
        ]
        pl.when(c == 0)(pairs[0][0].start)
        pl.when(c == 1)(pairs[0][1].start)
        pl.when(c == 0)(pairs[1][0].start)
    else:
        x_pieces = pieces_of(v.own_x, v.in_x, v.sum_x, N_X)[:X_EARLY]
        listed = [(piece,) for piece in out_pieces + gate_pieces + x_pieces]
        done = None
    pump = Pump(
        SeqSum(lay, [entry[0] for entry in listed], (v.seq1, v.seq2, v.seq3, v.seq4)), done
    )
    tick = pump.tick
    scan = Scan(lay, False, v.expm, scan_refs(v, "b_"))
    if more:
        pump.ready += N_X - X_EARLY + 1
        pump.feed()

    p = params(lay, v.pk, layer)
    v.expm[...] = expander(lay)
    expm = v.expm
    v.psm[...] = jnp.zeros(v.psm.shape, F32)
    v.acch[...] = jnp.zeros(v.acch.shape, F32)
    lower, upper, strict = tri("lower"), tri("upper"), tri("strict")
    col_n = 256

    def cols_at(j, size=col_n):
        return pl.ds(pl.multiple_of(j * size, LANES), size)

    def tile(i):
        return pl.ds(pl.multiple_of(8 * i, 8), 8)

    def weight_grad(left, low, theirs, got, own):
        width = low.shape[1]
        step_n = min(width, col_n)
        for side, into in ((1 - c, theirs), (c, own)):
            rows = left(side)

            @pl.loop(0, width // step_n)
            def _(j):
                at = cols_at(j, step_n)
                into[:, at] = dot(rows, low[:, at]).astype(BF)

            if into is theirs:
                copy = send(theirs, got, lay.sibling())
        return copy

    def pair_sum(copy, own, got):
        copy.wait()
        own[...] = (own[...].astype(F32) + got[...].astype(F32)).astype(BF)

    def normed_half(side):
        return v.nt[pl.ds(pl.multiple_of(side * (m // 2), 16), m // 2), :]

    def out_half(side):
        return jnp.transpose(v.no[:, pl.ds(pl.multiple_of(side * (w // 2), LANES), w // 2)])

    late_sums = []

    def project():
        for k in range(lay.parts):
            cols = slice(k * lay.share, (k + 1) * lay.share)
            v.dnp[k] = dot(v.go[...], v.wo[:, cols]).astype(BF)

    if more:
        tables = run_decays(lay, v, p)
    else:
        v.normed, v.go, v.local = v.full, v.lowx, v.lamloc
        weights = (v.wsm, v.wx, v.wg)
        forward(lay, v, p, v.resid, weights, lambda at: loads[at].wait(), project)
        tables = []

    @pl.loop(0, nb)
    def _(i):
        if more:
            pre = conv_pre(conv_cat(v.xp, i), p["conv_x"], p["bias_x"])
            v.xc[block(i), :] = pre * jax.nn.sigmoid(pre)
        x = v.xc[block(i), :]
        g = v.gate[block(i), :]
        gated = (v.ysd[block(i), :] + p["skip"] * x) * (g * jax.nn.sigmoid(g))
        inv = to_col(lax.rsqrt(v.sqt[tile(i), :][:1, :] / lay.inner + EPS))
        v.no[block(i), :] = (gated * inv * p["gain_out"]).astype(BF)

    rows_in.wait()
    if more:
        tick()
    copy_o = weight_grad(out_half, v.up, v.gs_o, v.gr_o, v.own_o)
    if more:
        loads[0].wait()

    @pl.loop(0, w // col_n)
    def _(j):
        v.dy[:, cols_at(j)] = dot(v.up[...], v.wo[cols_at(j), :], NT)

    @pl.loop(0, nb)
    def _(i):
        g = v.gate[block(i), :]
        gated = (v.ysd[block(i), :] + p["skip"] * v.xc[block(i), :]) * (g * jax.nn.sigmoid(g))
        row = to_row(v.dy[block(i), :] * p["gain_out"] * gated)
        v.rsb[q, tile(i), :] = jnp.broadcast_to(row, (8, Q))

    row_sends = [send(v.rsb.at[q], v.rsb.at[q], target) for _, target in peers]
    pair_sum(copy_o, v.own_o, v.gr_o)
    pump.ready += N_OUT
    if more:
        tick()
    pump.feed()
    for copy in row_sends:
        copy.wait()
    if late:
        for k, target in peers:
            copy = remote(
                v.dnp.at[lax.rem(q + k, lay.parts)],
                v.late_got.at[k - 1],
                v.late_send.at[k - 1],
                v.late_recv.at[k - 1],
                target,
            )
            copy.start()
            late_sums.append(copy)
    @pl.loop(0, nb)
    def _(i):
        rd = v.rsb[0, tile(i), :]
        for k in range(1, lay.parts):
            rd = rd + v.rsb[k, tile(i), :]
        inv = to_col(lax.rsqrt(v.sqt[tile(i), :][:1, :] / lay.inner + EPS))
        rdc = to_col(rd[:1, :])
        g, x, d = v.gate[block(i), :], v.xc[block(i), :], v.dy[block(i), :]
        sg = jax.nn.sigmoid(g)
        act = g * sg
        mixed = v.ysd[block(i), :] + p["skip"] * x
        gated = mixed * act
        v.psm[5:6, :] += jnp.sum(d * (gated * inv), axis=0, keepdims=True)
        dgated = inv * p["gain_out"] * d - gated * (inv * inv * inv * rdc / lay.inner)
        dmix = dgated * act
        v.lowg[block(i), :] = (dgated * mixed * (sg * (1.0 + g * (1.0 - sg)))).astype(BF)
        v.psm[8:9, :] += jnp.sum(dmix * x, axis=0, keepdims=True)
        v.dy[block(i), :] = dmix

    lam = jnp.zeros((n, w), F32)
    total = jnp.zeros((1, LANES), F32)
    for i in reversed(range(nb)):
        rows = pl.ds(i * Q, Q)
        cum = v.cums[1, rows, :]
        last = cum[Q - 1 :, :]
        v.lamloc[i] = lam
        v.dsuf[8 * i : 8 * (i + 1), :] = jnp.broadcast_to(total, (8, LANES))
        faded = (expand(lay, expm[...], jnp.exp(cum)) * v.dy[rows, :]).astype(BF)
        dec = expand(lay, expm[...], jnp.broadcast_to(jnp.exp(last), (8, LANES)))[:1, :]
        lam = lam * dec + dot(v.bc[rows, n:], faded, TN)
        total = total + last
    v.own_state[...] = lam
    for copy in tables:
        copy.wait()
    scan.start()

    copy_g = weight_grad(
        normed_half, v.lowg, v.wo.at[:, :w], v.gr_g, v.own_g
    )
    pair_sum(copy_g, v.own_g, v.gr_g)
    pump.ready += N_GATE
    tick()

    in_loop = pump.later() if more else None

    @pl.loop(0, nb)
    def _(i):
        if scan.steps > 1:
            pl.when(i == 2)(functools.partial(scan.advance, 0))
        if more:
            pl.when(i == 3)(in_loop)
        causal = iota((Q, Q), 0) >= iota((Q, Q), 1)
        cum = v.cums[1, block(i), :]
        cum_t = jnp.transpose(cum)
        b_rows, c_rows = v.bc[block(i), :n], v.bc[block(i), n:]
        scores = dot(c_rows, b_rows, NT)
        stepped = (v.xc[block(i), :] * expand(lay, expm[...], v.cums[0, block(i), :])).astype(BF)
        grad = v.dy[block(i), :]
        low = grad.astype(BF)
        dscores = jnp.zeros((Q, Q), F32)
        for pair in range(lay.heads // 2):
            cols = slice(pair * LANES, (pair + 1) * LANES)
            fades = [decay_tile(cum, cum_t, lay.off + 2 * pair + e, causal) for e in range(2)]
            mixes = [(scores * fade).astype(BF) for fade in fades]
            xl, xr = halves(stepped[:, cols])
            dl, dr = halves(low[:, cols])
            dmix = dot(low[:, cols], jnp.concatenate([xl, xr], axis=0), NT)
            dscores = dscores + dmix[:, :Q] * fades[0] + dmix[:, Q:] * fades[1]
            v.dx[block(i), cols] = dot(
                jnp.concatenate(mixes, axis=0), jnp.concatenate([dl, dr], axis=0), TN
            )
        diff = low.astype(F32) * v.ysd[block(i), :] - stepped.astype(F32) * v.dx[block(i), :]
        v.rcs[block(i), :] = sum3(upper, head_sum(expm[...], diff))
        faded = (expand(lay, expm[...], jnp.exp(cum)) * grad).astype(BF)
        dsc = dscores.astype(BF)
        v.dbc[block(i), :n] = dot(dsc, c_rows, TN)
        v.dbc[block(i), n:] = dot(dsc, b_rows) + dot2(faded, v.sin[i], NT)

    for step in range(1 if scan.steps > 1 else 0, scan.steps):
        scan.advance(step)
    scan.hand_over()
    tick()
    scan.result()
    carry = v.enter[...]
    at = next(counter)
    halo_x = remote(v.hxs, v.hxr, v.ssem.at[at], v.rsem.at[at], lay.prev_run())

    in_loop = pump.later()

    @pl.loop(0, nb)
    def _(i):
        pl.when(i == 2)(in_loop)
        cat = conv_cat(v.xp, i)
        pre = conv_pre(cat, p["conv_x"], p["bias_x"])
        x = v.xc[block(i), :]
        step, cum = v.cums[0, block(i), :], v.cums[1, block(i), :]
        last = cum[Q - 1 :, :]
        fade = expand(lay, expm[...], jnp.exp(last - cum))
        step_w = expand(lay, expm[...], step)
        gone = jnp.exp(v.dsuf[tile(i), :])
        lam_out = v.lamloc[i] + expand(lay, expm[...], gone)[:1, :] * carry
        lam_b = dot2(v.bc[block(i), :n], lam_out)
        xw = x * step_w * fade
        v.dbc[block(i), :n] += dot2(xw.astype(BF), lam_out, NT)
        within = jnp.sum(lam_out * v.sin[i], axis=0, keepdims=True)
        kept = head_sum(expm[...], jnp.broadcast_to(within, (8, w)))[:1, :] * jnp.exp(last)
        dxt = v.dx[block(i), :] + fade * lam_b
        g = v.rcs[block(i), :] + sum3(strict, head_sum(expm[...], xw * lam_b)) + kept
        dstep = head_sum(expm[...], x * dxt) + p["rate"] * g
        v.acch[1:2, :] += jnp.sum(step * g, axis=0, keepdims=True)
        dpre_step = dstep * jax.nn.sigmoid(v.sm[block(i, base=16), :] + p["step_bias"])
        v.acch[0:1, :] += jnp.sum(dpre_step, axis=0, keepdims=True)
        v.dsp[block(i), :] = dpre_step
        d_xin = step_w * dxt + p["skip"] * v.dy[block(i), :]
        dpre = d_xin * silu_grad(pre)
        v.xdp[block(i), :] = dpre
        for k in range(4):
            v.psm[k : k + 1, :] += jnp.sum(dpre * cat[5 + k : 5 + k + Q, :], axis=0, keepdims=True)
        v.psm[4:5, :] += jnp.sum(dpre, axis=0, keepdims=True)

        @pl.when(i == 0)
        def _():
            v.hxs[...] = v.xdp[:16, :].astype(BF)
            halo_x.start()

    sel_top, sel_bottom = selectors(lay)
    pieces = dot(v.dbc[:half, :].astype(BF), sel_top, NT) + dot(
        v.dbc[half:, :].astype(BF), sel_bottom, NT
    )
    for k in range(lay.parts):
        v.dbs[k] = pieces[:, k * LANES : (k + 1) * LANES].astype(BF)
    bc_sends = [
        send(v.dbs.at[lax.rem(q + k, lay.parts)], v.dbr.at[k - 1], target) for k, target in peers
    ]
    inside = jnp.where((c == 1) & (z == lay.seqs - 1), 0.0, 1.0)
    tick()
    if late:
        for copy in late_sums:
            copy.wait()
        cols = pl.ds(pl.multiple_of(q * lay.share, LANES), lay.share)
        for i in range(nb):
            rows = pl.ds(i * Q, Q)
            value = v.dnp[q, rows, :].astype(F32)
            for k, _ in peers:
                value = value + v.late_got[k - 1, rows, :].astype(F32)
            inv = to_col(lax.rsqrt(v.sqt[8 * i : 8 * i + 1, :] / lay.inner + EPS))
            v.hid[rows, :] = v.resid[rows, cols].astype(F32) + inv * value
    halo_x.wait()
    v.xdp[lay.rows :, :] = v.hxr[...].astype(F32) * inside

    @pl.loop(0, nb)
    def _(i):
        cat = v.xdp[pl.ds(pl.multiple_of(i * Q, 8), Q + 8), :]
        grad = jnp.zeros((Q, w), F32)
        for k in range(4):
            grad = grad + p["conv_x"][k : k + 1, :] * cat[3 - k : 3 - k + Q, :]
        v.lowx[block(i), :] = grad.astype(BF)

    for load in loads[1:] if more else []:
        load.wait()
    copy_x = weight_grad(normed_half, v.lowx, v.wo.at[:, w:], v.gr_x, v.own_x)
    tick()

    for copy in bc_sends:
        copy.wait()
    summed = v.dbs[q].astype(F32)
    for k in range(1, lay.parts):
        summed = summed + v.dbr[k - 1].astype(F32)
    for i in range(nb):
        rows = pl.ds(i * Q, Q)
        if i < nb // 2:
            d_conv = summed[i * Q : (i + 1) * Q, :]
        else:
            d_conv = pltpu.roll(summed[i * Q - half : (i + 1) * Q - half, :], LANES // 2, 1)
        cat = conv_cat(v.sm, i)
        pre = conv_pre(cat, p["conv_sm"], p["bias_sm"])
        valid = iota((Q, LANES), 1) < lay.off
        dpre = jnp.where(valid, d_conv * silu_grad(pre), 0.0)
        v.smdp[rows, :] = dpre
        for k in range(4):
            v.psm[7:8, k * LANES : (k + 1) * LANES] += jnp.sum(
                dpre * cat[5 + k : 5 + k + Q, :], axis=0, keepdims=True
            )
        v.psm[7:8, 4 * LANES : 5 * LANES] += jnp.sum(dpre, axis=0, keepdims=True)
    v.hss[...] = v.smdp[:16, :].astype(BF)
    halo_s = send(v.hss, v.hsr, lay.prev_run())
    v.psm[6:7, :LANES] = head_sum(expm[...], v.psm[8:9, :])
    v.psm[6:7, LANES : 2 * LANES] = v.acch[0:1, :]
    v.psm[6:7, 2 * LANES : 3 * LANES] = v.acch[1:2, :] * p["rate"]
    pair_sum(copy_x, v.own_x, v.gr_x)
    halo_s.wait()
    v.smdp[lay.rows :, :] = v.hsr[...].astype(F32) * inside
    for i in range(nb):
        rows = pl.ds(i * Q, Q)
        cat = v.smdp[i * Q : (i + 1) * Q + 8, :]
        grad = jnp.zeros((Q, LANES), F32)
        for k in range(4):
            grad = grad + p["conv_sm"][k : k + 1, :] * cat[3 - k : 3 - k + Q, :]
        lane = iota((Q, LANES), 1)
        first = jnp.where(lane < lay.off + GROUP, v.dsp[rows, :], 0.0)
        v.lowsm[rows, :] = jnp.where(lane < lay.off, grad, first).astype(BF)
    copy_s = weight_grad(normed_half, v.lowsm, v.gs_s, v.gr_s, v.own_s)
    pump.ready += N_X if more else X_EARLY
    if not more:
        v.rest_x[...] = v.own_x[m // 2 // N_X * X_EARLY :, :]
    tick()

    v.rdacc[...] = jnp.zeros(v.rdacc.shape, F32)
    sums = [[] for _ in range(nb)]
    for k in range(lay.parts):
        cols = slice(k * lay.share, (k + 1) * lay.share)
        grad = dot(v.lowg[...], v.wg[cols, :], NT) + dot(v.lowx[...], v.wx[cols, :], NT)
        grad = grad + dot(v.lowsm[...], v.wsm[cols, :], NT)
        v.dnp[k] = grad.astype(BF)
        v.rdacc[...] += fold(grad * p["gain"][:, cols] * v.resid[:, cols].astype(F32))
    for i in range(nb):
        rows = pl.ds(i * Q, Q)
        for k, target in peers:
            copy = remote(
                v.dnp.at[lax.rem(q + k, lay.parts), rows],
                v.got.at[k - 1, rows],
                v.rs_send.at[k - 1, i],
                v.rs_recv.at[k - 1, i],
                target,
            )
            copy.start()
            sums[i].append(copy)
    for i in range(nb):
        row = to_row(v.rdacc[i * Q : (i + 1) * Q, :])
        v.rd2[8 * i : 8 * (i + 1), :] = jnp.broadcast_to(row, (8, Q))
    rd_sends = [send(v.rd2, v.got_rows.at[k - 1], target) for k, target in peers]
    pair_sum(copy_s, v.own_s, v.gr_s)
    if more:
        pump.ready += 1
    cols = pl.ds(pl.multiple_of(q * lay.share, LANES), lay.share)
    v.gains[...] = jnp.broadcast_to(p["gain"], (8, m))
    own_gain = v.gains[:1, cols]
    tick()
    for copy in rd_sends:
        copy.wait()
    inner = v.rd2[...]
    for k, _ in peers:
        inner = inner + v.got_rows[k - 1]
    given = []
    rms_sum = jnp.zeros((1, lay.share), F32)
    for i in range(nb):
        rows = pl.ds(i * Q, Q)
        for copy in sums[i]:
            copy.wait()
        total = v.dnp[q, rows, :].astype(F32)
        for k, _ in peers:
            total = total + v.got[k - 1, rows, :].astype(F32)
        start = v.resid[rows, cols].astype(F32)
        x = v.resid[rows, :].astype(F32)
        scale = lax.rsqrt(jnp.mean(x * x, axis=1, keepdims=True) + EPS)
        value = (
            v.up[rows, cols].astype(F32)
            + scale * (own_gain * total)
            - start * (scale * scale * scale * to_col(inner[8 * i : 8 * i + 1, :] / m))
        )
        rms_sum = rms_sum + jnp.sum(total * start * scale, axis=0, keepdims=True)
        v.gt[rows, :] = value
        if gather:
            v.full[rows, cols] = value.astype(BF)
            for k, target in peers:
                copy = remote(
                    v.full.at[rows, cols],
                    v.full.at[rows, cols],
                    v.ag_send.at[k - 1, i],
                    v.ag_recv.at[k - 1, i],
                    target,
                )
                copy.start()
                given.append(copy)
        if i % 2:
            tick()
    v.psm[8:9, :] = jnp.zeros((1, w), F32)
    v.psm[8:9, : lay.share] = rms_sum
    if more:
        pl.when(c == 1)(pairs[1][1].start)
        column = [(a, b) for a in range(2) for b in range(lay.seqs) if a or b]
        own_slot = c * lay.seqs + z
        smalls = []
        for at, (a, b) in enumerate(column):
            to_c, to_z = (c + a) % 2, lax.rem(z + b, lay.seqs)
            to = (to_c, to_z, q)
            pair = [
                remote(src, v.slots.at[own_slot], v.slot_sem.at[0, at], v.slot_sem.at[1, at], to)
                for src in (v.psm, v.small)
            ]
            pl.when(to_c == 0)(pair[0].start)
            pl.when(to_c == 1)(pair[1].start)
            smalls.append(pair[0])
        v.slots[own_slot] = jnp.where(c == 0, v.psm[...], v.small[...])
        tick()
        for copy in smalls:
            copy.wait()
        value = v.slots[0]
        for k in range(1, 2 * lay.seqs):
            value = value + v.slots[k]
        v.total[:16, :] = value
        v.rest_rows[q] = value[8:16, :]
        parts = []
        for k, target in peers:
            copy = remote(
                v.rest_rows.at[q],
                v.rest_rows.at[q],
                v.part_sem.at[0, k - 1],
                v.part_sem.at[1, k - 1],
                target,
            )
            copy.start()
            parts.append(copy)
        tick()
        for copy in parts:
            copy.wait()
        for k in range(lay.parts):
            v.total[16 + 8 * k : 24 + 8 * k, :] = v.rest_rows[k]
    pump.finish()
    for copy in given:
        copy.wait()
    if more:
        for of, here, there in finals:
            pl.when(c == of)(here.wait)
            pl.when(c == of)(there.wait_recv)
            pl.when(c != of)(there.wait_send)
        for pair in pairs:
            pair[0].wait()


def bwd_layer(lay, layer, args, more):
    late = gather = not more
    outs, scratch = back_outs(lay, late, gather, more), back_scratch(lay, late, gather, more)
    vmem, hbm = pl.BlockSpec(memory_space=VM), pl.BlockSpec(memory_space=HB)
    names = back_ins(lay, more)
    away = {"tokens", "cotangent", "hid0", "hid1", "gt1"}
    specs = [hbm if name in away or name[:3] in ("own", "oth") else vmem for name in names]
    out_specs = [vmem] * len(outs)
    if more:
        out_specs[-6:] = [hbm] * 6
    got = pl.pallas_call(
        functools.partial(bwd_kernel, lay, layer, late, gather, more),
        out_shape=tuple(outs.values()),
        in_specs=specs,
        out_specs=tuple(out_specs),
        scratch_shapes=list(scratch.values()),
        compiler_params=pltpu.CompilerParams(
            collective_id=5 + layer, has_side_effects=True, vmem_limit_bytes=63 << 20
        ),
        name=f"mixer_backward_{layer}",
    )(*(args[name] for name in names))
    return Names(list(outs), got)


def on_device(
    mesh_shape, tokens, cotangent, rms_gain, proj_gate, proj_x, proj_bc, proj_step, conv_x, conv_x_bias,
    conv_bc, conv_bc_bias, step_bias, decay_log, skip_gain, norm_gain, proj_out,
):
    pieces, rows, model = tokens.shape
    width, heads, local_state = proj_x.shape[2], proj_step.shape[2], proj_bc.shape[3]
    lay = Lay(mesh_shape, rows, width, model, heads, local_state)
    section = lax.axis_index("section")
    group = jnp.pad(proj_step[0], ((0, 0), (0, GROUP - heads)))
    w_small = jnp.concatenate(
        [
            proj_bc[0].reshape(model, lay.off),
            group,
            group,
            group,
            jnp.zeros((model, LANES - lay.off - 3 * GROUP), BF),
        ],
        axis=1,
    )
    taps = conv_x.shape[1]
    own = (proj_gate[0], proj_x[0], w_small, proj_out[0])
    first = start_layer(
        lay,
        tokens,
        *own,
        conv_x[0],
        conv_x_bias,
        norm_gain,
        rms_gain,
        conv_bc.reshape(taps, lay.off),
        conv_bc_bias.reshape(1, lay.off),
        step_bias,
        decay_log,
        skip_gain,
    )
    args = dict(vars(first), tokens=tokens, cotangent=cotangent, resid=first.full)
    args.update({f"own{k}": weight for k, weight in enumerate(own)})
    one = bwd_layer(lay, 1, args, False)
    args.update(up=one.full, prev_x=one.rest_x, prev_s=one.own_s, done_o=one.sum_o, done_g=one.sum_g)
    args.update(done_x=one.sum_x, small=one.psm, hid0=first.hid, hid1=one.hid, gt1=one.gt)
    zero = bwd_layer(lay, 0, args, True)
    at_zero = section == 0

    def both_pieces(ours0, ours1, theirs):
        ours = jnp.where(at_zero, ours0, ours1)
        return jnp.stack([jnp.where(at_zero, ours, theirs), jnp.where(at_zero, theirs, ours)])[None]

    hid = both_pieces(first.hid, one.hid, zero.got_hid)
    gt = both_pieces(zero.gt, one.gt, zero.got_gt)
    g_gate, g_x, g_out, g_sm = (
        a.astype(F32)[None] for a in (zero.fin_g, zero.fin_x, zero.fin_o, zero.fin_s)
    )
    total = zero.total
    lane = lay.off
    rms_all = total[16:].reshape(lay.parts, 8, width)[:, 0, : lay.share].reshape(1, model)
    conv_small = total[7].reshape(-1, LANES)[:5, : lay.off]

    def head_row(k):
        return total[6, k * LANES + lane : k * LANES + lane + heads][None]

    return (
        hid,
        gt,
        rms_all,
        g_gate,
        g_x,
        g_sm[:, :, : lay.off].reshape(1, model, 2, local_state),
        g_sm[:, :, lane : lane + heads],
        total[None, 0:4],
        total[4:5],
        conv_small[:4].reshape(1, 4, 2, local_state),
        conv_small[4].reshape(1, 2, local_state),
        head_row(1),
        head_row(2),
        head_row(0),
        total[5:6],
        g_out,
    )


def solution(mesh):
    placed = (
        P(None, "seq", None),
        P(None, "seq", None),
        P("section", None),
        P("section", None, "head"),
        P("section", None, "head"),
        P("section", None, None, "head"),
        P("section", None, "head"),
        P("section", None, "head"),
        P("section", "head"),
        P("section", None, None, "head"),
        P("section", None, "head"),
        P("section", "head"),
        P("section", "head"),
        P("section", "head"),
        P("section", "head"),
        P("section", "head", None),
    )
    back = (P("section", None, "seq", "head"),) * 2 + placed[2:]
    shape = tuple(mesh.shape[name] for name in ("section", "seq", "head"))
    return jax.shard_map(
        functools.partial(on_device, shape),
        mesh=mesh,
        in_specs=placed,
        out_specs=back,
        check_vma=False,
    )
```

```python
import functools

import jax
import jax.numpy as jnp
from jax import lax
from jax.experimental import pallas as pl
from jax.experimental.pallas import tpu as pltpu
from jax.sharding import PartitionSpec as P

F32, BF = jnp.float32, jnp.bfloat16
MESH = pl.DeviceIdType.MESH
EPS = 1e-05
Q = 128
LANES = 128
GROUP = 16
NN, NT, TN = ((1,), (0,)), ((1,), (1,)), ((0,), (0,))
VM, HB = pltpu.VMEM, pl.ANY


def dot(a, b, dims=NN):
    return lax.dot_general(a, b, (dims, ((), ())), preferred_element_type=F32)


def iota(shape, dim):
    return lax.broadcasted_iota(jnp.int32, shape, dim)


def split3(v):
    hi = v.astype(BF)
    rest = v - hi.astype(F32)
    mid = rest.astype(BF)
    return hi, mid, (rest - mid.astype(F32)).astype(BF)


def sum3(matrix, v, dims=NN):
    hi, mid, low = split3(v)
    return dot(matrix, hi, dims) + dot(matrix, mid, dims) + dot(matrix, low, dims)


def dot2(a, v, dims=NN):
    hi = v.astype(BF)
    return dot(a, hi, dims) + dot(a, (v - hi.astype(F32)).astype(BF), dims)


def silu_grad(v):
    sg = jax.nn.sigmoid(v)
    return sg * (1.0 + v * (1.0 - sg))


def fold(v):
    total = v[:, :LANES]
    for k in range(1, v.shape[1] // LANES):
        total = total + v[:, k * LANES : (k + 1) * LANES]
    return total


def to_row(v):
    return jnp.sum(jnp.transpose(fold(v)), axis=0, keepdims=True)


def to_col(row):
    return jnp.transpose(jnp.broadcast_to(row, (Q, Q)))[:, :1]


class Lay:
    def __init__(self, mesh_shape, rows, width, model, heads, local_state):
        self.sections, self.seqs, self.parts = mesh_shape
        self.rows, self.width, self.model, self.heads = rows, width, model, heads
        self.nb = rows // Q
        self.share = model // self.parts
        self.ls = local_state
        self.off = 2 * local_state
        self.hp = width // heads
        self.inner = width * self.parts
        self.state = local_state * self.parts

    def place(self):
        self.c = lax.axis_index("section")
        self.z = lax.axis_index("seq")
        self.q = lax.axis_index("head")

    def heads_peers(self):
        return [
            (k, (self.c, self.z, lax.rem(self.q + k, self.parts)))
            for k in range(1, self.parts)
        ]

    def seq_peers(self):
        return [(k, (self.c, lax.rem(self.z + k, self.seqs), self.q)) for k in range(1, self.seqs)]

    def sibling(self):
        return (1 - self.c, self.z, self.q)

    def next_run(self):
        last = self.z == self.seqs - 1
        return (
            jnp.where(last, 1 - self.c, self.c),
            jnp.where(last, 0, self.z + 1),
            self.q,
        )

    def prev_run(self):
        first = self.z == 0
        return (
            jnp.where(first, 1 - self.c, self.c),
            jnp.where(first, self.seqs - 1, self.z - 1),
            self.q,
        )


def meet(targets):
    barrier = pltpu.get_barrier_semaphore()
    for target in targets:
        pl.semaphore_signal(barrier, inc=1, device_id=target, device_id_type=MESH)
    pl.semaphore_wait(barrier, len(targets))


def column_and_heads(lay):
    column = [
        ((lay.c + s) % 2, lax.rem(lay.z + k, lay.seqs), lay.q)
        for s in range(2)
        for k in range(lay.seqs)
        if s or k
    ]
    return column + [target for _, target in lay.heads_peers()]


def remote(src, dst, send, recv, target):
    return pltpu.make_async_remote_copy(
        src_ref=src,
        dst_ref=dst,
        send_sem=send,
        recv_sem=recv,
        device_id=target,
        device_id_type=MESH,
    )


class SeqSum:
    def __init__(self, lay, pieces, sems):
        self.pieces, self.sems = pieces, sems
        z, n = lay.z, lay.seqs
        self.left = z < n // 2
        depth = jnp.where(self.left, z, n - 1 - z)
        self.outer = depth > 0
        self.middle = depth == n // 2 - 1
        self.inside = (lay.c, jnp.where(self.left, z + 1, z - 1), lay.q)
        self.outside = (lay.c, jnp.clip(jnp.where(self.left, z - 1, z + 1), 0, n - 1), lay.q)

    def pass_on(self, k, src):
        own, inner, result, rows = self.pieces[k]
        ssem, asem, tsem, _ = self.sems

        def to_middle():
            remote(src, result.at[rows], ssem.at[k], tsem.at[k], self.inside).start()

        def to_next():
            remote(src, inner.at[rows], ssem.at[k], asem.at[k], self.inside).start()

        pl.when(self.middle)(to_middle)
        pl.when(jnp.logical_not(self.middle))(to_next)

    def inward(self, k):
        own, inner, result, rows = self.pieces[k]
        ssem, asem, tsem, _ = self.sems

        @pl.when(self.outer)
        def _():
            remote(own.at[rows], inner.at[rows], ssem.at[k], asem.at[k], self.inside).wait_recv()
            inner[rows, :] = inner[rows, :] + own[rows, :]
            self.pass_on(k, inner.at[rows])

    def push(self, k):
        @pl.when(jnp.logical_not(self.outer))
        def _():
            own, _, _, rows = self.pieces[k]
            self.pass_on(k, own.at[rows])

    def outward(self, k):
        own, inner, result, rows = self.pieces[k]
        ssem, _, tsem, osem = self.sems

        def arrived():
            remote(own.at[rows], result.at[rows], ssem.at[k], tsem.at[k], self.inside).wait_recv()

        @pl.when(self.outer)
        def _():
            arrived()

            @pl.when(self.middle)
            def _():
                result[rows, :] = result[rows, :] + inner[rows, :]

            remote(result.at[rows], result.at[rows], osem.at[k], tsem.at[k], self.outside).start()

    def ending(self, k):
        own, inner, result, rows = self.pieces[k]
        ssem, _, tsem, _ = self.sems

        @pl.when(jnp.logical_not(self.outer))
        def _():
            remote(own.at[rows], result.at[rows], ssem.at[k], tsem.at[k], self.inside).wait_recv()

            @pl.when(self.middle)
            def _():
                result[rows, :] = result[rows, :] + own[rows, :]

    def finish(self):
        for k, (own, inner, result, rows) in enumerate(self.pieces):
            ssem, _, tsem, osem = self.sems
            remote(own.at[rows], result.at[rows], ssem.at[k], tsem.at[k], self.inside).wait_send()

            @pl.when(self.outer)
            def _():
                remote(
                    result.at[rows], result.at[rows], osem.at[k], tsem.at[k], self.outside
                ).wait_send()


class Pump:
    def __init__(self, seq_sum, done=None):
        self.sum, self.done = seq_sum, done
        self.ready = self.pushed = self.taken = self.given = self.ended = 0

    def end(self, k):
        self.sum.ending(k)
        if self.done is not None:
            self.done(k)

    def plan(self):
        steps = []

        def feed():
            while self.pushed < min(self.ready, self.taken + 2):
                steps.append((self.sum.push, self.pushed))
                self.pushed += 1

        feed()
        if self.taken < self.pushed:
            steps.append((self.sum.inward, self.taken))
            self.taken += 1
            feed()
        if self.given < self.taken - 1:
            steps.append((self.sum.outward, self.given))
            self.given += 1
        if self.ended < self.given - 2:
            steps.append((self.end, self.ended))
            self.ended += 1
        return steps

    def feed(self):
        while self.pushed < min(self.ready, self.taken + 2):
            self.sum.push(self.pushed)
            self.pushed += 1

    def tick(self):
        self.later()()

    def later(self):
        steps = self.plan()

        def act():
            for kind, piece in steps:
                kind(piece)

        return act

    def finish(self):
        while self.taken < self.ready:
            self.tick()
        while self.given < self.taken:
            self.sum.outward(self.given)
            self.given += 1
        while self.ended < self.given:
            self.end(self.ended)
            self.ended += 1
        self.sum.finish()


class Scan:
    def __init__(self, lay, forward, expm, v):
        self.lay, self.expm, self.v = lay, expm, v
        self.steps = max(lay.seqs - 1, 0).bit_length()
        assert 1 << self.steps == lay.seqs
        self.forward = forward
        self.u = lay.z if forward else lay.seqs - 1 - lay.z
        self.first = lay.c == (0 if forward else 1)

    def device(self, u):
        u = jnp.clip(u, 0, self.lay.seqs - 1)
        return (self.lay.c, u if self.forward else self.lay.seqs - 1 - u, self.lay.q)

    def row(self, chosen):
        total = jnp.ones((8, LANES), F32)
        for u in range(self.lay.seqs):
            z = u if self.forward else self.lay.seqs - 1 - u
            total = jnp.where(chosen(u), total * self.v.table[z], total)
        return expand(self.lay, self.expm[...], total)[:1, :]

    def copies(self, s, ahead, only=None):
        v = self.v
        src, dst = (v.main_s, v.main_r) if ahead else (v.back_s, v.back_r)
        send, recv = (v.scan_sem.at[0 if ahead else 2], v.scan_sem.at[1 if ahead else 3])
        out = []
        for t in range(1 << s) if only is None else (only,):
            u = self.u + 1 + t if ahead else self.u - 1 - t
            out.append(
                remote(src, dst.at[s], send.at[(1 << s) - 1 + t], recv.at[s], self.device(u))
            )
        return out

    def gives(self, s, ahead):
        place = self.u if ahead else self.lay.seqs - 1 - self.u
        return lax.rem(place, 2 << s) == (1 << s) - 1

    def takes(self, s, ahead):
        place = self.u if ahead else self.lay.seqs - 1 - self.u
        return lax.rem(place // (1 << s), 2) == 1

    def give(self, s):
        v = self.v

        @pl.when(self.gives(s, True))
        def _():
            own_decay = self.row(lambda u: u == self.u)
            v.main_s[...] = (v.enter[...] * own_decay + v.own_state[...]).astype(BF)
            for copy in self.copies(s, True):
                copy.start()

        @pl.when(self.first & self.gives(s, False))
        def _():
            v.back_s[...] = (v.rest[...] + v.own_state[...] * self.row(lambda u: u > self.u)).astype(BF)
            for copy in self.copies(s, False):
                copy.start()

    def start(self):
        v = self.v
        v.enter[...] = jnp.zeros(v.enter.shape, F32)
        v.rest[...] = jnp.zeros(v.rest.shape, F32)
        if self.steps:
            self.give(0)

    def advance(self, s):
        v = self.v

        @pl.when(self.takes(s, True))
        def _():
            self.copies(s, True, 0)[0].wait_recv()
            begin = (self.u // (1 << s)) * (1 << s)
            between = self.row(lambda u: (u >= begin) & (u < self.u))
            v.enter[...] += between * v.main_r[s].astype(F32)

        @pl.when(self.first & self.takes(s, False))
        def _():
            self.copies(s, False, 0)[0].wait_recv()
            v.rest[...] += v.back_r[s].astype(F32)

        if s + 1 < self.steps:
            self.give(s + 1)

    def hand_over(self):
        v = self.v
        self.total = remote(
            v.total_s, v.total_r, v.total_sem.at[0], v.total_sem.at[1], self.lay.sibling()
        )

        @pl.when(self.first)
        def _():
            own_decay = self.row(lambda u: u == self.u)
            after = self.row(lambda u: u > self.u)
            through = (v.enter[...] * own_decay + v.own_state[...]) * after
            v.total_s[...] = (through + v.rest[...]).astype(BF)
            self.total.start()

    def result(self):
        v = self.v

        @pl.when(jnp.logical_not(self.first))
        def _():
            self.total.wait_recv()
            v.enter[...] += self.row(lambda u: u < self.u) * v.total_r[...].astype(F32)

        pl.when(self.first)(self.total.wait_send)
        for s in range(self.steps):
            for ahead in (True, False):
                gives = self.gives(s, ahead)

                @pl.when(gives if ahead else self.first & gives)
                def _():
                    for copy in self.copies(s, ahead):
                        copy.wait_send()


def scan_scratch(lay, kinds):
    n, w, steps = lay.state, lay.width, max(lay.seqs - 1, 1).bit_length()
    dma = pltpu.SemaphoreType.DMA
    out = dict(
        table=VM((lay.seqs, 8, LANES), F32),
        own_state=VM((n, w), F32),
        enter=VM((n, w), F32),
        rest=VM((n, w), F32),
        main_s=VM((n, w), BF),
        back_s=VM((n, w), BF),
        total_s=VM((n, w), BF),
        table_sem=dma((2, max(lay.seqs - 1, 1))),
    )
    for kind in kinds:
        out[kind + "main_r"] = VM((steps, n, w), BF)
        out[kind + "back_r"] = VM((steps, n, w), BF)
        out[kind + "total_r"] = VM((n, w), BF)
        out[kind + "scan_sem"] = dma((4, max(lay.seqs - 1, 1)))
        out[kind + "total_sem"] = dma((2,))
    return out


def scan_refs(v, kind):
    shared = ["table", "own_state", "enter", "rest", "main_s", "back_s", "total_s"]
    own = ["main_r", "back_r", "total_r", "scan_sem", "total_sem"]
    refs = [getattr(v, name) for name in shared] + [getattr(v, kind + name) for name in own]
    return Names(shared + own, refs)


def share_table(lay, v):
    copies = [
        remote(v.table.at[lay.z], v.table.at[lay.z], v.table_sem.at[0, k - 1], v.table_sem.at[1, k - 1], to)
        for k, to in lay.seq_peers()
    ]
    for copy in copies:
        copy.start()
    return copies


class Names:
    def __init__(self, names, refs):
        assert len(names) == len(refs), (len(names), len(refs))
        self.__dict__.update(zip(names, refs))


def pieces_of(own, inner, result, count):
    size = own.shape[0] // count
    return [(own, inner, result, pl.ds(k * size, size)) for k in range(count)]


def expander(lay):
    lane = iota((LANES, lay.width), 0) - lay.off
    head = iota((LANES, lay.width), 1) // lay.hp
    hit = (lane >= 0) & (lane < 3 * GROUP) & (lax.rem(lane + GROUP * 8, GROUP) == head)
    return jnp.where(hit, 1.0, 0.0).astype(BF)


def expand(lay, exp_matrix, v):
    hi, mid, low = split3(v)
    lane = iota(v.shape, 1) - lay.off
    packed = jnp.where(
        lane < 0,
        0.0,
        jnp.where(
            lane < GROUP,
            hi.astype(F32),
            jnp.where(
                lane < 2 * GROUP, mid.astype(F32), jnp.where(lane < 3 * GROUP, low.astype(F32), 0.0)
            ),
        ),
    )
    return dot(packed.astype(BF), exp_matrix)


def head_sum(exp_matrix, v):
    hi, mid, low = split3(v)
    return dot(hi, exp_matrix, NT) + dot(mid, exp_matrix, NT) + dot(low, exp_matrix, NT)


def selectors(lay):
    shape = (lay.parts * LANES, 2 * lay.state)
    row, col = iota(shape, 0), iota(shape, 1)
    piece, lane = row // LANES, lax.rem(row, LANES)
    kind, n = col // lay.state, lax.rem(col, lay.state)
    want = kind * lay.ls + lax.rem(n, lay.ls)
    same = piece == n // lay.ls
    top = jnp.where(same & (lane == want), 1.0, 0.0).astype(BF)
    bottom = jnp.where(same & (lane == want + LANES // 2), 1.0, 0.0).astype(BF)
    return top, bottom


def tri(kind):
    row, col = iota((Q, Q), 0), iota((Q, Q), 1)
    hit = {"lower": row >= col, "upper": row <= col, "strict": row > col}[kind]
    return jnp.where(hit, 1.0, 0.0).astype(BF)


def block(i, size=Q, base=0):
    return pl.ds(pl.multiple_of(i * size + base, 8), size)


def conv_cat(ref, i):
    return ref[pl.ds(pl.multiple_of(i * Q + 8, 8), Q + 8), :]


def conv_pre(cat, kernel, bias):
    total = bias
    for k in range(4):
        total = total + kernel[k : k + 1, :] * cat[5 + k : 5 + k + Q, :]
    return total


def softplus(v):
    return jnp.maximum(v, 0.0) + jnp.log1p(jnp.exp(-jnp.abs(v)))


def params(lay, pk_ref, layer):
    pk = pk_ref[layer]
    w = lay.width
    out = dict(
        conv_x=pk[0:4, :],
        bias_x=pk[4:5, :],
        gain_out=pk[5:6, :],
        skip=pk[6:7, :],
        gain=jnp.concatenate([pk[7:8, :], pk[8:9, :]], axis=1)
        if lay.model == 2 * w
        else None,
        conv_sm=jnp.concatenate([pk[9:10, k * LANES : (k + 1) * LANES] for k in range(4)], axis=0),
        bias_sm=pk[9:10, 4 * LANES : 5 * LANES],
        step_bias=pk[10:11, 0:LANES],
        rate=pk[10:11, LANES : 2 * LANES],
    )
    return out


def decay_tile(cum, cum_t, lane, causal):
    diff = cum[:, lane : lane + 1] - cum_t[lane : lane + 1, :]
    return jnp.exp(jnp.where(causal, diff, -1e30))


def halves(v):
    lane = iota(v.shape, 1)
    left = lane < LANES // 2
    zero = jnp.zeros_like(v)
    return jnp.where(left, v, zero), jnp.where(left, zero, v)


class HeadSum:
    def __init__(self, lay, part, got, send, recv, full=None, gsend=None, grecv=None):
        assert lay.parts == 4
        self.lay, self.part, self.got, self.send, self.recv = lay, part, got, send, recv
        self.full, self.gsend, self.grecv = full, gsend, grecv
        q = lay.q
        self.index = (q, q + 1 - 2 * lax.rem(q, 2), lax.rem(q + 2, 4), 3 - q)
        self.out = []

    def target(self, mask):
        return (self.lay.c, self.lay.z, self.index[mask])

    def cols(self, mask):
        return pl.ds(pl.multiple_of(self.index[mask] * self.lay.share, LANES), self.lay.share)

    def near(self, i):
        return 1 if i % 2 == 0 else 2

    def rows(self, i):
        return pl.ds(i * Q, Q)

    def copy(self, kind, i):
        near, rows = self.near(i), self.rows(i)
        src = (near, 3, 3 - near)[kind]
        return remote(
            self.part.at[src, rows],
            self.got.at[kind, rows],
            self.send.at[kind, i],
            self.recv.at[kind, i],
            self.target(near if kind < 2 else 3 - near),
        )

    def first(self, i):
        self.steps = getattr(self, "steps", {})
        self.steps[i] = [self.copy(kind, i) for kind in range(2)]
        for copy in self.steps[i]:
            copy.start()

    def second(self, i):
        for copy in self.steps[i]:
            copy.wait()
        far, rows = 3 - self.near(i), self.rows(i)
        both = self.part[far, rows, :].astype(F32) + self.got[1, rows, :].astype(F32)
        self.part[far, rows, :] = both.astype(BF)
        copy = self.copy(2, i)
        copy.start()
        self.steps[i] = copy

    def total(self, i):
        self.steps[i].wait()
        rows = self.rows(i)
        value = self.part[0, rows, :].astype(F32) + self.got[0, rows, :].astype(F32)
        return value + self.got[2, rows, :].astype(F32)

    def spread(self, i, mask, kind, to):
        block = self.full.at[self.rows(i), self.cols(mask)]
        copy = remote(block, block, self.gsend.at[kind, i], self.grecv.at[kind, i], self.target(to))
        copy.start()
        return copy

    def give(self, i):
        self.steps[i] = [self.spread(i, 0, 0, 1), self.spread(i, 0, 1, 2)]

    def relay(self, i):
        near = self.near(i)
        self.steps[i][2 - near].wait()
        self.steps[i] = [self.steps[i][near - 1], self.spread(i, 3 - near, 2, near)]

    def finish(self):
        for copies in self.steps.values():
            for copy in copies:
                copy.wait()


class Load:
    def __init__(self, own, other, dst, sem, mine):
        self.mine = mine
        self.copies = [pltpu.make_async_copy(src, dst, sem) for src in (own, other)]

    def start(self):
        pl.when(self.mine)(self.copies[0].start)
        pl.when(jnp.logical_not(self.mine))(self.copies[1].start)

    def wait(self):
        self.copies[0].wait()


def forward(lay, v, p, resid, weights, ready, project, meanwhile=None):
    c, z, q = lay.c, lay.z, lay.q
    nb, w, n = lay.nb, lay.width, lay.state
    wsm, wx, wg = weights
    expm, normed, sm, xp, cums, bc = v.expm, v.normed, v.sm, v.xp, v.cums, v.bc
    scan = Scan(lay, True, expm, scan_refs(v, "f_"))
    counter = iter(range(16))

    def send(src, dst, target):
        at = next(counter)
        copy = remote(src, dst, v.fsend.at[at], v.frecv.at[at], target)
        copy.start()
        return copy

    @pl.loop(0, nb)
    def _(i):
        x = resid[block(i), :].astype(F32)
        scale = lax.rsqrt(jnp.mean(x * x, axis=1, keepdims=True) + EPS)
        normed[block(i), :] = (x * scale * p["gain"]).astype(BF)

    ready(0)
    sm[16:, :] = dot(normed[...], wsm[...])
    v.shs[...] = sm[lay.rows :, :].astype(BF)
    after = lay.next_run()
    halo_s = send(v.shs, v.shr, after)
    tables = run_decays(lay, v, p)
    ready(1)
    step_n = 256

    @pl.loop(0, w // step_n)
    def _(j):
        cols = pl.ds(pl.multiple_of(j * step_n, step_n), step_n)
        xp[16:, cols] = dot(normed[...], wx[:, cols])

    v.xhs[...] = xp[lay.rows :, :].astype(BF)
    halo_x = send(v.xhs, v.xhr, after)
    halo_s.wait()
    inside = jnp.where((c == 0) & (z == 0), 0.0, 1.0)
    sm[:16, :] = v.shr[...].astype(F32) * inside

    half = lay.rows // 2
    conv_rows = []
    for i in range(nb):
        pre = conv_pre(conv_cat(sm, i), p["conv_sm"], p["bias_sm"])
        conv_rows.append(pre * jax.nn.sigmoid(pre))
    top = jnp.concatenate(conv_rows[: nb // 2], axis=0)
    bottom = jnp.concatenate(conv_rows[nb // 2 :], axis=0)
    lane = iota(top.shape, 1)
    v.bcg[q] = jnp.where(lane < LANES // 2, top, pltpu.roll(bottom, LANES // 2, 1)).astype(BF)
    sends = [send(v.bcg.at[q], v.bcg.at[q], target) for _, target in lay.heads_peers()]
    halo_x.wait()
    xp[:16, :] = v.xhr[...].astype(F32) * inside

    @pl.loop(0, nb)
    def _(i):
        pre = conv_pre(conv_cat(xp, i), p["conv_x"], p["bias_x"])
        v.xc[block(i), :] = pre * jax.nn.sigmoid(pre)

    for copy in sends:
        copy.wait()
    pieces = jnp.concatenate([v.bcg[k] for k in range(lay.parts)], axis=1)
    sel_top, sel_bottom = selectors(lay)
    bc[:half, :] = dot(pieces, sel_top).astype(BF)
    bc[half:, :] = dot(pieces, sel_bottom).astype(BF)

    v.local[0] = jnp.zeros((n, w), F32)
    v.dpre[...] = jnp.zeros(v.dpre.shape, F32)
    state = None
    total = jnp.zeros((1, LANES), F32)
    for i in range(nb):
        rows = pl.ds(i * Q, Q)
        cum = cums[1, rows, :]
        last = cum[Q - 1 :, :]
        weight = jnp.exp(last - cum) * cums[0, rows, :]
        xw = (v.xc[rows, :] * expand(lay, expm[...], weight)).astype(BF)
        update = dot(bc[rows, :n], xw, TN)
        dec = expand(lay, expm[...], jnp.broadcast_to(jnp.exp(last), (8, LANES)))[:1, :]
        state = update if i == 0 else state * dec + update
        total = total + last
        if i < nb - 1:
            v.local[i + 1] = state
            v.dpre[8 * (i + 1) : 8 * (i + 2), :] = jnp.broadcast_to(total, (8, LANES))
    v.own_state[...] = state
    for copy in tables:
        copy.wait()
    scan.start()
    ready(2)

    @pl.loop(0, w // step_n)
    def _(j):
        cols = pl.ds(pl.multiple_of(j * step_n, step_n), step_n)
        v.gate[:, cols] = dot(normed[...], wg[:, cols])

    @pl.loop(0, nb)
    def _(i):
        if scan.steps > 1:
            pl.when(i == nb - 1)(functools.partial(scan.advance, 0))
        causal = iota((Q, Q), 0) >= iota((Q, Q), 1)
        cum = cums[1, block(i), :]
        cum_t = jnp.transpose(cum)
        scores = dot(bc[block(i), n:], bc[block(i), :n], NT)
        stepped = (v.xc[block(i), :] * expand(lay, expm[...], cums[0, block(i), :])).astype(BF)
        for pair in range(lay.heads // 2):
            cols = slice(pair * LANES, (pair + 1) * LANES)
            mixes = [
                (scores * decay_tile(cum, cum_t, lay.off + 2 * pair + e, causal)).astype(BF)
                for e in range(2)
            ]
            xl, xr = halves(stepped[:, cols])
            v.ysd[block(i), cols] = dot(
                jnp.concatenate(mixes, axis=1), jnp.concatenate([xl, xr], axis=0)
            )

    @pl.loop(0, nb)
    def _(i):
        v.nt[:, pl.ds(pl.multiple_of(i * Q, Q), Q)] = jnp.transpose(normed[block(i), :])

    if meanwhile is not None:
        meanwhile()
    for step in range(1 if scan.steps > 1 else 0, scan.steps):
        scan.advance(step)
    scan.hand_over()
    scan.result()
    start = v.enter[...]

    @pl.loop(0, nb)
    def _(i):
        cum = cums[1, block(i), :]
        dec = jnp.exp(v.dpre[pl.ds(pl.multiple_of(8 * i, 8), 8), :])
        full = v.local[i] + expand(lay, expm[...], dec)[:1, :] * start
        v.sin[i] = full
        carried = dot2(bc[block(i), n:], full) * expand(lay, expm[...], jnp.exp(cum))
        y = v.ysd[block(i), :] + carried
        v.ysd[block(i), :] = y
        g = v.gate[block(i), :]
        gated = (y + p["skip"] * v.xc[block(i), :]) * (g * jax.nn.sigmoid(g))
        row = to_row(gated * gated)
        v.sqb[q, pl.ds(pl.multiple_of(8 * i, 8), 8), :] = jnp.broadcast_to(row, (8, Q))
        v.go[block(i), :] = (gated * p["gain_out"]).astype(BF)

    squares = [send(v.sqb.at[q], v.sqb.at[q], target) for _, target in lay.heads_peers()]
    if meanwhile is None:
        ready(3)
    project()
    for copy in squares:
        copy.wait()
    total_sq = v.sqb[0]
    for k in range(1, lay.parts):
        total_sq = total_sq + v.sqb[k]
    v.sqt[...] = total_sq


def run_decays(lay, v, p):
    lower = tri("lower")
    lasts = []
    for i in range(lay.nb):
        rows = pl.ds(i * Q, Q)
        step = softplus(v.sm[16 + i * Q : 16 + (i + 1) * Q, :] + p["step_bias"])
        v.cums[0, rows, :] = step
        cum = sum3(lower, step * p["rate"])
        v.cums[1, rows, :] = cum
        lasts.append(cum[Q - 1 :, :])
    v.table[lay.z] = jnp.broadcast_to(jnp.exp(sum(lasts)), (8, LANES))
    return share_table(lay, v)


def kept_shapes(lay):
    r, w, m, n = lay.rows, lay.width, lay.model, lay.state
    return dict(
        nt=((m, r), BF),
        gate=((r, w), F32),
        xp=((r + 16, w), F32),
        sm=((r + 16, LANES), F32),
        ysd=((r, w), F32),
        sin=((lay.nb, n, w), F32),
        bc=((r, 2 * n), BF),
        sqt=((8 * lay.nb, Q), F32),
    )


def fwd_scratch(lay):
    r, w = lay.rows, lay.width
    dma = pltpu.SemaphoreType.DMA
    n_sem = 2 + 2 * (lay.parts - 1)
    return dict(
        xhs=VM((16, w), BF),
        xhr=VM((16, w), BF),
        shs=VM((16, LANES), BF),
        shr=VM((16, LANES), BF),
        bcg=VM((lay.parts, r // 2, LANES), BF),
        dpre=VM((8 * lay.nb, LANES), F32),
        sqb=VM((lay.parts, 8 * lay.nb, Q), F32),
        fsend=dma((n_sem,)),
        frecv=dma((n_sem,)),
    )


START_SMALL = ["conv_x", "bias_x", "gain_out", "rms", "conv_sm", "bias_sm"]
START_HEADS = ["step_bias", "decay", "skip"]


def start_ins():
    return ["tokens"] + [f"own{k}" for k in range(4)] + START_SMALL + START_HEADS


def start_outs(lay):
    r, w, m = lay.rows, lay.width, lay.model
    sds = jax.ShapeDtypeStruct
    out = {name: sds(*spec) for name, spec in kept_shapes(lay).items()}
    out.update(
        pk=sds((2, 16, w), F32),
        hid=sds((r, lay.share), F32),
        full=sds((r, m), BF),
        other0=sds((m, w), BF),
        other1=sds((m, w), BF),
        other2=sds((m, LANES), BF),
        other3=sds((w, m), BF),
    )
    return out


def start_scratch(lay):
    r, w, m, n = lay.rows, lay.width, lay.model, lay.state
    dma = pltpu.SemaphoreType.DMA
    peers = lay.parts - 1
    out = dict(
        resid=VM((r, m), BF),
        wg=VM((2, m, w), BF),
        wx=VM((2, m, w), BF),
        wsm=VM((2, m, LANES), BF),
        wo=VM((2, w, m), BF),
        expm=VM((LANES, w), BF),
        normed=VM((r, m), BF),
        xc=VM((r, w), F32),
        cums=VM((2, r, LANES), F32),
        go=VM((r, w), BF),
        local=VM((lay.nb, n, w), F32),
        tmp=VM((16, LANES), F32),
        part=VM((peers, r, lay.share), BF),
        own_part=VM((r, lay.share), F32),
        got=VM((peers, r, lay.share), BF),
        wsem=dma((5,)),
        psem=dma((9,)),
        vsem=dma((5,)),
        rs_send=dma((peers, lay.nb)),
        rs_recv=dma((peers, lay.nb)),
        ag_send=dma((peers, lay.nb)),
        ag_recv=dma((peers, lay.nb)),
    )
    out.update(fwd_scratch(lay))
    out.update(scan_scratch(lay, ["f_"]))
    return out


def pack(lay, v):
    c, w, heads, off = lay.c, lay.width, lay.heads, lay.off
    f = lambda ref: ref[...].astype(F32)
    v.tmp[...] = jnp.zeros(v.tmp.shape, F32)
    v.tmp[0:4, :off] = f(v.conv_sm)
    v.tmp[4:5, :off] = f(v.bias_sm)
    v.tmp[8:9, :heads] = v.step_bias[...]
    v.tmp[9:10, :heads] = -jnp.exp(v.decay[...])
    v.tmp[10:11, :heads] = v.skip[...]
    rows = v.tmp[8:16, :]
    groups = rows * 0.0
    for k in range(3):
        groups = groups + pltpu.roll(rows, off + k * GROUP, 1)
    v.pk[c] = jnp.zeros((16, w), F32)
    v.pk[c, 0:4, :] = f(v.conv_x)
    v.pk[c, 4:5, :] = f(v.bias_x)
    v.pk[c, 5:6, :] = f(v.gain_out)
    v.pk[c, 6:7, :] = expand(lay, v.expm[...], groups)[2:3, :]
    rms = f(v.rms)
    for k in range(lay.model // w):
        v.pk[c, 7 + k : 8 + k, :] = rms[:, k * w : (k + 1) * w]
    for k in range(5):
        v.pk[c, 9:10, k * LANES : (k + 1) * LANES] = v.tmp[k : k + 1, :]
    for k in range(2):
        v.pk[c, 10:11, k * LANES : (k + 1) * LANES] = groups[k : k + 1, :]


def start_kernel(lay, *refs):
    v = Names(start_ins() + list(start_outs(lay)) + list(start_scratch(lay)), refs)
    lay.place()
    c, q, nb = lay.c, lay.q, lay.nb
    both, own_w = (v.wg, v.wx, v.wsm, v.wo), (v.own0, v.own1, v.own2, v.own3)
    kept_w = (v.other0, v.other1, v.other2, v.other3)
    order = (2, 1, 0, 3)
    loads = [pltpu.make_async_copy(v.tokens.at[c], v.resid, v.wsem.at[4])]
    loads += [
        pltpu.make_async_copy(own_w[k], both[k].at[c], v.wsem.at[at]) for at, k in enumerate(order)
    ]
    for load in loads:
        load.start()
    v.expm[...] = expander(lay)
    pack(lay, v)
    meet(column_and_heads(lay))
    swaps = [remote(v.pk.at[c], v.pk.at[c], v.psem.at[4], v.vsem.at[4], lay.sibling())]
    swaps += [
        remote(own_w[k], both[k].at[c], v.psem.at[at], v.vsem.at[at], lay.sibling())
        for at, k in enumerate(order)
    ]
    for copy in swaps:
        copy.start()
    keeps = [
        pltpu.make_async_copy(both[k].at[1 - c], kept_w[k], v.psem.at[5 + at])
        for at, k in enumerate(order)
    ]
    wg, wx, wsm, wo = (ref.at[0] for ref in both)
    swaps[0].wait()
    loads[0].wait()

    def ready(at):
        loads[1 + at].wait()
        swaps[1 + at].wait()
        keeps[at].start()

    peers = lay.heads_peers()
    chunks = [[] for _ in range(nb)]

    def project():
        for k, target in peers + [(0, None)]:
            owner = lax.rem(q + k, lay.parts)
            cols = pl.ds(pl.multiple_of(owner * lay.share, LANES), lay.share)
            product = dot(v.go[...], wo[:, cols])
            if k == 0:
                v.own_part[...] = product
                continue
            v.part[k - 1] = product.astype(BF)
            for i in range(nb):
                rows = pl.ds(i * Q, Q)
                copy = remote(
                    v.part.at[k - 1, rows],
                    v.got.at[k - 1, rows],
                    v.rs_send.at[k - 1, i],
                    v.rs_recv.at[k - 1, i],
                    target,
                )
                copy.start()
                chunks[i].append(copy)

    p = params(lay, v.pk, 0)
    forward(lay, v, p, v.resid, (wsm, wx, wg), ready, project)
    cols = pl.ds(pl.multiple_of(q * lay.share, LANES), lay.share)
    given = []
    for i in range(nb):
        rows = pl.ds(i * Q, Q)
        for copy in chunks[i]:
            copy.wait()
        total = v.own_part[rows, :]
        for k, _ in peers:
            total = total + v.got[k - 1, rows, :].astype(F32)
        row = v.sqt[8 * i : 8 * i + 1, :]
        value = v.resid[rows, cols].astype(F32) + to_col(lax.rsqrt(row / lay.inner + EPS)) * total
        v.hid[rows, :] = value
        v.full[rows, cols] = value.astype(BF)
        for k, target in peers:
            copy = remote(
                v.full.at[rows, cols],
                v.full.at[rows, cols],
                v.ag_send.at[k - 1, i],
                v.ag_recv.at[k - 1, i],
                target,
            )
            copy.start()
            given.append(copy)
    for copy in given + keeps:
        copy.wait()


def start_layer(lay, *args):
    outs, scratch = start_outs(lay), start_scratch(lay)
    vmem, hbm = pl.BlockSpec(memory_space=VM), pl.BlockSpec(memory_space=HB)
    got = pl.pallas_call(
        functools.partial(start_kernel, lay),
        out_shape=tuple(outs.values()),
        in_specs=[hbm] * 5 + [vmem] * (len(args) - 5),
        out_specs=tuple([vmem] * (len(outs) - 4) + [hbm] * 4),
        scratch_shapes=list(scratch.values()),
        compiler_params=pltpu.CompilerParams(
            collective_id=1, has_side_effects=True, vmem_limit_bytes=58 << 20
        ),
        name="mixer_start",
    )(*args)
    return Names(list(outs), got)


EARLIER = ["prev_x", "prev_s", "done_o", "done_g", "done_x", "small", "hid0", "hid1", "gt1"]
X_EARLY = 1


def staged(lay):
    r, w, m = lay.rows, lay.width, lay.model
    rest = m // 2 - m // 2 // N_X * X_EARLY
    out = dict(prev_x=((rest, w), BF), prev_s=((m // 2, LANES), BF), pk=((2, 16, w), F32))
    kept = kept_shapes(lay)
    for name in ("sm", "xp", "ysd", "gate", "sqt"):
        out[name] = kept[name]
    out["up"] = ((r, m), BF)
    for name in ("nt", "bc", "sin"):
        out[name] = kept[name]
    out.update(done_o=((w // 2, m), BF), done_g=((m // 2, w), BF))
    out.update(done_x=((m // 2 // N_X * X_EARLY, w), BF), small=((16, w), F32))
    return out


def back_ins(lay, more):
    weights = [f"own{k}" for k in range(4)] + [f"other{k}" for k in range(4)]
    if more:
        return ["from_" + name for name in staged(lay)] + ["tokens"] + weights + EARLIER[-3:]
    return ["cotangent", "resid"] + weights + ["pk"]


def back_outs(lay, late, gather, more):
    r, w, m = lay.rows, lay.width, lay.model
    sds = jax.ShapeDtypeStruct
    out = dict(gt=sds((r, lay.share), F32))
    if more:
        out["total"] = sds((16 + 8 * lay.parts, w), F32)
    else:
        out.update(
            sum_o=sds((w // 2, m), BF),
            sum_g=sds((m // 2, w), BF),
            sum_x=sds((m // 2 // N_X * X_EARLY, w), BF),
            rest_x=sds((m // 2 - m // 2 // N_X * X_EARLY, w), BF),
            own_s=sds((m // 2, LANES), BF),
            psm=sds((16, w), F32),
        )
    if gather:
        out["full"] = sds((r, m), BF)
    if late:
        out["hid"] = sds((r, lay.share), F32)
    if more:
        out.update(
            fin_o=sds((w, m), BF),
            fin_g=sds((m, w), BF),
            fin_x=sds((m, w), BF),
            fin_s=sds((m, LANES), BF),
            got_hid=sds((r, lay.share), F32),
            got_gt=sds((r, lay.share), F32),
        )
    return out


N_OUT = N_GATE = N_X = 4


def back_scratch(lay, late, gather, more):
    r, w, m, n, nb = lay.rows, lay.width, lay.model, lay.state, lay.nb
    dma = pltpu.SemaphoreType.DMA
    peers = lay.parts - 1
    n_sem = 2 * peers + 2 + 4 + peers
    n_seq = N_OUT + N_GATE + (2 * (N_X + 1) - X_EARLY if more else X_EARLY)
    out = dict(
        wg=VM((m, w), BF),
        wx=VM((m, w), BF),
        wsm=VM((m, LANES), BF),
        wo=VM((w, m), BF),
        expm=VM((LANES, w), BF),
        xc=VM((r, w), F32),
        dy=VM((r, w), F32),
        dx=VM((r, w), F32),
        cums=VM((2, r, LANES), F32),
        rcs=VM((r, LANES), F32),
        lowg=VM((r, w), BF),
        lowx=VM((r, w), BF),
        lowsm=VM((r, LANES), BF),
        no=VM((r, w), BF),
        rsb=VM((lay.parts, 8 * nb, Q), F32),
        lamloc=VM((nb, n, w), F32),
        dsuf=VM((8 * nb, LANES), F32),
        dbc=VM((r, 2 * n), F32),
        dbs=VM((lay.parts, r // 2, LANES), BF),
        dbr=VM((peers, r // 2, LANES), BF),
        xdp=VM((r + 16, w), F32),
        smdp=VM((r + 16, LANES), F32),
        hxs=VM((16, w), BF),
        hxr=VM((16, w), BF),
        hss=VM((16, LANES), BF),
        hsr=VM((16, LANES), BF),
        dsp=VM((r, LANES), F32),
        gr_g=VM((m // 2, w), BF),
        gr_x=VM((m // 2, w), BF),
        gs_o=VM((w // 2, m), BF),
        gr_o=VM((w // 2, m), BF),
        gr_s=VM((m // 2, LANES), BF),
        rdacc=VM((r, LANES), F32),
        acch=VM((8, LANES), F32),
        own_o=VM((w // 2, m), BF),
        own_g=VM((m // 2, w), BF),
        in_o=VM((w // 2, m), BF),
        in_g=VM((m // 2, w), BF),
        in_x=VM((m // 2, w), BF),
        dnp=VM((lay.parts, r, lay.share), BF),
        got=VM((peers, r, lay.share), BF),
        rd2=VM((8 * nb, Q), F32),
        got_rows=VM((peers, 8 * nb, Q), F32),
        gains=VM((8, m), F32),
        wsem=dma((5,)),
        ssem=dma((n_sem,)),
        rsem=dma((n_sem,)),
        rs_send=dma((peers, nb)),
        rs_recv=dma((peers, nb)),
        seq1=dma((n_seq,)),
        seq2=dma((n_seq,)),
        seq3=dma((n_seq,)),
        seq4=dma((n_seq,)),
    )
    if gather:
        out.update(ag_send=dma((peers, nb)), ag_recv=dma((peers, nb)))
    out["own_x"] = VM((m // 2, w), BF)
    if more:
        for kind in ("in_s", "in_ps", "own_s", "sum_s", "sum_ps"):
            out[kind] = VM((m // 2, LANES), BF)
        for kind in ("sum_x", "sum_g"):
            out[kind] = VM((m // 2, w), BF)
        for kind in ("in_px", "sum_px"):
            out[kind] = VM((m // 2 - m // 2 // N_X * X_EARLY, w), BF)
        column = 2 * lay.seqs
        out.update(
            sum_o=VM((w // 2, m), BF),
            psm=VM((16, w), F32),
            slots=VM((column, 16, w), F32),
            rest_rows=VM((lay.parts, 8, w), F32),
            fin_sem=dma((3, n_seq + 3)),
            pair_sem=dma((2, 2)),
            slot_sem=dma((2, column - 1)),
            part_sem=dma((2, peers)),
        )
        out["resid"] = VM((r, m), BF)
        out.update({name: VM(*spec) for name, spec in staged(lay).items()})
        out["stage_sem"] = dma((len(staged(lay)),))
    out.update(scan_scratch(lay, ["b_"] if more else ["f_", "b_"]))
    if late:
        out.update(
                late_got=VM((peers, r, lay.share), BF),
            late_send=dma((peers,)),
            late_recv=dma((peers,)),
            up=VM((r, m), BF),
        )
        out.update({name: VM(*spec) for name, spec in kept_shapes(lay).items()})
        out.update(fwd_scratch(lay))
    return out


def bwd_kernel(lay, layer, late, gather, more, *refs):
    outs, scratch = back_outs(lay, late, gather, more), back_scratch(lay, late, gather, more)
    v = Names(back_ins(lay, more) + list(outs) + list(scratch), refs)
    lay.place()
    c, z, q = lay.c, lay.z, lay.q
    nb, w, n, m = lay.nb, lay.width, lay.state, lay.model
    half = lay.rows // 2
    own_w, other_w = (v.own0, v.own1, v.own2, v.own3), (v.other0, v.other1, v.other2, v.other3)
    loads = [
        Load(own_w[k], other_w[k], (v.wg, v.wx, v.wsm, v.wo)[k], v.wsem.at[at], c == layer)
        for at, k in enumerate((3, 0, 1, 2) if more else (2, 1, 0, 3))
    ]
    stages = {}
    if more:
        for k, name in enumerate(staged(lay)):
            src, dst = getattr(v, "from_" + name), getattr(v, name)
            stages[name] = pltpu.make_async_copy(src, dst, v.stage_sem.at[k])
            stages[name].start()
        rows_in = pltpu.make_async_copy(v.tokens.at[c], v.resid, v.wsem.at[4])
    else:
        rows_in = pltpu.make_async_copy(v.cotangent.at[c], v.up, v.wsem.at[4])
    for load in loads + [rows_in]:
        load.start()
    meet(column_and_heads(lay))
    peers = lay.heads_peers()
    counter = iter(range(64))

    def send(src, dst, target):
        at = next(counter)
        copy = remote(src, dst, v.ssem.at[at], v.rsem.at[at], target)
        copy.start()
        return copy

    out_pieces = pieces_of(v.own_o, v.in_o, v.sum_o, N_OUT)
    gate_pieces = pieces_of(v.own_g, v.in_g, v.sum_g, N_GATE)
    finals = []

    def plan_settling(ref, fin, of, rows, skipped=0):
        size = ref.shape[0] if rows is None else rows.size
        offset = skipped + (0 if rows is None else rows.start)
        at = len(finals)
        into = fin.at[pl.ds(pl.multiple_of(c * (fin.shape[0] // 2) + offset, 16), size)]
        src = ref if rows is None else ref.at[rows]
        here = pltpu.make_async_copy(src, into, v.fin_sem.at[0, at])
        there = remote(src, into, v.fin_sem.at[1, at], v.fin_sem.at[2, at], lay.sibling())
        finals.append((of, here, there))

    def settle(at):
        of, here, there = finals[at]
        pl.when(c == of)(here.start)
        pl.when(c != of)(there.start)

    if more:
        kinds = [(pieces_of(v.prev_x, v.in_px, v.sum_px, N_X - X_EARLY), v.fin_x, 1)]
        kinds += [(pieces_of(v.prev_s, v.in_ps, v.sum_ps, 1), v.fin_s, 1)]
        kinds += [(out_pieces, v.fin_o, 0), (gate_pieces, v.fin_g, 0)]
        kinds += [(pieces_of(v.own_x, v.in_x, v.sum_x, N_X), v.fin_x, 0)]
        kinds += [(pieces_of(v.own_s, v.in_s, v.sum_s, 1), v.fin_s, 0)]
        listed = [(piece, fin, of) for pieces, fin, of in kinds for piece in pieces]

        for (_, _, result, rows), fin, of in listed:
            skipped = m // 2 // N_X * X_EARLY if result is v.sum_px else 0
            plan_settling(result, fin, of, rows, skipped)
        done = settle
        plan_settling(v.done_o, v.fin_o, 1, None)
        plan_settling(v.done_g, v.fin_g, 1, None)
        plan_settling(v.done_x, v.fin_x, 1, None)
        pairs = [
            [
                remote(src, dst, v.pair_sem.at[0, k], v.pair_sem.at[1, k], lay.sibling())
                for src in srcs
            ]
            for k, (dst, srcs) in enumerate(
                ((v.got_hid, (v.hid1, v.hid0)), (v.got_gt, (v.gt1, v.gt)))
            )
        ]
        pl.when(c == 0)(pairs[0][0].start)
        pl.when(c == 1)(pairs[0][1].start)
        pl.when(c == 0)(pairs[1][0].start)
    else:
        x_pieces = pieces_of(v.own_x, v.in_x, v.sum_x, N_X)[:X_EARLY]
        listed = [(piece,) for piece in out_pieces + gate_pieces + x_pieces]
        done = None
    pump = Pump(
        SeqSum(lay, [entry[0] for entry in listed], (v.seq1, v.seq2, v.seq3, v.seq4)), done
    )
    tick = pump.tick
    scan = Scan(lay, False, v.expm, scan_refs(v, "b_"))
    if more:
        for name in ("prev_x", "prev_s"):
            stages.pop(name).wait()
        pump.ready += N_X - X_EARLY + 1
        pump.feed()
        for stage in stages.values():
            stage.wait()
        for at in range(len(listed), len(finals)):
            settle(at)

    p = params(lay, v.pk, layer)
    v.expm[...] = expander(lay)
    expm = v.expm
    v.psm[...] = jnp.zeros(v.psm.shape, F32)
    v.acch[...] = jnp.zeros(v.acch.shape, F32)
    lower, upper, strict = tri("lower"), tri("upper"), tri("strict")
    col_n = 256

    def cols_at(j, size=col_n):
        return pl.ds(pl.multiple_of(j * size, LANES), size)

    def tile(i):
        return pl.ds(pl.multiple_of(8 * i, 8), 8)

    def weight_grad(left, low, theirs, got, own):
        width = low.shape[1]
        step_n = min(width, col_n)
        for side, into in ((1 - c, theirs), (c, own)):
            rows = left(side)

            @pl.loop(0, width // step_n)
            def _(j):
                at = cols_at(j, step_n)
                into[:, at] = dot(rows, low[:, at]).astype(BF)

            if into is theirs:
                copy = send(theirs, got, lay.sibling())
        return copy

    def pair_sum(copy, own, got):
        copy.wait()
        own[...] = (own[...].astype(F32) + got[...].astype(F32)).astype(BF)

    def normed_half(side):
        return v.nt[pl.ds(pl.multiple_of(side * (m // 2), 16), m // 2), :]

    def out_half(side):
        return jnp.transpose(v.no[:, pl.ds(pl.multiple_of(side * (w // 2), LANES), w // 2)])

    late_sums = []

    def project():
        for k in range(lay.parts):
            cols = slice(k * lay.share, (k + 1) * lay.share)
            v.dnp[k] = dot(v.go[...], v.wo[:, cols]).astype(BF)

    def out_grad():
        @pl.loop(0, w // col_n)
        def _(j):
            v.dy[:, cols_at(j)] = dot(v.up[...], v.wo[cols_at(j), :], NT)

    if more:
        tables = run_decays(lay, v, p)
    else:
        v.normed, v.go, v.local = v.full, v.lowx, v.lamloc
        weights = (v.wsm, v.wx, v.wg)

        def meanwhile():
            loads[3].wait()
            rows_in.wait()
            out_grad()

        forward(lay, v, p, v.resid, weights, lambda at: loads[at].wait(), project, meanwhile)
        tables = []

    @pl.loop(0, nb)
    def _(i):
        if more:
            pre = conv_pre(conv_cat(v.xp, i), p["conv_x"], p["bias_x"])
            v.xc[block(i), :] = pre * jax.nn.sigmoid(pre)
        x = v.xc[block(i), :]
        g = v.gate[block(i), :]
        gated = (v.ysd[block(i), :] + p["skip"] * x) * (g * jax.nn.sigmoid(g))
        inv = to_col(lax.rsqrt(v.sqt[tile(i), :][:1, :] / lay.inner + EPS))
        v.no[block(i), :] = (gated * inv * p["gain_out"]).astype(BF)

    if more:
        rows_in.wait()
        tick()
    copy_o = weight_grad(out_half, v.up, v.gs_o, v.gr_o, v.own_o)
    if more:
        loads[0].wait()
        out_grad()

    @pl.loop(0, nb)
    def _(i):
        g = v.gate[block(i), :]
        gated = (v.ysd[block(i), :] + p["skip"] * v.xc[block(i), :]) * (g * jax.nn.sigmoid(g))
        row = to_row(v.dy[block(i), :] * p["gain_out"] * gated)
        v.rsb[q, tile(i), :] = jnp.broadcast_to(row, (8, Q))

    row_sends = [send(v.rsb.at[q], v.rsb.at[q], target) for _, target in peers]
    pair_sum(copy_o, v.own_o, v.gr_o)
    pump.ready += N_OUT
    if more:
        tick()
    pump.feed()
    for copy in row_sends:
        copy.wait()
    if late:
        for k, target in peers:
            copy = remote(
                v.dnp.at[lax.rem(q + k, lay.parts)],
                v.late_got.at[k - 1],
                v.late_send.at[k - 1],
                v.late_recv.at[k - 1],
                target,
            )
            copy.start()
            late_sums.append(copy)
    @pl.loop(0, nb)
    def _(i):
        rd = v.rsb[0, tile(i), :]
        for k in range(1, lay.parts):
            rd = rd + v.rsb[k, tile(i), :]
        inv = to_col(lax.rsqrt(v.sqt[tile(i), :][:1, :] / lay.inner + EPS))
        rdc = to_col(rd[:1, :])
        g, x, d = v.gate[block(i), :], v.xc[block(i), :], v.dy[block(i), :]
        sg = jax.nn.sigmoid(g)
        act = g * sg
        mixed = v.ysd[block(i), :] + p["skip"] * x
        gated = mixed * act
        v.psm[5:6, :] += jnp.sum(d * (gated * inv), axis=0, keepdims=True)
        dgated = inv * p["gain_out"] * d - gated * (inv * inv * inv * rdc / lay.inner)
        dmix = dgated * act
        v.lowg[block(i), :] = (dgated * mixed * (sg * (1.0 + g * (1.0 - sg)))).astype(BF)
        v.psm[8:9, :] += jnp.sum(dmix * x, axis=0, keepdims=True)
        v.dy[block(i), :] = dmix

    lam = jnp.zeros((n, w), F32)
    total = jnp.zeros((1, LANES), F32)
    for i in reversed(range(nb)):
        rows = pl.ds(i * Q, Q)
        cum = v.cums[1, rows, :]
        last = cum[Q - 1 :, :]
        v.lamloc[i] = lam
        v.dsuf[8 * i : 8 * (i + 1), :] = jnp.broadcast_to(total, (8, LANES))
        faded = (expand(lay, expm[...], jnp.exp(cum)) * v.dy[rows, :]).astype(BF)
        dec = expand(lay, expm[...], jnp.broadcast_to(jnp.exp(last), (8, LANES)))[:1, :]
        lam = lam * dec + dot(v.bc[rows, n:], faded, TN)
        total = total + last
    if more:
        tick()
    v.own_state[...] = lam
    for copy in tables:
        copy.wait()
    scan.start()

    copy_g = weight_grad(
        normed_half, v.lowg, v.wo.at[:, :w], v.gr_g, v.own_g
    )
    pair_sum(copy_g, v.own_g, v.gr_g)
    pump.ready += N_GATE
    tick()

    in_loop = pump.later() if more else None

    @pl.loop(0, nb)
    def _(i):
        if scan.steps > 1:
            pl.when(i == 2)(functools.partial(scan.advance, 0))
        if more:
            pl.when(i == 3)(in_loop)
        causal = iota((Q, Q), 0) >= iota((Q, Q), 1)
        cum = v.cums[1, block(i), :]
        cum_t = jnp.transpose(cum)
        b_rows, c_rows = v.bc[block(i), :n], v.bc[block(i), n:]
        scores = dot(c_rows, b_rows, NT)
        stepped = (v.xc[block(i), :] * expand(lay, expm[...], v.cums[0, block(i), :])).astype(BF)
        grad = v.dy[block(i), :]
        low = grad.astype(BF)
        dscores = jnp.zeros((Q, Q), F32)
        for pair in range(lay.heads // 2):
            cols = slice(pair * LANES, (pair + 1) * LANES)
            fades = [decay_tile(cum, cum_t, lay.off + 2 * pair + e, causal) for e in range(2)]
            mixes = [(scores * fade).astype(BF) for fade in fades]
            xl, xr = halves(stepped[:, cols])
            dl, dr = halves(low[:, cols])
            dmix = dot(low[:, cols], jnp.concatenate([xl, xr], axis=0), NT)
            dscores = dscores + dmix[:, :Q] * fades[0] + dmix[:, Q:] * fades[1]
            v.dx[block(i), cols] = dot(
                jnp.concatenate(mixes, axis=0), jnp.concatenate([dl, dr], axis=0), TN
            )
        diff = low.astype(F32) * v.ysd[block(i), :] - stepped.astype(F32) * v.dx[block(i), :]
        v.rcs[block(i), :] = sum3(upper, head_sum(expm[...], diff))
        faded = (expand(lay, expm[...], jnp.exp(cum)) * grad).astype(BF)
        dsc = dscores.astype(BF)
        v.dbc[block(i), :n] = dot(dsc, c_rows, TN)
        v.dbc[block(i), n:] = dot(dsc, b_rows) + dot2(faded, v.sin[i], NT)

    for step in range(1 if scan.steps > 1 else 0, scan.steps):
        scan.advance(step)
    scan.hand_over()
    tick()
    scan.result()
    carry = v.enter[...]
    at = next(counter)
    halo_x = remote(v.hxs, v.hxr, v.ssem.at[at], v.rsem.at[at], lay.prev_run())

    in_loop = pump.later()

    @pl.loop(0, nb)
    def _(i):
        pl.when(i == 2)(in_loop)
        cat = conv_cat(v.xp, i)
        pre = conv_pre(cat, p["conv_x"], p["bias_x"])
        x = v.xc[block(i), :]
        step, cum = v.cums[0, block(i), :], v.cums[1, block(i), :]
        last = cum[Q - 1 :, :]
        fade = expand(lay, expm[...], jnp.exp(last - cum))
        step_w = expand(lay, expm[...], step)
        gone = jnp.exp(v.dsuf[tile(i), :])
        lam_out = v.lamloc[i] + expand(lay, expm[...], gone)[:1, :] * carry
        lam_b = dot2(v.bc[block(i), :n], lam_out)
        xw = x * step_w * fade
        v.dbc[block(i), :n] += dot2(xw.astype(BF), lam_out, NT)
        within = jnp.sum(lam_out * v.sin[i], axis=0, keepdims=True)
        kept = head_sum(expm[...], jnp.broadcast_to(within, (8, w)))[:1, :] * jnp.exp(last)
        dxt = v.dx[block(i), :] + fade * lam_b
        g = v.rcs[block(i), :] + sum3(strict, head_sum(expm[...], xw * lam_b)) + kept
        dstep = head_sum(expm[...], x * dxt) + p["rate"] * g
        v.acch[1:2, :] += jnp.sum(step * g, axis=0, keepdims=True)
        dpre_step = dstep * jax.nn.sigmoid(v.sm[block(i, base=16), :] + p["step_bias"])
        v.acch[0:1, :] += jnp.sum(dpre_step, axis=0, keepdims=True)
        v.dsp[block(i), :] = dpre_step
        d_xin = step_w * dxt + p["skip"] * v.dy[block(i), :]
        dpre = d_xin * silu_grad(pre)
        v.xdp[block(i), :] = dpre
        for k in range(4):
            v.psm[k : k + 1, :] += jnp.sum(dpre * cat[5 + k : 5 + k + Q, :], axis=0, keepdims=True)
        v.psm[4:5, :] += jnp.sum(dpre, axis=0, keepdims=True)

        @pl.when(i == 0)
        def _():
            v.hxs[...] = v.xdp[:16, :].astype(BF)
            halo_x.start()

    sel_top, sel_bottom = selectors(lay)
    pieces = dot(v.dbc[:half, :].astype(BF), sel_top, NT) + dot(
        v.dbc[half:, :].astype(BF), sel_bottom, NT
    )
    for k in range(lay.parts):
        v.dbs[k] = pieces[:, k * LANES : (k + 1) * LANES].astype(BF)
    bc_sends = [
        send(v.dbs.at[lax.rem(q + k, lay.parts)], v.dbr.at[k - 1], target) for k, target in peers
    ]
    inside = jnp.where((c == 1) & (z == lay.seqs - 1), 0.0, 1.0)
    tick()
    if late:
        for copy in late_sums:
            copy.wait()
        cols = pl.ds(pl.multiple_of(q * lay.share, LANES), lay.share)
        for i in range(nb):
            rows = pl.ds(i * Q, Q)
            value = v.dnp[q, rows, :].astype(F32)
            for k, _ in peers:
                value = value + v.late_got[k - 1, rows, :].astype(F32)
            inv = to_col(lax.rsqrt(v.sqt[8 * i : 8 * i + 1, :] / lay.inner + EPS))
            v.hid[rows, :] = v.resid[rows, cols].astype(F32) + inv * value
    halo_x.wait()
    v.xdp[lay.rows :, :] = v.hxr[...].astype(F32) * inside

    @pl.loop(0, nb)
    def _(i):
        cat = v.xdp[pl.ds(pl.multiple_of(i * Q, 8), Q + 8), :]
        grad = jnp.zeros((Q, w), F32)
        for k in range(4):
            grad = grad + p["conv_x"][k : k + 1, :] * cat[3 - k : 3 - k + Q, :]
        v.lowx[block(i), :] = grad.astype(BF)

    for load in loads[1:] if more else []:
        load.wait()
    copy_x = weight_grad(normed_half, v.lowx, v.wo.at[:, w:], v.gr_x, v.own_x)
    tick()

    for copy in bc_sends:
        copy.wait()
    summed = v.dbs[q].astype(F32)
    for k in range(1, lay.parts):
        summed = summed + v.dbr[k - 1].astype(F32)
    for i in range(nb):
        rows = pl.ds(i * Q, Q)
        if i < nb // 2:
            d_conv = summed[i * Q : (i + 1) * Q, :]
        else:
            d_conv = pltpu.roll(summed[i * Q - half : (i + 1) * Q - half, :], LANES // 2, 1)
        cat = conv_cat(v.sm, i)
        pre = conv_pre(cat, p["conv_sm"], p["bias_sm"])
        valid = iota((Q, LANES), 1) < lay.off
        dpre = jnp.where(valid, d_conv * silu_grad(pre), 0.0)
        v.smdp[rows, :] = dpre
        for k in range(4):
            v.psm[7:8, k * LANES : (k + 1) * LANES] += jnp.sum(
                dpre * cat[5 + k : 5 + k + Q, :], axis=0, keepdims=True
            )
        v.psm[7:8, 4 * LANES : 5 * LANES] += jnp.sum(dpre, axis=0, keepdims=True)
    v.hss[...] = v.smdp[:16, :].astype(BF)
    halo_s = send(v.hss, v.hsr, lay.prev_run())
    v.psm[6:7, :LANES] = head_sum(expm[...], v.psm[8:9, :])
    v.psm[6:7, LANES : 2 * LANES] = v.acch[0:1, :]
    v.psm[6:7, 2 * LANES : 3 * LANES] = v.acch[1:2, :] * p["rate"]
    pair_sum(copy_x, v.own_x, v.gr_x)
    halo_s.wait()
    v.smdp[lay.rows :, :] = v.hsr[...].astype(F32) * inside
    for i in range(nb):
        rows = pl.ds(i * Q, Q)
        cat = v.smdp[i * Q : (i + 1) * Q + 8, :]
        grad = jnp.zeros((Q, LANES), F32)
        for k in range(4):
            grad = grad + p["conv_sm"][k : k + 1, :] * cat[3 - k : 3 - k + Q, :]
        lane = iota((Q, LANES), 1)
        first = jnp.where(lane < lay.off + GROUP, v.dsp[rows, :], 0.0)
        v.lowsm[rows, :] = jnp.where(lane < lay.off, grad, first).astype(BF)
    copy_s = weight_grad(normed_half, v.lowsm, v.wo.at[:, :LANES], v.gr_s, v.own_s)
    pump.ready += N_X if more else X_EARLY
    if not more:
        v.rest_x[...] = v.own_x[m // 2 // N_X * X_EARLY :, :]
    tick()

    v.rdacc[...] = jnp.zeros(v.rdacc.shape, F32)
    v.gains[...] = jnp.broadcast_to(p["gain"], (8, m))
    spread = (v.full, v.ag_send, v.ag_recv) if gather else ()
    head_sum_of = HeadSum(lay, v.dnp, v.got, v.rs_send, v.rs_recv, *spread)
    for k in (3, 1, 2, 0):
        cols = head_sum_of.cols(k)
        grad = dot(v.lowg[...], v.wg[cols, :], NT) + dot(v.lowx[...], v.wx[cols, :], NT)
        grad = grad + dot(v.lowsm[...], v.wsm[cols, :], NT)
        v.dnp[k] = grad.astype(BF)
        v.rdacc[...] += fold(grad * v.gains[:1, cols] * v.resid[:, cols].astype(F32))
        for i in range(nb):
            if k == head_sum_of.near(i):
                head_sum_of.first(i)
    for i in range(nb):
        row = to_row(v.rdacc[i * Q : (i + 1) * Q, :])
        v.rd2[8 * i : 8 * (i + 1), :] = jnp.broadcast_to(row, (8, Q))
    rd_sends = [send(v.rd2, v.got_rows.at[k - 1], target) for k, target in peers]
    pair_sum(copy_s, v.own_s, v.gr_s)
    if more:
        pump.ready += 1
    cols = pl.ds(pl.multiple_of(q * lay.share, LANES), lay.share)
    own_gain = v.gains[:1, cols]
    tick()
    for copy in rd_sends:
        copy.wait()
    inner = v.rd2[...]
    for k, _ in peers:
        inner = inner + v.got_rows[k - 1]
    rms_sum = jnp.zeros((1, lay.share), F32)
    for i in range(nb + 2):
        if i < nb:
            head_sum_of.second(i)
        if 1 <= i <= nb:
            at = i - 1
            rows = pl.ds(at * Q, Q)
            total = head_sum_of.total(at)
            start = v.resid[rows, cols].astype(F32)
            x = v.resid[rows, :].astype(F32)
            scale = lax.rsqrt(jnp.mean(x * x, axis=1, keepdims=True) + EPS)
            value = (
                v.up[rows, cols].astype(F32)
                + scale * (own_gain * total)
                - start * (scale * scale * scale * to_col(inner[8 * at : 8 * at + 1, :] / m))
            )
            rms_sum = rms_sum + jnp.sum(total * start * scale, axis=0, keepdims=True)
            v.gt[rows, :] = value
            if gather:
                v.full[rows, cols] = value.astype(BF)
                head_sum_of.give(at)
        if i >= 2 and gather:
            head_sum_of.relay(i - 2)
        if i % 2:
            tick()
    v.psm[8:9, :] = jnp.zeros((1, w), F32)
    v.psm[8:9, : lay.share] = rms_sum
    if more:
        pl.when(c == 1)(pairs[1][1].start)
        column = [(a, b) for a in range(2) for b in range(lay.seqs) if a or b]
        own_slot = c * lay.seqs + z
        smalls = []
        for at, (a, b) in enumerate(column):
            to_c, to_z = (c + a) % 2, lax.rem(z + b, lay.seqs)
            to = (to_c, to_z, q)
            pair = [
                remote(src, v.slots.at[own_slot], v.slot_sem.at[0, at], v.slot_sem.at[1, at], to)
                for src in (v.psm, v.small)
            ]
            pl.when(to_c == 0)(pair[0].start)
            pl.when(to_c == 1)(pair[1].start)
            smalls.append(pair[0])
        v.slots[own_slot] = jnp.where(c == 0, v.psm[...], v.small[...])
        tick()
        for copy in smalls:
            copy.wait()
        value = v.slots[0]
        for k in range(1, 2 * lay.seqs):
            value = value + v.slots[k]
        v.total[:16, :] = value
        v.rest_rows[q] = value[8:16, :]
        parts = []
        for k, target in peers:
            copy = remote(
                v.rest_rows.at[q],
                v.rest_rows.at[q],
                v.part_sem.at[0, k - 1],
                v.part_sem.at[1, k - 1],
                target,
            )
            copy.start()
            parts.append(copy)
        tick()
        for copy in parts:
            copy.wait()
        for k in range(lay.parts):
            v.total[16 + 8 * k : 24 + 8 * k, :] = v.rest_rows[k]
    pump.finish()
    if gather:
        head_sum_of.finish()
    if more:
        for of, here, there in finals:
            pl.when(c == of)(here.wait)
            pl.when(c == of)(there.wait_recv)
            pl.when(c != of)(there.wait_send)
        for pair in pairs:
            pair[0].wait()


def bwd_layer(lay, layer, args, more):
    late = gather = not more
    outs, scratch = back_outs(lay, late, gather, more), back_scratch(lay, late, gather, more)
    vmem, hbm = pl.BlockSpec(memory_space=VM), pl.BlockSpec(memory_space=HB)
    names = back_ins(lay, more)
    specs = [vmem if name in ("resid", "pk") else hbm for name in names]
    out_specs = [vmem] * len(outs)
    if more:
        out_specs[-6:] = [hbm] * 6
    got = pl.pallas_call(
        functools.partial(bwd_kernel, lay, layer, late, gather, more),
        out_shape=tuple(outs.values()),
        in_specs=specs,
        out_specs=tuple(out_specs),
        scratch_shapes=list(scratch.values()),
        compiler_params=pltpu.CompilerParams(
            collective_id=5 + layer, has_side_effects=True, vmem_limit_bytes=63 << 20
        ),
        name=f"mixer_backward_{layer}",
    )(*(args[name.removeprefix("from_")] for name in names))
    return Names(list(outs), got)


def on_device(
    mesh_shape, tokens, cotangent, rms_gain, proj_gate, proj_x, proj_bc, proj_step, conv_x, conv_x_bias,
    conv_bc, conv_bc_bias, step_bias, decay_log, skip_gain, norm_gain, proj_out,
):
    pieces, rows, model = tokens.shape
    width, heads, local_state = proj_x.shape[2], proj_step.shape[2], proj_bc.shape[3]
    lay = Lay(mesh_shape, rows, width, model, heads, local_state)
    section = lax.axis_index("section")
    group = jnp.pad(proj_step[0], ((0, 0), (0, GROUP - heads)))
    w_small = jnp.concatenate(
        [
            proj_bc[0].reshape(model, lay.off),
            group,
            group,
            group,
            jnp.zeros((model, LANES - lay.off - 3 * GROUP), BF),
        ],
        axis=1,
    )
    taps = conv_x.shape[1]
    own = (proj_gate[0], proj_x[0], w_small, proj_out[0])
    first = start_layer(
        lay,
        tokens,
        *own,
        conv_x[0],
        conv_x_bias,
        norm_gain,
        rms_gain,
        conv_bc.reshape(taps, lay.off),
        conv_bc_bias.reshape(1, lay.off),
        step_bias,
        decay_log,
        skip_gain,
    )
    args = dict(vars(first), tokens=tokens, cotangent=cotangent, resid=first.full)
    args.update({f"own{k}": weight for k, weight in enumerate(own)})
    one = bwd_layer(lay, 1, args, False)
    args.update(up=one.full, prev_x=one.rest_x, prev_s=one.own_s, done_o=one.sum_o, done_g=one.sum_g)
    args.update(done_x=one.sum_x, small=one.psm, hid0=first.hid, hid1=one.hid, gt1=one.gt)
    zero = bwd_layer(lay, 0, args, True)
    at_zero = section == 0

    def both_pieces(ours0, ours1, theirs):
        ours = jnp.where(at_zero, ours0, ours1)
        return jnp.stack([jnp.where(at_zero, ours, theirs), jnp.where(at_zero, theirs, ours)])[None]

    hid = both_pieces(first.hid, one.hid, zero.got_hid)
    gt = both_pieces(zero.gt, one.gt, zero.got_gt)
    g_gate, g_x, g_out, g_sm = (
        a.astype(F32)[None] for a in (zero.fin_g, zero.fin_x, zero.fin_o, zero.fin_s)
    )
    total = zero.total
    lane = lay.off
    rms_all = total[16:].reshape(lay.parts, 8, width)[:, 0, : lay.share].reshape(1, model)
    conv_small = total[7].reshape(-1, LANES)[:5, : lay.off]

    def head_row(k):
        return total[6, k * LANES + lane : k * LANES + lane + heads][None]

    return (
        hid,
        gt,
        rms_all,
        g_gate,
        g_x,
        g_sm[:, :, : lay.off].reshape(1, model, 2, local_state),
        g_sm[:, :, lane : lane + heads],
        total[None, 0:4],
        total[4:5],
        conv_small[:4].reshape(1, 4, 2, local_state),
        conv_small[4].reshape(1, 2, local_state),
        head_row(1),
        head_row(2),
        head_row(0),
        total[5:6],
        g_out,
    )


def solution(mesh):
    placed = (
        P(None, "seq", None),
        P(None, "seq", None),
        P("section", None),
        P("section", None, "head"),
        P("section", None, "head"),
        P("section", None, None, "head"),
        P("section", None, "head"),
        P("section", None, "head"),
        P("section", "head"),
        P("section", None, None, "head"),
        P("section", None, "head"),
        P("section", "head"),
        P("section", "head"),
        P("section", "head"),
        P("section", "head"),
        P("section", "head", None),
    )
    back = (P("section", None, "seq", "head"),) * 2 + placed[2:]
    shape = tuple(mesh.shape[name] for name in ("section", "seq", "head"))
    return jax.shard_map(
        functools.partial(on_device, shape),
        mesh=mesh,
        in_specs=placed,
        out_specs=back,
        check_vma=False,
    )
```

```python
import functools

import jax
import jax.numpy as jnp
from jax import lax
from jax.experimental import pallas as pl
from jax.experimental.pallas import tpu as pltpu
from jax.sharding import PartitionSpec as P

F32, BF = jnp.float32, jnp.bfloat16
MESH = pl.DeviceIdType.MESH
EPS = 1e-05
Q = 128
LANES = 128
GROUP = 16
NN, NT, TN = ((1,), (0,)), ((1,), (1,)), ((0,), (0,))
VM, HB = pltpu.VMEM, pl.ANY


def dot(a, b, dims=NN):
    return lax.dot_general(a, b, (dims, ((), ())), preferred_element_type=F32)


def iota(shape, dim):
    return lax.broadcasted_iota(jnp.int32, shape, dim)


def split3(v):
    hi = v.astype(BF)
    rest = v - hi.astype(F32)
    mid = rest.astype(BF)
    return hi, mid, (rest - mid.astype(F32)).astype(BF)


def sum3(matrix, v, dims=NN):
    hi, mid, low = split3(v)
    return dot(matrix, hi, dims) + dot(matrix, mid, dims) + dot(matrix, low, dims)


def dot2(a, v, dims=NN):
    hi = v.astype(BF)
    return dot(a, hi, dims) + dot(a, (v - hi.astype(F32)).astype(BF), dims)


def silu_grad(v):
    sg = jax.nn.sigmoid(v)
    return sg * (1.0 + v * (1.0 - sg))


def fold(v):
    total = v[:, :LANES]
    for k in range(1, v.shape[1] // LANES):
        total = total + v[:, k * LANES : (k + 1) * LANES]
    return total


def to_row(v):
    return jnp.sum(jnp.transpose(fold(v)), axis=0, keepdims=True)


def to_col(row):
    return jnp.transpose(jnp.broadcast_to(row, (Q, Q)))[:, :1]


class Lay:
    def __init__(self, mesh_shape, rows, width, model, heads, local_state):
        self.sections, self.seqs, self.parts = mesh_shape
        self.rows, self.width, self.model, self.heads = rows, width, model, heads
        self.nb = rows // Q
        self.share = model // self.parts
        self.ls = local_state
        self.off = 2 * local_state
        self.hp = width // heads
        self.inner = width * self.parts
        self.state = local_state * self.parts

    def place(self):
        self.c = lax.axis_index("section")
        self.z = lax.axis_index("seq")
        self.q = lax.axis_index("head")

    def heads_peers(self):
        return [
            (k, (self.c, self.z, lax.rem(self.q + k, self.parts)))
            for k in range(1, self.parts)
        ]

    def seq_peers(self):
        return [(k, (self.c, lax.rem(self.z + k, self.seqs), self.q)) for k in range(1, self.seqs)]

    def sibling(self):
        return (1 - self.c, self.z, self.q)

    def next_run(self):
        last = self.z == self.seqs - 1
        return (
            jnp.where(last, 1 - self.c, self.c),
            jnp.where(last, 0, self.z + 1),
            self.q,
        )

    def prev_run(self):
        first = self.z == 0
        return (
            jnp.where(first, 1 - self.c, self.c),
            jnp.where(first, self.seqs - 1, self.z - 1),
            self.q,
        )


def meet(targets):
    barrier = pltpu.get_barrier_semaphore()
    for target in targets:
        pl.semaphore_signal(barrier, inc=1, device_id=target, device_id_type=MESH)
    pl.semaphore_wait(barrier, len(targets))


def column_and_heads(lay):
    column = [
        ((lay.c + s) % 2, lax.rem(lay.z + k, lay.seqs), lay.q)
        for s in range(2)
        for k in range(lay.seqs)
        if s or k
    ]
    return column + [target for _, target in lay.heads_peers()]


def remote(src, dst, send, recv, target):
    return pltpu.make_async_remote_copy(
        src_ref=src,
        dst_ref=dst,
        send_sem=send,
        recv_sem=recv,
        device_id=target,
        device_id_type=MESH,
    )


class SeqSum:
    def __init__(self, lay, pieces, sems):
        self.pieces, self.sems = pieces, sems
        z, n = lay.z, lay.seqs
        self.left = z < n // 2
        depth = jnp.where(self.left, z, n - 1 - z)
        self.outer = depth > 0
        self.middle = depth == n // 2 - 1
        self.inside = (lay.c, jnp.where(self.left, z + 1, z - 1), lay.q)
        self.outside = (lay.c, jnp.clip(jnp.where(self.left, z - 1, z + 1), 0, n - 1), lay.q)

    def pass_on(self, k, src):
        own, inner, result, rows = self.pieces[k]
        ssem, asem, tsem, _ = self.sems

        def to_middle():
            remote(src, result.at[rows], ssem.at[k], tsem.at[k], self.inside).start()

        def to_next():
            remote(src, inner.at[rows], ssem.at[k], asem.at[k], self.inside).start()

        pl.when(self.middle)(to_middle)
        pl.when(jnp.logical_not(self.middle))(to_next)

    def inward(self, k):
        own, inner, result, rows = self.pieces[k]
        ssem, asem, tsem, _ = self.sems

        @pl.when(self.outer)
        def _():
            remote(own.at[rows], inner.at[rows], ssem.at[k], asem.at[k], self.inside).wait_recv()
            inner[rows, :] = inner[rows, :] + own[rows, :]
            self.pass_on(k, inner.at[rows])

    def push(self, k):
        @pl.when(jnp.logical_not(self.outer))
        def _():
            own, _, _, rows = self.pieces[k]
            self.pass_on(k, own.at[rows])

    def outward(self, k):
        own, inner, result, rows = self.pieces[k]
        ssem, _, tsem, osem = self.sems

        def arrived():
            remote(own.at[rows], result.at[rows], ssem.at[k], tsem.at[k], self.inside).wait_recv()

        @pl.when(self.outer)
        def _():
            arrived()

            @pl.when(self.middle)
            def _():
                result[rows, :] = result[rows, :] + inner[rows, :]

            remote(result.at[rows], result.at[rows], osem.at[k], tsem.at[k], self.outside).start()

    def ending(self, k):
        own, inner, result, rows = self.pieces[k]
        ssem, _, tsem, _ = self.sems

        @pl.when(jnp.logical_not(self.outer))
        def _():
            remote(own.at[rows], result.at[rows], ssem.at[k], tsem.at[k], self.inside).wait_recv()

            @pl.when(self.middle)
            def _():
                result[rows, :] = result[rows, :] + own[rows, :]

    def finish(self):
        for k, (own, inner, result, rows) in enumerate(self.pieces):
            ssem, _, tsem, osem = self.sems
            remote(own.at[rows], result.at[rows], ssem.at[k], tsem.at[k], self.inside).wait_send()

            @pl.when(self.outer)
            def _():
                remote(
                    result.at[rows], result.at[rows], osem.at[k], tsem.at[k], self.outside
                ).wait_send()


class Pump:
    def __init__(self, seq_sum, done=None):
        self.sum, self.done = seq_sum, done
        self.ready = self.pushed = self.taken = self.given = self.ended = 0

    def end(self, k):
        self.sum.ending(k)
        if self.done is not None:
            self.done(k)

    def plan(self):
        steps = []

        def feed():
            while self.pushed < min(self.ready, self.taken + 2):
                steps.append((self.sum.push, self.pushed))
                self.pushed += 1

        feed()
        if self.taken < self.pushed:
            steps.append((self.sum.inward, self.taken))
            self.taken += 1
            feed()
        if self.given < self.taken - 1:
            steps.append((self.sum.outward, self.given))
            self.given += 1
        if self.ended < self.given - 2:
            steps.append((self.end, self.ended))
            self.ended += 1
        return steps

    def feed(self):
        while self.pushed < min(self.ready, self.taken + 2):
            self.sum.push(self.pushed)
            self.pushed += 1

    def tick(self):
        self.later()()

    def later(self):
        steps = self.plan()

        def act():
            for kind, piece in steps:
                kind(piece)

        return act

    def finish(self):
        while self.taken < self.ready:
            self.tick()
        while self.given < self.taken:
            self.sum.outward(self.given)
            self.given += 1
        while self.ended < self.given:
            self.end(self.ended)
            self.ended += 1
        self.sum.finish()


class Scan:
    def __init__(self, lay, forward, expm, v):
        self.lay, self.expm, self.v = lay, expm, v
        self.steps = max(lay.seqs - 1, 0).bit_length()
        assert 1 << self.steps == lay.seqs
        self.forward = forward
        self.u = lay.z if forward else lay.seqs - 1 - lay.z
        self.first = lay.c == (0 if forward else 1)

    def device(self, u):
        u = jnp.clip(u, 0, self.lay.seqs - 1)
        return (self.lay.c, u if self.forward else self.lay.seqs - 1 - u, self.lay.q)

    def row(self, chosen):
        total = jnp.ones((8, LANES), F32)
        for u in range(self.lay.seqs):
            z = u if self.forward else self.lay.seqs - 1 - u
            total = jnp.where(chosen(u), total * self.v.table[z], total)
        return expand(self.lay, self.expm[...], total)[:1, :]

    def copies(self, s, ahead, only=None):
        v = self.v
        src, dst = (v.main_s, v.main_r) if ahead else (v.back_s, v.back_r)
        send, recv = (v.scan_sem.at[0 if ahead else 2], v.scan_sem.at[1 if ahead else 3])
        out = []
        for t in range(1 << s) if only is None else (only,):
            u = self.u + 1 + t if ahead else self.u - 1 - t
            out.append(
                remote(src, dst.at[s], send.at[(1 << s) - 1 + t], recv.at[s], self.device(u))
            )
        return out

    def gives(self, s, ahead):
        place = self.u if ahead else self.lay.seqs - 1 - self.u
        return lax.rem(place, 2 << s) == (1 << s) - 1

    def takes(self, s, ahead):
        place = self.u if ahead else self.lay.seqs - 1 - self.u
        return lax.rem(place // (1 << s), 2) == 1

    def give(self, s):
        v = self.v

        @pl.when(self.gives(s, True))
        def _():
            own_decay = self.row(lambda u: u == self.u)
            v.main_s[...] = (v.enter[...] * own_decay + v.own_state[...]).astype(BF)
            for copy in self.copies(s, True):
                copy.start()

        @pl.when(self.first & self.gives(s, False))
        def _():
            v.back_s[...] = (v.rest[...] + v.own_state[...] * self.row(lambda u: u > self.u)).astype(BF)
            for copy in self.copies(s, False):
                copy.start()

    def start(self):
        v = self.v
        v.enter[...] = jnp.zeros(v.enter.shape, F32)
        v.rest[...] = jnp.zeros(v.rest.shape, F32)
        if self.steps:
            self.give(0)

    def advance(self, s):
        v = self.v

        @pl.when(self.takes(s, True))
        def _():
            self.copies(s, True, 0)[0].wait_recv()
            begin = (self.u // (1 << s)) * (1 << s)
            between = self.row(lambda u: (u >= begin) & (u < self.u))
            v.enter[...] += between * v.main_r[s].astype(F32)

        @pl.when(self.first & self.takes(s, False))
        def _():
            self.copies(s, False, 0)[0].wait_recv()
            v.rest[...] += v.back_r[s].astype(F32)

        if s + 1 < self.steps:
            self.give(s + 1)

    def hand_over(self):
        v = self.v
        self.total = remote(
            v.total_s, v.total_r, v.total_sem.at[0], v.total_sem.at[1], self.lay.sibling()
        )

        @pl.when(self.first)
        def _():
            own_decay = self.row(lambda u: u == self.u)
            after = self.row(lambda u: u > self.u)
            through = (v.enter[...] * own_decay + v.own_state[...]) * after
            v.total_s[...] = (through + v.rest[...]).astype(BF)
            self.total.start()

    def result(self):
        v = self.v

        @pl.when(jnp.logical_not(self.first))
        def _():
            self.total.wait_recv()
            v.enter[...] += self.row(lambda u: u < self.u) * v.total_r[...].astype(F32)

        pl.when(self.first)(self.total.wait_send)
        for s in range(self.steps):
            for ahead in (True, False):
                gives = self.gives(s, ahead)

                @pl.when(gives if ahead else self.first & gives)
                def _():
                    for copy in self.copies(s, ahead):
                        copy.wait_send()


def scan_scratch(lay, kinds):
    n, w, steps = lay.state, lay.width, max(lay.seqs - 1, 1).bit_length()
    dma = pltpu.SemaphoreType.DMA
    out = dict(
        table=VM((lay.seqs, 8, LANES), F32),
        own_state=VM((n, w), F32),
        enter=VM((n, w), F32),
        rest=VM((n, w), F32),
        main_s=VM((n, w), BF),
        back_s=VM((n, w), BF),
        total_s=VM((n, w), BF),
        table_sem=dma((2, max(lay.seqs - 1, 1))),
    )
    for kind in kinds:
        out[kind + "main_r"] = VM((steps, n, w), BF)
        out[kind + "back_r"] = VM((steps, n, w), BF)
        out[kind + "total_r"] = VM((n, w), BF)
        out[kind + "scan_sem"] = dma((4, max(lay.seqs - 1, 1)))
        out[kind + "total_sem"] = dma((2,))
    return out


def scan_refs(v, kind):
    shared = ["table", "own_state", "enter", "rest", "main_s", "back_s", "total_s"]
    own = ["main_r", "back_r", "total_r", "scan_sem", "total_sem"]
    refs = [getattr(v, name) for name in shared] + [getattr(v, kind + name) for name in own]
    return Names(shared + own, refs)


def share_table(lay, v):
    copies = [
        remote(v.table.at[lay.z], v.table.at[lay.z], v.table_sem.at[0, k - 1], v.table_sem.at[1, k - 1], to)
        for k, to in lay.seq_peers()
    ]
    for copy in copies:
        copy.start()
    return copies


class Names:
    def __init__(self, names, refs):
        assert len(names) == len(refs), (len(names), len(refs))
        self.__dict__.update(zip(names, refs))


def pieces_of(own, inner, result, count):
    size = own.shape[0] // count
    return [(own, inner, result, pl.ds(k * size, size)) for k in range(count)]


def expander(lay):
    lane = iota((LANES, lay.width), 0) - lay.off
    head = iota((LANES, lay.width), 1) // lay.hp
    hit = (lane >= 0) & (lane < 3 * GROUP) & (lax.rem(lane + GROUP * 8, GROUP) == head)
    return jnp.where(hit, 1.0, 0.0).astype(BF)


def expand(lay, exp_matrix, v):
    hi, mid, low = split3(v)
    lane = iota(v.shape, 1) - lay.off
    packed = jnp.where(
        lane < 0,
        0.0,
        jnp.where(
            lane < GROUP,
            hi.astype(F32),
            jnp.where(
                lane < 2 * GROUP, mid.astype(F32), jnp.where(lane < 3 * GROUP, low.astype(F32), 0.0)
            ),
        ),
    )
    return dot(packed.astype(BF), exp_matrix)


def head_sum(exp_matrix, v):
    hi, mid, low = split3(v)
    return dot(hi, exp_matrix, NT) + dot(mid, exp_matrix, NT) + dot(low, exp_matrix, NT)


def selectors(lay):
    shape = (lay.parts * LANES, 2 * lay.state)
    row, col = iota(shape, 0), iota(shape, 1)
    piece, lane = row // LANES, lax.rem(row, LANES)
    kind, n = col // lay.state, lax.rem(col, lay.state)
    want = kind * lay.ls + lax.rem(n, lay.ls)
    same = piece == n // lay.ls
    top = jnp.where(same & (lane == want), 1.0, 0.0).astype(BF)
    bottom = jnp.where(same & (lane == want + LANES // 2), 1.0, 0.0).astype(BF)
    return top, bottom


def tri(kind):
    row, col = iota((Q, Q), 0), iota((Q, Q), 1)
    hit = {"lower": row >= col, "upper": row <= col, "strict": row > col}[kind]
    return jnp.where(hit, 1.0, 0.0).astype(BF)


def block(i, size=Q, base=0):
    return pl.ds(pl.multiple_of(i * size + base, 8), size)


def conv_cat(ref, i):
    return ref[pl.ds(pl.multiple_of(i * Q + 8, 8), Q + 8), :]


def conv_pre(cat, kernel, bias):
    total = bias
    for k in range(4):
        total = total + kernel[k : k + 1, :] * cat[5 + k : 5 + k + Q, :]
    return total


def softplus(v):
    return jnp.maximum(v, 0.0) + jnp.log1p(jnp.exp(-jnp.abs(v)))


def params(lay, pk_ref, layer):
    pk = pk_ref[layer]
    w = lay.width
    out = dict(
        conv_x=pk[0:4, :],
        bias_x=pk[4:5, :],
        gain_out=pk[5:6, :],
        skip=pk[6:7, :],
        gain=jnp.concatenate([pk[7:8, :], pk[8:9, :]], axis=1)
        if lay.model == 2 * w
        else None,
        conv_sm=jnp.concatenate([pk[9:10, k * LANES : (k + 1) * LANES] for k in range(4)], axis=0),
        bias_sm=pk[9:10, 4 * LANES : 5 * LANES],
        step_bias=pk[10:11, 0:LANES],
        rate=pk[10:11, LANES : 2 * LANES],
    )
    return out


def decay_tile(cum, cum_t, lane, causal):
    diff = cum[:, lane : lane + 1] - cum_t[lane : lane + 1, :]
    return jnp.exp(jnp.where(causal, diff, -1e30))


def halves(v):
    lane = iota(v.shape, 1)
    left = lane < LANES // 2
    zero = jnp.zeros_like(v)
    return jnp.where(left, v, zero), jnp.where(left, zero, v)


class HeadSum:
    def __init__(self, lay, part, got, send, recv, full=None, gsend=None, grecv=None):
        assert lay.parts == 4
        self.lay, self.part, self.got, self.send, self.recv = lay, part, got, send, recv
        self.full, self.gsend, self.grecv = full, gsend, grecv
        q = lay.q
        self.index = (q, q + 1 - 2 * lax.rem(q, 2), lax.rem(q + 2, 4), 3 - q)
        self.out = []

    def target(self, mask):
        return (self.lay.c, self.lay.z, self.index[mask])

    def cols(self, mask):
        return pl.ds(pl.multiple_of(self.index[mask] * self.lay.share, LANES), self.lay.share)

    def near(self, i):
        return 1 if i % 2 == 0 else 2

    def rows(self, i):
        return pl.ds(i * Q, Q)

    def copy(self, kind, i):
        near, rows = self.near(i), self.rows(i)
        src = (near, 3, 3 - near)[kind]
        return remote(
            self.part.at[src, rows],
            self.got.at[kind, rows],
            self.send.at[kind, i],
            self.recv.at[kind, i],
            self.target(near if kind < 2 else 3 - near),
        )

    def first(self, i):
        self.steps = getattr(self, "steps", {})
        self.steps[i] = [self.copy(kind, i) for kind in range(2)]
        for copy in self.steps[i]:
            copy.start()

    def second(self, i):
        for copy in self.steps[i]:
            copy.wait()
        far, rows = 3 - self.near(i), self.rows(i)
        both = self.part[far, rows, :].astype(F32) + self.got[1, rows, :].astype(F32)
        self.part[far, rows, :] = both.astype(BF)
        copy = self.copy(2, i)
        copy.start()
        self.steps[i] = copy

    def total(self, i):
        self.steps[i].wait()
        rows = self.rows(i)
        value = self.part[0, rows, :].astype(F32) + self.got[0, rows, :].astype(F32)
        return value + self.got[2, rows, :].astype(F32)

    def spread(self, i, mask, kind, to):
        block = self.full.at[self.rows(i), self.cols(mask)]
        copy = remote(block, block, self.gsend.at[kind, i], self.grecv.at[kind, i], self.target(to))
        copy.start()
        return copy

    def give(self, i):
        self.steps[i] = [self.spread(i, 0, 0, 1), self.spread(i, 0, 1, 2)]

    def relay(self, i):
        near = self.near(i)
        self.steps[i][2 - near].wait()
        self.steps[i] = [self.steps[i][near - 1], self.spread(i, 3 - near, 2, near)]

    def finish(self):
        for copies in self.steps.values():
            for copy in copies:
                copy.wait()


class Load:
    def __init__(self, own, other, dst, sem, mine):
        self.mine = mine
        self.copies = [pltpu.make_async_copy(src, dst, sem) for src in (own, other)]

    def start(self):
        pl.when(self.mine)(self.copies[0].start)
        pl.when(jnp.logical_not(self.mine))(self.copies[1].start)

    def wait(self):
        self.copies[0].wait()


def forward(lay, v, p, resid, weights, ready, project, meanwhile=None):
    c, z, q = lay.c, lay.z, lay.q
    nb, w, n = lay.nb, lay.width, lay.state
    wsm, wx, wg = weights
    expm, normed, sm, xp, cums, bc = v.expm, v.normed, v.sm, v.xp, v.cums, v.bc
    scan = Scan(lay, True, expm, scan_refs(v, "f_"))
    counter = iter(range(16))

    def send(src, dst, target):
        at = next(counter)
        copy = remote(src, dst, v.fsend.at[at], v.frecv.at[at], target)
        copy.start()
        return copy

    @pl.loop(0, nb)
    def _(i):
        x = resid[block(i), :].astype(F32)
        scale = lax.rsqrt(jnp.mean(x * x, axis=1, keepdims=True) + EPS)
        normed[block(i), :] = (x * scale * p["gain"]).astype(BF)

    ready(0)
    sm[16:, :] = dot(normed[...], wsm[...])
    v.shs[...] = sm[lay.rows :, :].astype(BF)
    after = lay.next_run()
    halo_s = send(v.shs, v.shr, after)
    tables = run_decays(lay, v, p)
    ready(1)
    step_n = 256

    @pl.loop(0, w // step_n)
    def _(j):
        cols = pl.ds(pl.multiple_of(j * step_n, step_n), step_n)
        xp[16:, cols] = dot(normed[...], wx[:, cols])

    v.xhs[...] = xp[lay.rows :, :].astype(BF)
    halo_x = send(v.xhs, v.xhr, after)
    halo_s.wait()
    inside = jnp.where((c == 0) & (z == 0), 0.0, 1.0)
    sm[:16, :] = v.shr[...].astype(F32) * inside

    half = lay.rows // 2
    conv_rows = []
    for i in range(nb):
        pre = conv_pre(conv_cat(sm, i), p["conv_sm"], p["bias_sm"])
        conv_rows.append(pre * jax.nn.sigmoid(pre))
    top = jnp.concatenate(conv_rows[: nb // 2], axis=0)
    bottom = jnp.concatenate(conv_rows[nb // 2 :], axis=0)
    lane = iota(top.shape, 1)
    v.bcg[q] = jnp.where(lane < LANES // 2, top, pltpu.roll(bottom, LANES // 2, 1)).astype(BF)
    sends = [send(v.bcg.at[q], v.bcg.at[q], target) for _, target in lay.heads_peers()]
    halo_x.wait()
    xp[:16, :] = v.xhr[...].astype(F32) * inside

    @pl.loop(0, nb)
    def _(i):
        pre = conv_pre(conv_cat(xp, i), p["conv_x"], p["bias_x"])
        v.xc[block(i), :] = pre * jax.nn.sigmoid(pre)

    for copy in sends:
        copy.wait()
    pieces = jnp.concatenate([v.bcg[k] for k in range(lay.parts)], axis=1)
    sel_top, sel_bottom = selectors(lay)
    bc[:half, :] = dot(pieces, sel_top).astype(BF)
    bc[half:, :] = dot(pieces, sel_bottom).astype(BF)

    v.local[0] = jnp.zeros((n, w), F32)
    v.dpre[...] = jnp.zeros(v.dpre.shape, F32)
    state = None
    total = jnp.zeros((1, LANES), F32)
    for i in range(nb):
        rows = pl.ds(i * Q, Q)
        cum = cums[1, rows, :]
        last = cum[Q - 1 :, :]
        weight = jnp.exp(last - cum) * cums[0, rows, :]
        xw = (v.xc[rows, :] * expand(lay, expm[...], weight)).astype(BF)
        update = dot(bc[rows, :n], xw, TN)
        dec = expand(lay, expm[...], jnp.broadcast_to(jnp.exp(last), (8, LANES)))[:1, :]
        state = update if i == 0 else state * dec + update
        total = total + last
        if i < nb - 1:
            v.local[i + 1] = state
            v.dpre[8 * (i + 1) : 8 * (i + 2), :] = jnp.broadcast_to(total, (8, LANES))
    v.own_state[...] = state
    for copy in tables:
        copy.wait()
    scan.start()
    ready(2)

    @pl.loop(0, w // step_n)
    def _(j):
        cols = pl.ds(pl.multiple_of(j * step_n, step_n), step_n)
        v.gate[:, cols] = dot(normed[...], wg[:, cols])

    @pl.loop(0, nb)
    def _(i):
        if scan.steps > 1:
            pl.when(i == nb - 1)(functools.partial(scan.advance, 0))
        causal = iota((Q, Q), 0) >= iota((Q, Q), 1)
        cum = cums[1, block(i), :]
        cum_t = jnp.transpose(cum)
        scores = dot(bc[block(i), n:], bc[block(i), :n], NT)
        stepped = (v.xc[block(i), :] * expand(lay, expm[...], cums[0, block(i), :])).astype(BF)
        for pair in range(lay.heads // 2):
            cols = slice(pair * LANES, (pair + 1) * LANES)
            mixes = [
                (scores * decay_tile(cum, cum_t, lay.off + 2 * pair + e, causal)).astype(BF)
                for e in range(2)
            ]
            xl, xr = halves(stepped[:, cols])
            v.ysd[block(i), cols] = dot(
                jnp.concatenate(mixes, axis=1), jnp.concatenate([xl, xr], axis=0)
            )

    @pl.loop(0, nb)
    def _(i):
        v.nt[:, pl.ds(pl.multiple_of(i * Q, Q), Q)] = jnp.transpose(normed[block(i), :])

    if meanwhile is not None:
        meanwhile()
    for step in range(1 if scan.steps > 1 else 0, scan.steps):
        scan.advance(step)
    scan.hand_over()
    scan.result()
    start = v.enter[...]

    @pl.loop(0, nb)
    def _(i):
        cum = cums[1, block(i), :]
        dec = jnp.exp(v.dpre[pl.ds(pl.multiple_of(8 * i, 8), 8), :])
        full = v.local[i] + expand(lay, expm[...], dec)[:1, :] * start
        v.sin[i] = full
        carried = dot2(bc[block(i), n:], full) * expand(lay, expm[...], jnp.exp(cum))
        y = v.ysd[block(i), :] + carried
        v.ysd[block(i), :] = y
        g = v.gate[block(i), :]
        gated = (y + p["skip"] * v.xc[block(i), :]) * (g * jax.nn.sigmoid(g))
        row = to_row(gated * gated)
        v.sqb[q, pl.ds(pl.multiple_of(8 * i, 8), 8), :] = jnp.broadcast_to(row, (8, Q))
        v.go[block(i), :] = (gated * p["gain_out"]).astype(BF)

    squares = [send(v.sqb.at[q], v.sqb.at[q], target) for _, target in lay.heads_peers()]
    if meanwhile is None:
        ready(3)
    project()
    for copy in squares:
        copy.wait()
    total_sq = v.sqb[0]
    for k in range(1, lay.parts):
        total_sq = total_sq + v.sqb[k]
    v.sqt[...] = total_sq


def run_decays(lay, v, p):
    lower = tri("lower")
    lasts = []
    for i in range(lay.nb):
        rows = pl.ds(i * Q, Q)
        step = softplus(v.sm[16 + i * Q : 16 + (i + 1) * Q, :] + p["step_bias"])
        v.cums[0, rows, :] = step
        cum = sum3(lower, step * p["rate"])
        v.cums[1, rows, :] = cum
        lasts.append(cum[Q - 1 :, :])
    v.table[lay.z] = jnp.broadcast_to(jnp.exp(sum(lasts)), (8, LANES))
    return share_table(lay, v)


def kept_shapes(lay):
    r, w, m, n = lay.rows, lay.width, lay.model, lay.state
    return dict(
        nt=((m, r), BF),
        gate=((r, w), F32),
        xp=((r + 16, w), F32),
        sm=((r + 16, LANES), F32),
        ysd=((r, w), F32),
        sin=((lay.nb, n, w), F32),
        bc=((r, 2 * n), BF),
        sqt=((8 * lay.nb, Q), F32),
    )


def fwd_scratch(lay):
    r, w = lay.rows, lay.width
    dma = pltpu.SemaphoreType.DMA
    n_sem = 2 + 2 * (lay.parts - 1)
    return dict(
        xhs=VM((16, w), BF),
        xhr=VM((16, w), BF),
        shs=VM((16, LANES), BF),
        shr=VM((16, LANES), BF),
        bcg=VM((lay.parts, r // 2, LANES), BF),
        dpre=VM((8 * lay.nb, LANES), F32),
        sqb=VM((lay.parts, 8 * lay.nb, Q), F32),
        fsend=dma((n_sem,)),
        frecv=dma((n_sem,)),
    )


START_SMALL = ["conv_x", "bias_x", "gain_out", "rms", "conv_sm", "bias_sm"]
START_HEADS = ["step_bias", "decay", "skip"]


def start_ins():
    return ["tokens"] + [f"own{k}" for k in range(4)] + START_SMALL + START_HEADS


def start_outs(lay):
    r, w, m = lay.rows, lay.width, lay.model
    sds = jax.ShapeDtypeStruct
    out = {name: sds(*spec) for name, spec in kept_shapes(lay).items()}
    out.update(
        pk=sds((2, 16, w), F32),
        hid=sds((r, lay.share), F32),
        full=sds((r, m), BF),
        other0=sds((m, w), BF),
        other1=sds((m, w), BF),
        other2=sds((m, LANES), BF),
        other3=sds((w, m), BF),
    )
    return out


def start_scratch(lay):
    r, w, m, n = lay.rows, lay.width, lay.model, lay.state
    dma = pltpu.SemaphoreType.DMA
    peers = lay.parts - 1
    out = dict(
        resid=VM((r, m), BF),
        wg=VM((2, m, w), BF),
        wx=VM((2, m, w), BF),
        wsm=VM((2, m, LANES), BF),
        wo=VM((2, w, m), BF),
        expm=VM((LANES, w), BF),
        normed=VM((r, m), BF),
        xc=VM((r, w), F32),
        cums=VM((2, r, LANES), F32),
        go=VM((r, w), BF),
        local=VM((lay.nb, n, w), F32),
        tmp=VM((16, LANES), F32),
        part=VM((peers, r, lay.share), BF),
        own_part=VM((r, lay.share), F32),
        got=VM((peers, r, lay.share), BF),
        wsem=dma((5,)),
        psem=dma((9,)),
        vsem=dma((5,)),
        rs_send=dma((peers, lay.nb)),
        rs_recv=dma((peers, lay.nb)),
        ag_send=dma((peers, lay.nb)),
        ag_recv=dma((peers, lay.nb)),
    )
    out.update(fwd_scratch(lay))
    out.update(scan_scratch(lay, ["f_"]))
    return out


def pack(lay, v):
    c, w, heads, off = lay.c, lay.width, lay.heads, lay.off
    f = lambda ref: ref[...].astype(F32)
    v.tmp[...] = jnp.zeros(v.tmp.shape, F32)
    v.tmp[0:4, :off] = f(v.conv_sm)
    v.tmp[4:5, :off] = f(v.bias_sm)
    v.tmp[8:9, :heads] = v.step_bias[...]
    v.tmp[9:10, :heads] = -jnp.exp(v.decay[...])
    v.tmp[10:11, :heads] = v.skip[...]
    rows = v.tmp[8:16, :]
    groups = rows * 0.0
    for k in range(3):
        groups = groups + pltpu.roll(rows, off + k * GROUP, 1)
    v.pk[c] = jnp.zeros((16, w), F32)
    v.pk[c, 0:4, :] = f(v.conv_x)
    v.pk[c, 4:5, :] = f(v.bias_x)
    v.pk[c, 5:6, :] = f(v.gain_out)
    v.pk[c, 6:7, :] = expand(lay, v.expm[...], groups)[2:3, :]
    rms = f(v.rms)
    for k in range(lay.model // w):
        v.pk[c, 7 + k : 8 + k, :] = rms[:, k * w : (k + 1) * w]
    for k in range(5):
        v.pk[c, 9:10, k * LANES : (k + 1) * LANES] = v.tmp[k : k + 1, :]
    for k in range(2):
        v.pk[c, 10:11, k * LANES : (k + 1) * LANES] = groups[k : k + 1, :]


def start_kernel(lay, *refs):
    v = Names(start_ins() + list(start_outs(lay)) + list(start_scratch(lay)), refs)
    lay.place()
    c, q, nb = lay.c, lay.q, lay.nb
    both, own_w = (v.wg, v.wx, v.wsm, v.wo), (v.own0, v.own1, v.own2, v.own3)
    kept_w = (v.other0, v.other1, v.other2, v.other3)
    order = (2, 1, 0, 3)
    loads = [pltpu.make_async_copy(v.tokens.at[c], v.resid, v.wsem.at[4])]
    loads += [
        pltpu.make_async_copy(own_w[k], both[k].at[c], v.wsem.at[at]) for at, k in enumerate(order)
    ]
    for load in loads:
        load.start()
    v.expm[...] = expander(lay)
    pack(lay, v)
    meet(column_and_heads(lay))
    swaps = [remote(v.pk.at[c], v.pk.at[c], v.psem.at[4], v.vsem.at[4], lay.sibling())]
    swaps += [
        remote(own_w[k], both[k].at[c], v.psem.at[at], v.vsem.at[at], lay.sibling())
        for at, k in enumerate(order)
    ]
    for copy in swaps:
        copy.start()
    keeps = [
        pltpu.make_async_copy(both[k].at[1 - c], kept_w[k], v.psem.at[5 + at])
        for at, k in enumerate(order)
    ]
    wg, wx, wsm, wo = (ref.at[0] for ref in both)
    swaps[0].wait()
    loads[0].wait()

    def ready(at):
        loads[1 + at].wait()
        swaps[1 + at].wait()
        keeps[at].start()

    peers = lay.heads_peers()
    chunks = [[] for _ in range(nb)]

    def project():
        for k, target in peers + [(0, None)]:
            owner = lax.rem(q + k, lay.parts)
            cols = pl.ds(pl.multiple_of(owner * lay.share, LANES), lay.share)
            product = dot(v.go[...], wo[:, cols])
            if k == 0:
                v.own_part[...] = product
                continue
            v.part[k - 1] = product.astype(BF)
            for i in range(nb):
                rows = pl.ds(i * Q, Q)
                copy = remote(
                    v.part.at[k - 1, rows],
                    v.got.at[k - 1, rows],
                    v.rs_send.at[k - 1, i],
                    v.rs_recv.at[k - 1, i],
                    target,
                )
                copy.start()
                chunks[i].append(copy)

    p = params(lay, v.pk, 0)
    forward(lay, v, p, v.resid, (wsm, wx, wg), ready, project)
    cols = pl.ds(pl.multiple_of(q * lay.share, LANES), lay.share)
    given = []
    for i in range(nb):
        rows = pl.ds(i * Q, Q)
        for copy in chunks[i]:
            copy.wait()
        total = v.own_part[rows, :]
        for k, _ in peers:
            total = total + v.got[k - 1, rows, :].astype(F32)
        row = v.sqt[8 * i : 8 * i + 1, :]
        value = v.resid[rows, cols].astype(F32) + to_col(lax.rsqrt(row / lay.inner + EPS)) * total
        v.hid[rows, :] = value
        v.full[rows, cols] = value.astype(BF)
        for k, target in peers:
            copy = remote(
                v.full.at[rows, cols],
                v.full.at[rows, cols],
                v.ag_send.at[k - 1, i],
                v.ag_recv.at[k - 1, i],
                target,
            )
            copy.start()
            given.append(copy)
    for copy in given + keeps:
        copy.wait()


def start_layer(lay, *args):
    outs, scratch = start_outs(lay), start_scratch(lay)
    vmem, hbm = pl.BlockSpec(memory_space=VM), pl.BlockSpec(memory_space=HB)
    got = pl.pallas_call(
        functools.partial(start_kernel, lay),
        out_shape=tuple(outs.values()),
        in_specs=[hbm] * 5 + [vmem] * (len(args) - 5),
        out_specs=tuple([vmem] * (len(outs) - 4) + [hbm] * 4),
        scratch_shapes=list(scratch.values()),
        compiler_params=pltpu.CompilerParams(
            collective_id=1, has_side_effects=True, vmem_limit_bytes=58 << 20
        ),
        name="mixer_start",
    )(*args)
    return Names(list(outs), got)


EARLIER = ["prev_x", "prev_s", "done_o", "done_g", "done_x", "small", "hid0", "hid1", "gt1"]
X_EARLY = 2


def staged(lay):
    r, w, m = lay.rows, lay.width, lay.model
    rest = m // 2 - m // 2 // N_X * X_EARLY
    out = dict(prev_x=((rest, w), BF), prev_s=((m // 2, LANES), BF), pk=((2, 16, w), F32))
    kept = kept_shapes(lay)
    for name in ("sm", "xp", "ysd", "gate", "sqt"):
        out[name] = kept[name]
    out["up"] = ((r, m), BF)
    for name in ("nt", "bc", "sin"):
        out[name] = kept[name]
    out.update(done_o=((w // 2, m), BF), done_g=((m // 2, w), BF))
    out.update(done_x=((m // 2 // N_X * X_EARLY, w), BF), small=((16, w), F32))
    return out


def back_ins(lay, more):
    weights = [f"own{k}" for k in range(4)] + [f"other{k}" for k in range(4)]
    if more:
        return ["from_" + name for name in staged(lay)] + ["tokens"] + weights + EARLIER[-3:]
    return ["cotangent", "resid"] + weights + ["pk"]


def back_outs(lay, late, gather, more):
    r, w, m = lay.rows, lay.width, lay.model
    sds = jax.ShapeDtypeStruct
    out = dict(gt=sds((r, lay.share), F32))
    if more:
        out["total"] = sds((16 + 8 * lay.parts, w), F32)
    else:
        out.update(
            sum_o=sds((w // 2, m), BF),
            sum_g=sds((m // 2, w), BF),
            sum_x=sds((m // 2 // N_X * X_EARLY, w), BF),
            rest_x=sds((m // 2 - m // 2 // N_X * X_EARLY, w), BF),
            own_s=sds((m // 2, LANES), BF),
            psm=sds((16, w), F32),
        )
    if gather:
        out["full"] = sds((r, m), BF)
    if late:
        out["hid"] = sds((r, lay.share), F32)
    if more:
        out.update(
            fin_o=sds((w, m), BF),
            fin_g=sds((m, w), BF),
            fin_x=sds((m, w), BF),
            fin_s=sds((m, LANES), BF),
            got_hid=sds((r, lay.share), F32),
            got_gt=sds((r, lay.share), F32),
        )
    return out


N_OUT = N_GATE = N_X = 4


def back_scratch(lay, late, gather, more):
    r, w, m, n, nb = lay.rows, lay.width, lay.model, lay.state, lay.nb
    dma = pltpu.SemaphoreType.DMA
    peers = lay.parts - 1
    n_sem = 2 * peers + 2 + 4 + peers
    n_seq = N_OUT + N_GATE + (2 * (N_X + 1) - X_EARLY if more else X_EARLY)
    out = dict(
        wg=VM((m, w), BF),
        wx=VM((m, w), BF),
        wsm=VM((m, LANES), BF),
        wo=VM((w, m), BF),
        expm=VM((LANES, w), BF),
        xc=VM((r, w), F32),
        dy=VM((r, w), F32),
        dx=VM((r, w), F32),
        cums=VM((2, r, LANES), F32),
        rcs=VM((r, LANES), F32),
        lowg=VM((r, w), BF),
        lowx=VM((r, w), BF),
        lowsm=VM((r, LANES), BF),
        no=VM((r, w), BF),
        rsb=VM((lay.parts, 8 * nb, Q), F32),
        lamloc=VM((nb, n, w), F32),
        dsuf=VM((8 * nb, LANES), F32),
        dbc=VM((r, 2 * n), F32),
        dbs=VM((lay.parts, r // 2, LANES), BF),
        dbr=VM((peers, r // 2, LANES), BF),
        xdp=VM((r + 16, w), F32),
        smdp=VM((r + 16, LANES), F32),
        hxs=VM((16, w), BF),
        hxr=VM((16, w), BF),
        hss=VM((16, LANES), BF),
        hsr=VM((16, LANES), BF),
        dsp=VM((r, LANES), F32),
        gr_g=VM((m // 2, w), BF),
        gr_x=VM((m // 2, w), BF),
        gs_o=VM((w // 2, m), BF),
        gr_o=VM((w // 2, m), BF),
        gr_s=VM((m // 2, LANES), BF),
        rdacc=VM((r, LANES), F32),
        acch=VM((8, LANES), F32),
        own_o=VM((w // 2, m), BF),
        own_g=VM((m // 2, w), BF),
        in_o=VM((w // 2, m), BF),
        in_g=VM((m // 2, w), BF),
        in_x=VM((m // 2, w), BF),
        dnp=VM((lay.parts, r, lay.share), BF),
        got=VM((peers, r, lay.share), BF),
        rd2=VM((8 * nb, Q), F32),
        got_rows=VM((peers, 8 * nb, Q), F32),
        gains=VM((8, m), F32),
        wsem=dma((5,)),
        ssem=dma((n_sem,)),
        rsem=dma((n_sem,)),
        rs_send=dma((peers, nb)),
        rs_recv=dma((peers, nb)),
        seq1=dma((n_seq,)),
        seq2=dma((n_seq,)),
        seq3=dma((n_seq,)),
        seq4=dma((n_seq,)),
    )
    if gather:
        out.update(ag_send=dma((peers, nb)), ag_recv=dma((peers, nb)))
    out["own_x"] = VM((m // 2, w), BF)
    if more:
        for kind in ("in_s", "in_ps", "own_s", "sum_s", "sum_ps"):
            out[kind] = VM((m // 2, LANES), BF)
        for kind in ("sum_x", "sum_g"):
            out[kind] = VM((m // 2, w), BF)
        for kind in ("in_px", "sum_px"):
            out[kind] = VM((m // 2 - m // 2 // N_X * X_EARLY, w), BF)
        column = 2 * lay.seqs
        out.update(
            sum_o=VM((w // 2, m), BF),
            psm=VM((16, w), F32),
            slots=VM((column, 16, w), F32),
            rest_rows=VM((lay.parts, 8, w), F32),
            fin_sem=dma((3, n_seq + 3)),
            pair_sem=dma((2, 2)),
            slot_sem=dma((2, column - 1)),
            part_sem=dma((2, peers)),
        )
        out["resid"] = VM((r, m), BF)
        out.update({name: VM(*spec) for name, spec in staged(lay).items()})
        out["stage_sem"] = dma((len(staged(lay)),))
    out.update(scan_scratch(lay, ["b_"] if more else ["f_", "b_"]))
    if late:
        out.update(
                late_got=VM((peers, r, lay.share), BF),
            late_send=dma((peers,)),
            late_recv=dma((peers,)),
            up=VM((r, m), BF),
        )
        out.update({name: VM(*spec) for name, spec in kept_shapes(lay).items()})
        out.update(fwd_scratch(lay))
    return out


def bwd_kernel(lay, layer, late, gather, more, *refs):
    outs, scratch = back_outs(lay, late, gather, more), back_scratch(lay, late, gather, more)
    v = Names(back_ins(lay, more) + list(outs) + list(scratch), refs)
    lay.place()
    c, z, q = lay.c, lay.z, lay.q
    nb, w, n, m = lay.nb, lay.width, lay.state, lay.model
    half = lay.rows // 2
    own_w, other_w = (v.own0, v.own1, v.own2, v.own3), (v.other0, v.other1, v.other2, v.other3)
    loads = [
        Load(own_w[k], other_w[k], (v.wg, v.wx, v.wsm, v.wo)[k], v.wsem.at[at], c == layer)
        for at, k in enumerate((3, 0, 1, 2) if more else (2, 1, 0, 3))
    ]
    stages = {}
    if more:
        for k, name in enumerate(staged(lay)):
            src, dst = getattr(v, "from_" + name), getattr(v, name)
            stages[name] = pltpu.make_async_copy(src, dst, v.stage_sem.at[k])
            stages[name].start()
        rows_in = pltpu.make_async_copy(v.tokens.at[c], v.resid, v.wsem.at[4])
    else:
        rows_in = pltpu.make_async_copy(v.cotangent.at[c], v.up, v.wsem.at[4])
    for load in loads + [rows_in]:
        load.start()
    meet(column_and_heads(lay))
    peers = lay.heads_peers()
    counter = iter(range(64))

    def send(src, dst, target):
        at = next(counter)
        copy = remote(src, dst, v.ssem.at[at], v.rsem.at[at], target)
        copy.start()
        return copy

    out_pieces = pieces_of(v.own_o, v.in_o, v.sum_o, N_OUT)
    gate_pieces = pieces_of(v.own_g, v.in_g, v.sum_g, N_GATE)
    finals = []

    def plan_settling(ref, fin, of, rows, skipped=0):
        size = ref.shape[0] if rows is None else rows.size
        offset = skipped + (0 if rows is None else rows.start)
        at = len(finals)
        into = fin.at[pl.ds(pl.multiple_of(c * (fin.shape[0] // 2) + offset, 16), size)]
        src = ref if rows is None else ref.at[rows]
        here = pltpu.make_async_copy(src, into, v.fin_sem.at[0, at])
        there = remote(src, into, v.fin_sem.at[1, at], v.fin_sem.at[2, at], lay.sibling())
        finals.append((of, here, there))

    def settle(at):
        of, here, there = finals[at]
        pl.when(c == of)(here.start)
        pl.when(c != of)(there.start)

    if more:
        kinds = [(pieces_of(v.prev_x, v.in_px, v.sum_px, N_X - X_EARLY), v.fin_x, 1)]
        kinds += [(pieces_of(v.prev_s, v.in_ps, v.sum_ps, 1), v.fin_s, 1)]
        kinds += [(out_pieces, v.fin_o, 0), (gate_pieces, v.fin_g, 0)]
        kinds += [(pieces_of(v.own_x, v.in_x, v.sum_x, N_X), v.fin_x, 0)]
        kinds += [(pieces_of(v.own_s, v.in_s, v.sum_s, 1), v.fin_s, 0)]
        listed = [(piece, fin, of) for pieces, fin, of in kinds for piece in pieces]

        for (_, _, result, rows), fin, of in listed:
            skipped = m // 2 // N_X * X_EARLY if result is v.sum_px else 0
            plan_settling(result, fin, of, rows, skipped)
        done = settle
        plan_settling(v.done_o, v.fin_o, 1, None)
        plan_settling(v.done_g, v.fin_g, 1, None)
        plan_settling(v.done_x, v.fin_x, 1, None)
        pairs = [
            [
                remote(src, dst, v.pair_sem.at[0, k], v.pair_sem.at[1, k], lay.sibling())
                for src in srcs
            ]
            for k, (dst, srcs) in enumerate(
                ((v.got_hid, (v.hid1, v.hid0)), (v.got_gt, (v.gt1, v.gt)))
            )
        ]
        pl.when(c == 0)(pairs[0][0].start)
        pl.when(c == 1)(pairs[0][1].start)
        pl.when(c == 0)(pairs[1][0].start)
    else:
        x_pieces = pieces_of(v.own_x, v.in_x, v.sum_x, N_X)[:X_EARLY]
        listed = [(piece,) for piece in out_pieces + gate_pieces + x_pieces]
        done = None
    pump = Pump(
        SeqSum(lay, [entry[0] for entry in listed], (v.seq1, v.seq2, v.seq3, v.seq4)), done
    )
    tick = pump.tick
    scan = Scan(lay, False, v.expm, scan_refs(v, "b_"))
    if more:
        for name in ("prev_x", "prev_s"):
            stages.pop(name).wait()
        pump.ready += N_X - X_EARLY + 1
        pump.feed()
        for stage in stages.values():
            stage.wait()
        for at in range(len(listed), len(finals)):
            settle(at)

    p = params(lay, v.pk, layer)
    v.expm[...] = expander(lay)
    expm = v.expm
    v.psm[...] = jnp.zeros(v.psm.shape, F32)
    v.acch[...] = jnp.zeros(v.acch.shape, F32)
    lower, upper, strict = tri("lower"), tri("upper"), tri("strict")
    col_n = 256

    def cols_at(j, size=col_n):
        return pl.ds(pl.multiple_of(j * size, LANES), size)

    def tile(i):
        return pl.ds(pl.multiple_of(8 * i, 8), 8)

    def weight_grad(left, low, theirs, got, own):
        width = low.shape[1]
        step_n = min(width, col_n)
        for side, into in ((1 - c, theirs), (c, own)):
            rows = left(side)

            @pl.loop(0, width // step_n)
            def _(j):
                at = cols_at(j, step_n)
                into[:, at] = dot(rows, low[:, at]).astype(BF)

            if into is theirs:
                copy = send(theirs, got, lay.sibling())
        return copy

    def pair_sum(copy, own, got):
        copy.wait()
        own[...] = own[...] + got[...]

    def normed_half(side):
        return v.nt[pl.ds(pl.multiple_of(side * (m // 2), 16), m // 2), :]

    def out_half(side):
        return jnp.transpose(v.no[:, pl.ds(pl.multiple_of(side * (w // 2), LANES), w // 2)])

    late_sums = []

    def project():
        for k in range(lay.parts):
            cols = slice(k * lay.share, (k + 1) * lay.share)
            v.dnp[k] = dot(v.go[...], v.wo[:, cols]).astype(BF)

    def out_grad():
        @pl.loop(0, w // col_n)
        def _(j):
            v.dy[:, cols_at(j)] = dot(v.up[...], v.wo[cols_at(j), :], NT)

    if more:
        tables = run_decays(lay, v, p)
    else:
        v.normed, v.go, v.local = v.full, v.lowx, v.lamloc
        weights = (v.wsm, v.wx, v.wg)

        def meanwhile():
            loads[3].wait()
            rows_in.wait()
            out_grad()

        forward(lay, v, p, v.resid, weights, lambda at: loads[at].wait(), project, meanwhile)
        tables = []

    @pl.loop(0, nb)
    def _(i):
        if more:
            pre = conv_pre(conv_cat(v.xp, i), p["conv_x"], p["bias_x"])
            v.xc[block(i), :] = pre * jax.nn.sigmoid(pre)
        x = v.xc[block(i), :]
        g = v.gate[block(i), :]
        gated = (v.ysd[block(i), :] + p["skip"] * x) * (g * jax.nn.sigmoid(g))
        inv = to_col(lax.rsqrt(v.sqt[tile(i), :][:1, :] / lay.inner + EPS))
        v.no[block(i), :] = (gated * inv * p["gain_out"]).astype(BF)

    if more:
        rows_in.wait()
        tick()
    copy_o = weight_grad(out_half, v.up, v.gs_o, v.gr_o, v.own_o)
    if more:
        loads[0].wait()
        out_grad()

    @pl.loop(0, nb)
    def _(i):
        g = v.gate[block(i), :]
        gated = (v.ysd[block(i), :] + p["skip"] * v.xc[block(i), :]) * (g * jax.nn.sigmoid(g))
        row = to_row(v.dy[block(i), :] * p["gain_out"] * gated)
        v.rsb[q, tile(i), :] = jnp.broadcast_to(row, (8, Q))

    row_sends = [send(v.rsb.at[q], v.rsb.at[q], target) for _, target in peers]
    pair_sum(copy_o, v.own_o, v.gr_o)
    pump.ready += N_OUT
    if more:
        tick()
    pump.feed()
    for copy in row_sends:
        copy.wait()
    if late:
        for k, target in peers:
            copy = remote(
                v.dnp.at[lax.rem(q + k, lay.parts)],
                v.late_got.at[k - 1],
                v.late_send.at[k - 1],
                v.late_recv.at[k - 1],
                target,
            )
            copy.start()
            late_sums.append(copy)
    @pl.loop(0, nb)
    def _(i):
        rd = v.rsb[0, tile(i), :]
        for k in range(1, lay.parts):
            rd = rd + v.rsb[k, tile(i), :]
        inv = to_col(lax.rsqrt(v.sqt[tile(i), :][:1, :] / lay.inner + EPS))
        rdc = to_col(rd[:1, :])
        g, x, d = v.gate[block(i), :], v.xc[block(i), :], v.dy[block(i), :]
        sg = jax.nn.sigmoid(g)
        act = g * sg
        mixed = v.ysd[block(i), :] + p["skip"] * x
        gated = mixed * act
        v.psm[5:6, :] += jnp.sum(d * (gated * inv), axis=0, keepdims=True)
        dgated = inv * p["gain_out"] * d - gated * (inv * inv * inv * rdc / lay.inner)
        dmix = dgated * act
        v.lowg[block(i), :] = (dgated * mixed * (sg * (1.0 + g * (1.0 - sg)))).astype(BF)
        v.psm[8:9, :] += jnp.sum(dmix * x, axis=0, keepdims=True)
        v.dy[block(i), :] = dmix

    lam = jnp.zeros((n, w), F32)
    total = jnp.zeros((1, LANES), F32)
    for i in reversed(range(nb)):
        rows = pl.ds(i * Q, Q)
        cum = v.cums[1, rows, :]
        last = cum[Q - 1 :, :]
        v.lamloc[i] = lam
        v.dsuf[8 * i : 8 * (i + 1), :] = jnp.broadcast_to(total, (8, LANES))
        faded = (expand(lay, expm[...], jnp.exp(cum)) * v.dy[rows, :]).astype(BF)
        dec = expand(lay, expm[...], jnp.broadcast_to(jnp.exp(last), (8, LANES)))[:1, :]
        lam = lam * dec + dot(v.bc[rows, n:], faded, TN)
        total = total + last
    if more:
        tick()
    v.own_state[...] = lam
    for copy in tables:
        copy.wait()
    scan.start()

    copy_g = weight_grad(
        normed_half, v.lowg, v.wo.at[:, :w], v.gr_g, v.own_g
    )
    pair_sum(copy_g, v.own_g, v.gr_g)
    pump.ready += N_GATE
    tick()

    in_loop = pump.later() if more else None

    @pl.loop(0, nb)
    def _(i):
        if scan.steps > 1:
            pl.when(i == 2)(functools.partial(scan.advance, 0))
        if more:
            pl.when(i == 3)(in_loop)
        causal = iota((Q, Q), 0) >= iota((Q, Q), 1)
        cum = v.cums[1, block(i), :]
        cum_t = jnp.transpose(cum)
        b_rows, c_rows = v.bc[block(i), :n], v.bc[block(i), n:]
        scores = dot(c_rows, b_rows, NT)
        stepped = (v.xc[block(i), :] * expand(lay, expm[...], v.cums[0, block(i), :])).astype(BF)
        grad = v.dy[block(i), :]
        low = grad.astype(BF)
        dscores = jnp.zeros((Q, Q), F32)
        for pair in range(lay.heads // 2):
            cols = slice(pair * LANES, (pair + 1) * LANES)
            fades = [decay_tile(cum, cum_t, lay.off + 2 * pair + e, causal) for e in range(2)]
            mixes = [(scores * fade).astype(BF) for fade in fades]
            xl, xr = halves(stepped[:, cols])
            dl, dr = halves(low[:, cols])
            dmix = dot(low[:, cols], jnp.concatenate([xl, xr], axis=0), NT)
            dscores = dscores + dmix[:, :Q] * fades[0] + dmix[:, Q:] * fades[1]
            v.dx[block(i), cols] = dot(
                jnp.concatenate(mixes, axis=0), jnp.concatenate([dl, dr], axis=0), TN
            )
        diff = low.astype(F32) * v.ysd[block(i), :] - stepped.astype(F32) * v.dx[block(i), :]
        v.rcs[block(i), :] = sum3(upper, head_sum(expm[...], diff))
        faded = (expand(lay, expm[...], jnp.exp(cum)) * grad).astype(BF)
        dsc = dscores.astype(BF)
        v.dbc[block(i), :n] = dot(dsc, c_rows, TN)
        v.dbc[block(i), n:] = dot(dsc, b_rows) + dot2(faded, v.sin[i], NT)

    for step in range(1 if scan.steps > 1 else 0, scan.steps):
        scan.advance(step)
    scan.hand_over()
    tick()
    scan.result()
    carry = v.enter[...]
    at = next(counter)
    halo_x = remote(v.hxs, v.hxr, v.ssem.at[at], v.rsem.at[at], lay.prev_run())

    in_loop = pump.later()

    @pl.loop(0, nb)
    def _(i):
        pl.when(i == 2)(in_loop)
        cat = conv_cat(v.xp, i)
        pre = conv_pre(cat, p["conv_x"], p["bias_x"])
        x = v.xc[block(i), :]
        step, cum = v.cums[0, block(i), :], v.cums[1, block(i), :]
        last = cum[Q - 1 :, :]
        fade = expand(lay, expm[...], jnp.exp(last - cum))
        step_w = expand(lay, expm[...], step)
        gone = jnp.exp(v.dsuf[tile(i), :])
        lam_out = v.lamloc[i] + expand(lay, expm[...], gone)[:1, :] * carry
        lam_b = dot2(v.bc[block(i), :n], lam_out)
        xw = x * step_w * fade
        v.dbc[block(i), :n] += dot2(xw.astype(BF), lam_out, NT)
        within = jnp.sum(lam_out * v.sin[i], axis=0, keepdims=True)
        kept = head_sum(expm[...], jnp.broadcast_to(within, (8, w)))[:1, :] * jnp.exp(last)
        dxt = v.dx[block(i), :] + fade * lam_b
        g = v.rcs[block(i), :] + sum3(strict, head_sum(expm[...], xw * lam_b)) + kept
        dstep = head_sum(expm[...], x * dxt) + p["rate"] * g
        v.acch[1:2, :] += jnp.sum(step * g, axis=0, keepdims=True)
        dpre_step = dstep * jax.nn.sigmoid(v.sm[block(i, base=16), :] + p["step_bias"])
        v.acch[0:1, :] += jnp.sum(dpre_step, axis=0, keepdims=True)
        v.dsp[block(i), :] = dpre_step
        d_xin = step_w * dxt + p["skip"] * v.dy[block(i), :]
        dpre = d_xin * silu_grad(pre)
        v.xdp[block(i), :] = dpre
        for k in range(4):
            v.psm[k : k + 1, :] += jnp.sum(dpre * cat[5 + k : 5 + k + Q, :], axis=0, keepdims=True)
        v.psm[4:5, :] += jnp.sum(dpre, axis=0, keepdims=True)

        @pl.when(i == 0)
        def _():
            v.hxs[...] = v.xdp[:16, :].astype(BF)
            halo_x.start()

    sel_top, sel_bottom = selectors(lay)
    pieces = dot(v.dbc[:half, :].astype(BF), sel_top, NT) + dot(
        v.dbc[half:, :].astype(BF), sel_bottom, NT
    )
    for k in range(lay.parts):
        v.dbs[k] = pieces[:, k * LANES : (k + 1) * LANES].astype(BF)
    bc_sends = [
        send(v.dbs.at[lax.rem(q + k, lay.parts)], v.dbr.at[k - 1], target) for k, target in peers
    ]
    inside = jnp.where((c == 1) & (z == lay.seqs - 1), 0.0, 1.0)
    tick()
    if late:
        for copy in late_sums:
            copy.wait()
        cols = pl.ds(pl.multiple_of(q * lay.share, LANES), lay.share)
        for i in range(nb):
            rows = pl.ds(i * Q, Q)
            value = v.dnp[q, rows, :].astype(F32)
            for k, _ in peers:
                value = value + v.late_got[k - 1, rows, :].astype(F32)
            inv = to_col(lax.rsqrt(v.sqt[8 * i : 8 * i + 1, :] / lay.inner + EPS))
            v.hid[rows, :] = v.resid[rows, cols].astype(F32) + inv * value
    halo_x.wait()
    v.xdp[lay.rows :, :] = v.hxr[...].astype(F32) * inside

    @pl.loop(0, nb)
    def _(i):
        cat = v.xdp[pl.ds(pl.multiple_of(i * Q, 8), Q + 8), :]
        grad = jnp.zeros((Q, w), F32)
        for k in range(4):
            grad = grad + p["conv_x"][k : k + 1, :] * cat[3 - k : 3 - k + Q, :]
        v.lowx[block(i), :] = grad.astype(BF)

    for load in loads[1:] if more else []:
        load.wait()
    copy_x = weight_grad(normed_half, v.lowx, v.wo.at[:, w:], v.gr_x, v.own_x)
    tick()

    for copy in bc_sends:
        copy.wait()
    summed = v.dbs[q].astype(F32)
    for k in range(1, lay.parts):
        summed = summed + v.dbr[k - 1].astype(F32)
    for i in range(nb):
        rows = pl.ds(i * Q, Q)
        if i < nb // 2:
            d_conv = summed[i * Q : (i + 1) * Q, :]
        else:
            d_conv = pltpu.roll(summed[i * Q - half : (i + 1) * Q - half, :], LANES // 2, 1)
        cat = conv_cat(v.sm, i)
        pre = conv_pre(cat, p["conv_sm"], p["bias_sm"])
        valid = iota((Q, LANES), 1) < lay.off
        dpre = jnp.where(valid, d_conv * silu_grad(pre), 0.0)
        v.smdp[rows, :] = dpre
        for k in range(4):
            v.psm[7:8, k * LANES : (k + 1) * LANES] += jnp.sum(
                dpre * cat[5 + k : 5 + k + Q, :], axis=0, keepdims=True
            )
        v.psm[7:8, 4 * LANES : 5 * LANES] += jnp.sum(dpre, axis=0, keepdims=True)
    v.hss[...] = v.smdp[:16, :].astype(BF)
    halo_s = send(v.hss, v.hsr, lay.prev_run())
    v.psm[6:7, :LANES] = head_sum(expm[...], v.psm[8:9, :])
    v.psm[6:7, LANES : 2 * LANES] = v.acch[0:1, :]
    v.psm[6:7, 2 * LANES : 3 * LANES] = v.acch[1:2, :] * p["rate"]
    pair_sum(copy_x, v.own_x, v.gr_x)
    halo_s.wait()
    v.smdp[lay.rows :, :] = v.hsr[...].astype(F32) * inside
    for i in range(nb):
        rows = pl.ds(i * Q, Q)
        cat = v.smdp[i * Q : (i + 1) * Q + 8, :]
        grad = jnp.zeros((Q, LANES), F32)
        for k in range(4):
            grad = grad + p["conv_sm"][k : k + 1, :] * cat[3 - k : 3 - k + Q, :]
        lane = iota((Q, LANES), 1)
        first = jnp.where(lane < lay.off + GROUP, v.dsp[rows, :], 0.0)
        v.lowsm[rows, :] = jnp.where(lane < lay.off, grad, first).astype(BF)
    copy_s = weight_grad(normed_half, v.lowsm, v.wo.at[:, :LANES], v.gr_s, v.own_s)
    pump.ready += N_X if more else X_EARLY
    if not more:
        v.rest_x[...] = v.own_x[m // 2 // N_X * X_EARLY :, :]
    tick()

    v.rdacc[...] = jnp.zeros(v.rdacc.shape, F32)
    v.gains[...] = jnp.broadcast_to(p["gain"], (8, m))
    spread = (v.full, v.ag_send, v.ag_recv) if gather else ()
    head_sum_of = HeadSum(lay, v.dnp, v.got, v.rs_send, v.rs_recv, *spread)
    for k in (3, 1, 2, 0):
        cols = head_sum_of.cols(k)
        grad = dot(v.lowg[...], v.wg[cols, :], NT) + dot(v.lowx[...], v.wx[cols, :], NT)
        grad = grad + dot(v.lowsm[...], v.wsm[cols, :], NT)
        v.dnp[k] = grad.astype(BF)
        v.rdacc[...] += fold(grad * v.gains[:1, cols] * v.resid[:, cols].astype(F32))
        for i in range(nb):
            if k == head_sum_of.near(i):
                head_sum_of.first(i)
    for i in range(nb):
        row = to_row(v.rdacc[i * Q : (i + 1) * Q, :])
        v.rd2[8 * i : 8 * (i + 1), :] = jnp.broadcast_to(row, (8, Q))
    rd_sends = [send(v.rd2, v.got_rows.at[k - 1], target) for k, target in peers]
    pair_sum(copy_s, v.own_s, v.gr_s)
    if more:
        pump.ready += 1
    cols = pl.ds(pl.multiple_of(q * lay.share, LANES), lay.share)
    own_gain = v.gains[:1, cols]
    tick()
    for copy in rd_sends:
        copy.wait()
    inner = v.rd2[...]
    for k, _ in peers:
        inner = inner + v.got_rows[k - 1]
    rms_sum = jnp.zeros((1, lay.share), F32)
    for i in range(nb + 2):
        if i < nb:
            head_sum_of.second(i)
        if 1 <= i <= nb:
            at = i - 1
            rows = pl.ds(at * Q, Q)
            total = head_sum_of.total(at)
            start = v.resid[rows, cols].astype(F32)
            x = v.resid[rows, :].astype(F32)
            scale = lax.rsqrt(jnp.mean(x * x, axis=1, keepdims=True) + EPS)
            value = (
                v.up[rows, cols].astype(F32)
                + scale * (own_gain * total)
                - start * (scale * scale * scale * to_col(inner[8 * at : 8 * at + 1, :] / m))
            )
            rms_sum = rms_sum + jnp.sum(total * start * scale, axis=0, keepdims=True)
            v.gt[rows, :] = value
            if gather:
                v.full[rows, cols] = value.astype(BF)
                head_sum_of.give(at)
        if i >= 2 and gather:
            head_sum_of.relay(i - 2)
        tick()
    v.psm[8:9, :] = jnp.zeros((1, w), F32)
    v.psm[8:9, : lay.share] = rms_sum
    if more:
        pl.when(c == 1)(pairs[1][1].start)
        column = [(a, b) for a in range(2) for b in range(lay.seqs) if a or b]
        own_slot = c * lay.seqs + z
        smalls = []
        for at, (a, b) in enumerate(column):
            to_c, to_z = (c + a) % 2, lax.rem(z + b, lay.seqs)
            to = (to_c, to_z, q)
            pair = [
                remote(src, v.slots.at[own_slot], v.slot_sem.at[0, at], v.slot_sem.at[1, at], to)
                for src in (v.psm, v.small)
            ]
            pl.when(to_c == 0)(pair[0].start)
            pl.when(to_c == 1)(pair[1].start)
            smalls.append(pair[0])
        v.slots[own_slot] = jnp.where(c == 0, v.psm[...], v.small[...])
        tick()
        for copy in smalls:
            copy.wait()
        value = v.slots[0]
        for k in range(1, 2 * lay.seqs):
            value = value + v.slots[k]
        v.total[:16, :] = value
        v.rest_rows[q] = value[8:16, :]
        parts = []
        for k, target in peers:
            copy = remote(
                v.rest_rows.at[q],
                v.rest_rows.at[q],
                v.part_sem.at[0, k - 1],
                v.part_sem.at[1, k - 1],
                target,
            )
            copy.start()
            parts.append(copy)
        tick()
        for copy in parts:
            copy.wait()
        for k in range(lay.parts):
            v.total[16 + 8 * k : 24 + 8 * k, :] = v.rest_rows[k]
    pump.finish()
    if gather:
        head_sum_of.finish()
    if more:
        for of, here, there in finals:
            pl.when(c == of)(here.wait)
            pl.when(c == of)(there.wait_recv)
            pl.when(c != of)(there.wait_send)
        for pair in pairs:
            pair[0].wait()


def bwd_layer(lay, layer, args, more):
    late = gather = not more
    outs, scratch = back_outs(lay, late, gather, more), back_scratch(lay, late, gather, more)
    vmem, hbm = pl.BlockSpec(memory_space=VM), pl.BlockSpec(memory_space=HB)
    names = back_ins(lay, more)
    specs = [vmem if name in ("resid", "pk") else hbm for name in names]
    out_specs = [vmem] * len(outs)
    if more:
        out_specs[-6:] = [hbm] * 6
    got = pl.pallas_call(
        functools.partial(bwd_kernel, lay, layer, late, gather, more),
        out_shape=tuple(outs.values()),
        in_specs=specs,
        out_specs=tuple(out_specs),
        scratch_shapes=list(scratch.values()),
        compiler_params=pltpu.CompilerParams(
            collective_id=5 + layer, has_side_effects=True, vmem_limit_bytes=63 << 20
        ),
        name=f"mixer_backward_{layer}",
    )(*(args[name.removeprefix("from_")] for name in names))
    return Names(list(outs), got)


def on_device(
    mesh_shape, tokens, cotangent, rms_gain, proj_gate, proj_x, proj_bc, proj_step, conv_x, conv_x_bias,
    conv_bc, conv_bc_bias, step_bias, decay_log, skip_gain, norm_gain, proj_out,
):
    pieces, rows, model = tokens.shape
    width, heads, local_state = proj_x.shape[2], proj_step.shape[2], proj_bc.shape[3]
    lay = Lay(mesh_shape, rows, width, model, heads, local_state)
    section = lax.axis_index("section")
    group = jnp.pad(proj_step[0], ((0, 0), (0, GROUP - heads)))
    w_small = jnp.concatenate(
        [
            proj_bc[0].reshape(model, lay.off),
            group,
            group,
            group,
            jnp.zeros((model, LANES - lay.off - 3 * GROUP), BF),
        ],
        axis=1,
    )
    taps = conv_x.shape[1]
    own = (proj_gate[0], proj_x[0], w_small, proj_out[0])
    first = start_layer(
        lay,
        tokens,
        *own,
        conv_x[0],
        conv_x_bias,
        norm_gain,
        rms_gain,
        conv_bc.reshape(taps, lay.off),
        conv_bc_bias.reshape(1, lay.off),
        step_bias,
        decay_log,
        skip_gain,
    )
    args = dict(vars(first), tokens=tokens, cotangent=cotangent, resid=first.full)
    args.update({f"own{k}": weight for k, weight in enumerate(own)})
    one = bwd_layer(lay, 1, args, False)
    args.update(up=one.full, prev_x=one.rest_x, prev_s=one.own_s, done_o=one.sum_o, done_g=one.sum_g)
    args.update(done_x=one.sum_x, small=one.psm, hid0=first.hid, hid1=one.hid, gt1=one.gt)
    zero = bwd_layer(lay, 0, args, True)
    at_zero = section == 0

    def both_pieces(ours0, ours1, theirs):
        ours = jnp.where(at_zero, ours0, ours1)
        return jnp.stack([jnp.where(at_zero, ours, theirs), jnp.where(at_zero, theirs, ours)])[None]

    hid = both_pieces(first.hid, one.hid, zero.got_hid)
    gt = both_pieces(zero.gt, one.gt, zero.got_gt)
    g_gate, g_x, g_out, g_sm = (
        a.astype(F32)[None] for a in (zero.fin_g, zero.fin_x, zero.fin_o, zero.fin_s)
    )
    total = zero.total
    lane = lay.off
    rms_all = total[16:].reshape(lay.parts, 8, width)[:, 0, : lay.share].reshape(1, model)
    conv_small = total[7].reshape(-1, LANES)[:5, : lay.off]

    def head_row(k):
        return total[6, k * LANES + lane : k * LANES + lane + heads][None]

    return (
        hid,
        gt,
        rms_all,
        g_gate,
        g_x,
        g_sm[:, :, : lay.off].reshape(1, model, 2, local_state),
        g_sm[:, :, lane : lane + heads],
        total[None, 0:4],
        total[4:5],
        conv_small[:4].reshape(1, 4, 2, local_state),
        conv_small[4].reshape(1, 2, local_state),
        head_row(1),
        head_row(2),
        head_row(0),
        total[5:6],
        g_out,
    )


def solution(mesh):
    placed = (
        P(None, "seq", None),
        P(None, "seq", None),
        P("section", None),
        P("section", None, "head"),
        P("section", None, "head"),
        P("section", None, None, "head"),
        P("section", None, "head"),
        P("section", None, "head"),
        P("section", "head"),
        P("section", None, None, "head"),
        P("section", None, "head"),
        P("section", "head"),
        P("section", "head"),
        P("section", "head"),
        P("section", "head"),
        P("section", "head", None),
    )
    back = (P("section", None, "seq", "head"),) * 2 + placed[2:]
    shape = tuple(mesh.shape[name] for name in ("section", "seq", "head"))
    return jax.shard_map(
        functools.partial(on_device, shape),
        mesh=mesh,
        in_specs=placed,
        out_specs=back,
        check_vma=False,
    )
```

```python
import functools

import jax
import jax.numpy as jnp
from jax import lax
from jax.experimental import pallas as pl
from jax.experimental.pallas import tpu as pltpu
from jax.sharding import PartitionSpec as P

F32, BF = jnp.float32, jnp.bfloat16
MESH = pl.DeviceIdType.MESH
EPS = 1e-05
Q = 128
LANES = 128
GROUP = 16
NN, NT, TN = ((1,), (0,)), ((1,), (1,)), ((0,), (0,))
VM, HB = pltpu.VMEM, pl.ANY


def dot(a, b, dims=NN):
    return lax.dot_general(a, b, (dims, ((), ())), preferred_element_type=F32)


def iota(shape, dim):
    return lax.broadcasted_iota(jnp.int32, shape, dim)


def split3(v):
    hi = v.astype(BF)
    rest = v - hi.astype(F32)
    mid = rest.astype(BF)
    return hi, mid, (rest - mid.astype(F32)).astype(BF)


def sum3(matrix, v, dims=NN):
    hi, mid, low = split3(v)
    return dot(matrix, hi, dims) + dot(matrix, mid, dims) + dot(matrix, low, dims)


def dot2(a, v, dims=NN):
    hi = v.astype(BF)
    return dot(a, hi, dims) + dot(a, (v - hi.astype(F32)).astype(BF), dims)


def silu_grad(v):
    sg = jax.nn.sigmoid(v)
    return sg * (1.0 + v * (1.0 - sg))


def fold(v):
    total = v[:, :LANES]
    for k in range(1, v.shape[1] // LANES):
        total = total + v[:, k * LANES : (k + 1) * LANES]
    return total


def to_row(v):
    return jnp.sum(jnp.transpose(fold(v)), axis=0, keepdims=True)


def to_col(row):
    return jnp.transpose(jnp.broadcast_to(row, (Q, Q)))[:, :1]


class Lay:
    def __init__(self, mesh_shape, rows, width, model, heads, local_state):
        self.sections, self.seqs, self.parts = mesh_shape
        self.rows, self.width, self.model, self.heads = rows, width, model, heads
        self.nb = rows // Q
        self.share = model // self.parts
        self.ls = local_state
        self.off = 2 * local_state
        self.hp = width // heads
        self.inner = width * self.parts
        self.state = local_state * self.parts

    def place(self):
        self.c = lax.axis_index("section")
        self.z = lax.axis_index("seq")
        self.q = lax.axis_index("head")

    def heads_peers(self):
        return [
            (k, (self.c, self.z, lax.rem(self.q + k, self.parts)))
            for k in range(1, self.parts)
        ]

    def seq_peers(self):
        return [(k, (self.c, lax.rem(self.z + k, self.seqs), self.q)) for k in range(1, self.seqs)]

    def sibling(self):
        return (1 - self.c, self.z, self.q)

    def next_run(self):
        last = self.z == self.seqs - 1
        return (
            jnp.where(last, 1 - self.c, self.c),
            jnp.where(last, 0, self.z + 1),
            self.q,
        )

    def prev_run(self):
        first = self.z == 0
        return (
            jnp.where(first, 1 - self.c, self.c),
            jnp.where(first, self.seqs - 1, self.z - 1),
            self.q,
        )


def meet(targets):
    barrier = pltpu.get_barrier_semaphore()
    for target in targets:
        pl.semaphore_signal(barrier, inc=1, device_id=target, device_id_type=MESH)
    pl.semaphore_wait(barrier, len(targets))


def column_and_heads(lay):
    column = [
        ((lay.c + s) % 2, lax.rem(lay.z + k, lay.seqs), lay.q)
        for s in range(2)
        for k in range(lay.seqs)
        if s or k
    ]
    return column + [target for _, target in lay.heads_peers()]


def remote(src, dst, send, recv, target):
    return pltpu.make_async_remote_copy(
        src_ref=src,
        dst_ref=dst,
        send_sem=send,
        recv_sem=recv,
        device_id=target,
        device_id_type=MESH,
    )


class SeqSum:
    def __init__(self, lay, pieces, sems):
        self.pieces, self.sems = pieces, sems
        z, n = lay.z, lay.seqs
        self.left = z < n // 2
        depth = jnp.where(self.left, z, n - 1 - z)
        self.outer = depth > 0
        self.middle = depth == n // 2 - 1
        self.inside = (lay.c, jnp.where(self.left, z + 1, z - 1), lay.q)
        self.outside = (lay.c, jnp.clip(jnp.where(self.left, z - 1, z + 1), 0, n - 1), lay.q)

    def pass_on(self, k, src):
        own, inner, result, rows = self.pieces[k]
        ssem, asem, tsem, _ = self.sems

        def to_middle():
            remote(src, result.at[rows], ssem.at[k], tsem.at[k], self.inside).start()

        def to_next():
            remote(src, inner.at[rows], ssem.at[k], asem.at[k], self.inside).start()

        pl.when(self.middle)(to_middle)
        pl.when(jnp.logical_not(self.middle))(to_next)

    def inward(self, k):
        own, inner, result, rows = self.pieces[k]
        ssem, asem, tsem, _ = self.sems

        @pl.when(self.outer)
        def _():
            remote(own.at[rows], inner.at[rows], ssem.at[k], asem.at[k], self.inside).wait_recv()
            inner[rows, :] = inner[rows, :] + own[rows, :]
            self.pass_on(k, inner.at[rows])

    def push(self, k):
        @pl.when(jnp.logical_not(self.outer))
        def _():
            own, _, _, rows = self.pieces[k]
            self.pass_on(k, own.at[rows])

    def outward(self, k):
        own, inner, result, rows = self.pieces[k]
        ssem, _, tsem, osem = self.sems

        def arrived():
            remote(own.at[rows], result.at[rows], ssem.at[k], tsem.at[k], self.inside).wait_recv()

        @pl.when(self.outer)
        def _():
            arrived()

            @pl.when(self.middle)
            def _():
                result[rows, :] = result[rows, :] + inner[rows, :]

            remote(result.at[rows], result.at[rows], osem.at[k], tsem.at[k], self.outside).start()

    def ending(self, k):
        own, inner, result, rows = self.pieces[k]
        ssem, _, tsem, _ = self.sems

        @pl.when(jnp.logical_not(self.outer))
        def _():
            remote(own.at[rows], result.at[rows], ssem.at[k], tsem.at[k], self.inside).wait_recv()

            @pl.when(self.middle)
            def _():
                result[rows, :] = result[rows, :] + own[rows, :]

    def finish(self):
        for k, (own, inner, result, rows) in enumerate(self.pieces):
            ssem, _, tsem, osem = self.sems
            remote(own.at[rows], result.at[rows], ssem.at[k], tsem.at[k], self.inside).wait_send()

            @pl.when(self.outer)
            def _():
                remote(
                    result.at[rows], result.at[rows], osem.at[k], tsem.at[k], self.outside
                ).wait_send()


class Pump:
    def __init__(self, seq_sum, done=None):
        self.sum, self.done = seq_sum, done
        self.ready = self.pushed = self.taken = self.given = self.ended = 0

    def end(self, k):
        self.sum.ending(k)
        if self.done is not None:
            self.done(k)

    def plan(self):
        steps = []

        def feed():
            while self.pushed < min(self.ready, self.taken + 3):
                steps.append((self.sum.push, self.pushed))
                self.pushed += 1

        feed()
        if self.taken < self.pushed:
            steps.append((self.sum.inward, self.taken))
            self.taken += 1
            feed()
        if self.given < self.taken - 1:
            steps.append((self.sum.outward, self.given))
            self.given += 1
        if self.ended < self.given - 2:
            steps.append((self.end, self.ended))
            self.ended += 1
        return steps

    def feed(self):
        while self.pushed < min(self.ready, self.taken + 3):
            self.sum.push(self.pushed)
            self.pushed += 1

    def tick(self):
        self.later()()

    def later(self):
        steps = self.plan()

        def act():
            for kind, piece in steps:
                kind(piece)

        return act

    def finish(self):
        while self.taken < self.ready:
            self.tick()
        while self.given < self.taken:
            self.sum.outward(self.given)
            self.given += 1
        while self.ended < self.given:
            self.end(self.ended)
            self.ended += 1
        self.sum.finish()


class Scan:
    def __init__(self, lay, forward, expm, v):
        self.lay, self.expm, self.v = lay, expm, v
        self.steps = max(lay.seqs - 1, 0).bit_length()
        assert 1 << self.steps == lay.seqs
        self.forward = forward
        self.u = lay.z if forward else lay.seqs - 1 - lay.z
        self.first = lay.c == (0 if forward else 1)

    def device(self, u):
        u = jnp.clip(u, 0, self.lay.seqs - 1)
        return (self.lay.c, u if self.forward else self.lay.seqs - 1 - u, self.lay.q)

    def row(self, chosen):
        total = jnp.ones((8, LANES), F32)
        for u in range(self.lay.seqs):
            z = u if self.forward else self.lay.seqs - 1 - u
            total = jnp.where(chosen(u), total * self.v.table[z], total)
        return expand(self.lay, self.expm[...], total)[:1, :]

    def copies(self, s, ahead, only=None):
        v = self.v
        src, dst = (v.main_s, v.main_r) if ahead else (v.back_s, v.back_r)
        send, recv = (v.scan_sem.at[0 if ahead else 2], v.scan_sem.at[1 if ahead else 3])
        out = []
        for t in range(1 << s) if only is None else (only,):
            u = self.u + 1 + t if ahead else self.u - 1 - t
            out.append(
                remote(src, dst.at[s], send.at[(1 << s) - 1 + t], recv.at[s], self.device(u))
            )
        return out

    def gives(self, s, ahead):
        place = self.u if ahead else self.lay.seqs - 1 - self.u
        return lax.rem(place, 2 << s) == (1 << s) - 1

    def takes(self, s, ahead):
        place = self.u if ahead else self.lay.seqs - 1 - self.u
        return lax.rem(place // (1 << s), 2) == 1

    def give(self, s):
        v = self.v

        @pl.when(self.gives(s, True))
        def _():
            own_decay = self.row(lambda u: u == self.u)
            v.main_s[...] = (v.enter[...] * own_decay + v.own_state[...]).astype(BF)
            for copy in self.copies(s, True):
                copy.start()

        @pl.when(self.first & self.gives(s, False))
        def _():
            v.back_s[...] = (v.rest[...] + v.own_state[...] * self.row(lambda u: u > self.u)).astype(BF)
            for copy in self.copies(s, False):
                copy.start()

    def start(self):
        v = self.v
        v.enter[...] = jnp.zeros(v.enter.shape, F32)
        v.rest[...] = jnp.zeros(v.rest.shape, F32)
        if self.steps:
            self.give(0)

    def advance(self, s):
        v = self.v

        @pl.when(self.takes(s, True))
        def _():
            self.copies(s, True, 0)[0].wait_recv()
            begin = (self.u // (1 << s)) * (1 << s)
            between = self.row(lambda u: (u >= begin) & (u < self.u))
            v.enter[...] += between * v.main_r[s].astype(F32)

        @pl.when(self.first & self.takes(s, False))
        def _():
            self.copies(s, False, 0)[0].wait_recv()
            v.rest[...] += v.back_r[s].astype(F32)

        if s + 1 < self.steps:
            self.give(s + 1)

    def hand_over(self):
        v = self.v
        self.total = remote(
            v.total_s, v.total_r, v.total_sem.at[0], v.total_sem.at[1], self.lay.sibling()
        )

        @pl.when(self.first)
        def _():
            own_decay = self.row(lambda u: u == self.u)
            after = self.row(lambda u: u > self.u)
            through = (v.enter[...] * own_decay + v.own_state[...]) * after
            v.total_s[...] = (through + v.rest[...]).astype(BF)
            self.total.start()

    def result(self):
        v = self.v

        @pl.when(jnp.logical_not(self.first))
        def _():
            self.total.wait_recv()
            v.enter[...] += self.row(lambda u: u < self.u) * v.total_r[...].astype(F32)

        pl.when(self.first)(self.total.wait_send)
        for s in range(self.steps):
            for ahead in (True, False):
                gives = self.gives(s, ahead)

                @pl.when(gives if ahead else self.first & gives)
                def _():
                    for copy in self.copies(s, ahead):
                        copy.wait_send()


def scan_scratch(lay, kinds):
    n, w, steps = lay.state, lay.width, max(lay.seqs - 1, 1).bit_length()
    dma = pltpu.SemaphoreType.DMA
    out = dict(
        table=VM((lay.seqs, 8, LANES), F32),
        own_state=VM((n, w), F32),
        enter=VM((n, w), F32),
        rest=VM((n, w), F32),
        main_s=VM((n, w), BF),
        back_s=VM((n, w), BF),
        total_s=VM((n, w), BF),
        table_sem=dma((2, max(lay.seqs - 1, 1))),
    )
    for kind in kinds:
        out[kind + "main_r"] = VM((steps, n, w), BF)
        out[kind + "back_r"] = VM((steps, n, w), BF)
        out[kind + "total_r"] = VM((n, w), BF)
        out[kind + "scan_sem"] = dma((4, max(lay.seqs - 1, 1)))
        out[kind + "total_sem"] = dma((2,))
    return out


def scan_refs(v, kind):
    shared = ["table", "own_state", "enter", "rest", "main_s", "back_s", "total_s"]
    own = ["main_r", "back_r", "total_r", "scan_sem", "total_sem"]
    refs = [getattr(v, name) for name in shared] + [getattr(v, kind + name) for name in own]
    return Names(shared + own, refs)


def share_table(lay, v):
    copies = [
        remote(v.table.at[lay.z], v.table.at[lay.z], v.table_sem.at[0, k - 1], v.table_sem.at[1, k - 1], to)
        for k, to in lay.seq_peers()
    ]
    for copy in copies:
        copy.start()
    return copies


class Names:
    def __init__(self, names, refs):
        assert len(names) == len(refs), (len(names), len(refs))
        self.__dict__.update(zip(names, refs))


def pieces_of(own, inner, result, count):
    size = own.shape[0] // count
    return [(own, inner, result, pl.ds(k * size, size)) for k in range(count)]


def expander(lay):
    lane = iota((LANES, lay.width), 0) - lay.off
    head = iota((LANES, lay.width), 1) // lay.hp
    hit = (lane >= 0) & (lane < 3 * GROUP) & (lax.rem(lane + GROUP * 8, GROUP) == head)
    return jnp.where(hit, 1.0, 0.0).astype(BF)


def expand(lay, exp_matrix, v):
    hi, mid, low = split3(v)
    lane = iota(v.shape, 1) - lay.off
    packed = jnp.where(
        lane < 0,
        0.0,
        jnp.where(
            lane < GROUP,
            hi.astype(F32),
            jnp.where(
                lane < 2 * GROUP, mid.astype(F32), jnp.where(lane < 3 * GROUP, low.astype(F32), 0.0)
            ),
        ),
    )
    return dot(packed.astype(BF), exp_matrix)


def head_sum(exp_matrix, v):
    hi, mid, low = split3(v)
    return dot(hi, exp_matrix, NT) + dot(mid, exp_matrix, NT) + dot(low, exp_matrix, NT)


def selectors(lay):
    shape = (lay.parts * LANES, 2 * lay.state)
    row, col = iota(shape, 0), iota(shape, 1)
    piece, lane = row // LANES, lax.rem(row, LANES)
    kind, n = col // lay.state, lax.rem(col, lay.state)
    want = kind * lay.ls + lax.rem(n, lay.ls)
    same = piece == n // lay.ls
    top = jnp.where(same & (lane == want), 1.0, 0.0).astype(BF)
    bottom = jnp.where(same & (lane == want + LANES // 2), 1.0, 0.0).astype(BF)
    return top, bottom


def tri(kind):
    row, col = iota((Q, Q), 0), iota((Q, Q), 1)
    hit = {"lower": row >= col, "upper": row <= col, "strict": row > col}[kind]
    return jnp.where(hit, 1.0, 0.0).astype(BF)


def block(i, size=Q, base=0):
    return pl.ds(pl.multiple_of(i * size + base, 8), size)


def conv_cat(ref, i):
    return ref[pl.ds(pl.multiple_of(i * Q + 8, 8), Q + 8), :]


def conv_pre(cat, kernel, bias):
    total = bias
    for k in range(4):
        total = total + kernel[k : k + 1, :] * cat[5 + k : 5 + k + Q, :]
    return total


def softplus(v):
    return jnp.maximum(v, 0.0) + jnp.log1p(jnp.exp(-jnp.abs(v)))


def params(lay, pk_ref, layer):
    pk = pk_ref[layer]
    w = lay.width
    out = dict(
        conv_x=pk[0:4, :],
        bias_x=pk[4:5, :],
        gain_out=pk[5:6, :],
        skip=pk[6:7, :],
        gain=jnp.concatenate([pk[7:8, :], pk[8:9, :]], axis=1)
        if lay.model == 2 * w
        else None,
        conv_sm=jnp.concatenate([pk[9:10, k * LANES : (k + 1) * LANES] for k in range(4)], axis=0),
        bias_sm=pk[9:10, 4 * LANES : 5 * LANES],
        step_bias=pk[10:11, 0:LANES],
        rate=pk[10:11, LANES : 2 * LANES],
    )
    return out


def decay_tile(cum, cum_t, lane, causal):
    diff = cum[:, lane : lane + 1] - cum_t[lane : lane + 1, :]
    return jnp.exp(jnp.where(causal, diff, -1e30))


def halves(v):
    lane = iota(v.shape, 1)
    left = lane < LANES // 2
    zero = jnp.zeros_like(v)
    return jnp.where(left, v, zero), jnp.where(left, zero, v)


class HeadSum:
    def __init__(self, lay, part, got, send, recv, full=None, gsend=None, grecv=None):
        assert lay.parts == 4
        self.lay, self.part, self.got, self.send, self.recv = lay, part, got, send, recv
        self.full, self.gsend, self.grecv = full, gsend, grecv
        q = lay.q
        self.index = (q, q + 1 - 2 * lax.rem(q, 2), lax.rem(q + 2, 4), 3 - q)
        self.out = []

    def target(self, mask):
        return (self.lay.c, self.lay.z, self.index[mask])

    def cols(self, mask):
        return pl.ds(pl.multiple_of(self.index[mask] * self.lay.share, LANES), self.lay.share)

    def near(self, i):
        return 1 if i % 2 == 0 else 2

    def rows(self, i):
        return pl.ds(i * Q, Q)

    def copy(self, kind, i):
        near, rows = self.near(i), self.rows(i)
        src = (near, 3, 3 - near)[kind]
        return remote(
            self.part.at[src, rows],
            self.got.at[kind, rows],
            self.send.at[kind, i],
            self.recv.at[kind, i],
            self.target(near if kind < 2 else 3 - near),
        )

    def first(self, i):
        self.steps = getattr(self, "steps", {})
        self.steps[i] = [self.copy(kind, i) for kind in range(2)]
        for copy in self.steps[i]:
            copy.start()

    def second(self, i):
        for copy in self.steps[i]:
            copy.wait()
        far, rows = 3 - self.near(i), self.rows(i)
        both = self.part[far, rows, :].astype(F32) + self.got[1, rows, :].astype(F32)
        self.part[far, rows, :] = both.astype(BF)
        copy = self.copy(2, i)
        copy.start()
        self.steps[i] = copy

    def total(self, i):
        self.steps[i].wait()
        rows = self.rows(i)
        value = self.part[0, rows, :].astype(F32) + self.got[0, rows, :].astype(F32)
        return value + self.got[2, rows, :].astype(F32)

    def spread(self, i, mask, kind, to):
        block = self.full.at[self.rows(i), self.cols(mask)]
        copy = remote(block, block, self.gsend.at[kind, i], self.grecv.at[kind, i], self.target(to))
        copy.start()
        return copy

    def give(self, i):
        self.steps[i] = [self.spread(i, 0, 0, 1), self.spread(i, 0, 1, 2)]

    def relay(self, i):
        near = self.near(i)
        self.steps[i][2 - near].wait()
        self.steps[i] = [self.steps[i][near - 1], self.spread(i, 3 - near, 2, near)]

    def finish(self):
        for copies in self.steps.values():
            for copy in copies:
                copy.wait()


class Load:
    def __init__(self, own, other, dst, sem, mine):
        self.mine = mine
        self.copies = [pltpu.make_async_copy(src, dst, sem) for src in (own, other)]

    def start(self):
        pl.when(self.mine)(self.copies[0].start)
        pl.when(jnp.logical_not(self.mine))(self.copies[1].start)

    def wait(self):
        self.copies[0].wait()


def forward(lay, v, p, resid, weights, ready, project, meanwhile=None):
    c, z, q = lay.c, lay.z, lay.q
    nb, w, n = lay.nb, lay.width, lay.state
    wsm, wx, wg = weights
    expm, normed, sm, xp, cums, bc = v.expm, v.normed, v.sm, v.xp, v.cums, v.bc
    scan = Scan(lay, True, expm, scan_refs(v, "f_"))
    counter = iter(range(16))

    def send(src, dst, target):
        at = next(counter)
        copy = remote(src, dst, v.fsend.at[at], v.frecv.at[at], target)
        copy.start()
        return copy

    @pl.loop(0, nb)
    def _(i):
        x = resid[block(i), :].astype(F32)
        scale = lax.rsqrt(jnp.mean(x * x, axis=1, keepdims=True) + EPS)
        normed[block(i), :] = (x * scale * p["gain"]).astype(BF)

    ready(0)
    sm[16:, :] = dot(normed[...], wsm[...])
    v.shs[...] = sm[lay.rows :, :].astype(BF)
    after = lay.next_run()
    halo_s = send(v.shs, v.shr, after)
    tables = run_decays(lay, v, p)
    ready(1)
    step_n = 256

    @pl.loop(0, w // step_n)
    def _(j):
        cols = pl.ds(pl.multiple_of(j * step_n, step_n), step_n)
        xp[16:, cols] = dot(normed[...], wx[:, cols])

    v.xhs[...] = xp[lay.rows :, :].astype(BF)
    halo_x = send(v.xhs, v.xhr, after)
    halo_s.wait()
    inside = jnp.where((c == 0) & (z == 0), 0.0, 1.0)
    sm[:16, :] = v.shr[...].astype(F32) * inside

    half = lay.rows // 2
    conv_rows = []
    for i in range(nb):
        pre = conv_pre(conv_cat(sm, i), p["conv_sm"], p["bias_sm"])
        conv_rows.append(pre * jax.nn.sigmoid(pre))
    top = jnp.concatenate(conv_rows[: nb // 2], axis=0)
    bottom = jnp.concatenate(conv_rows[nb // 2 :], axis=0)
    lane = iota(top.shape, 1)
    v.bcg[q] = jnp.where(lane < LANES // 2, top, pltpu.roll(bottom, LANES // 2, 1)).astype(BF)
    sends = [send(v.bcg.at[q], v.bcg.at[q], target) for _, target in lay.heads_peers()]
    halo_x.wait()
    xp[:16, :] = v.xhr[...].astype(F32) * inside

    @pl.loop(0, nb)
    def _(i):
        pre = conv_pre(conv_cat(xp, i), p["conv_x"], p["bias_x"])
        v.xc[block(i), :] = pre * jax.nn.sigmoid(pre)

    for copy in sends:
        copy.wait()
    pieces = jnp.concatenate([v.bcg[k] for k in range(lay.parts)], axis=1)
    sel_top, sel_bottom = selectors(lay)
    bc[:half, :] = dot(pieces, sel_top).astype(BF)
    bc[half:, :] = dot(pieces, sel_bottom).astype(BF)

    v.local[0] = jnp.zeros((n, w), F32)
    v.dpre[...] = jnp.zeros(v.dpre.shape, F32)
    state = None
    total = jnp.zeros((1, LANES), F32)
    for i in range(nb):
        rows = pl.ds(i * Q, Q)
        cum = cums[1, rows, :]
        last = cum[Q - 1 :, :]
        weight = jnp.exp(last - cum) * cums[0, rows, :]
        xw = (v.xc[rows, :] * expand(lay, expm[...], weight)).astype(BF)
        update = dot(bc[rows, :n], xw, TN)
        dec = expand(lay, expm[...], jnp.broadcast_to(jnp.exp(last), (8, LANES)))[:1, :]
        state = update if i == 0 else state * dec + update
        total = total + last
        if i < nb - 1:
            v.local[i + 1] = state
            v.dpre[8 * (i + 1) : 8 * (i + 2), :] = jnp.broadcast_to(total, (8, LANES))
    v.own_state[...] = state
    for copy in tables:
        copy.wait()
    scan.start()
    ready(2)

    @pl.loop(0, w // step_n)
    def _(j):
        cols = pl.ds(pl.multiple_of(j * step_n, step_n), step_n)
        v.gate[:, cols] = dot(normed[...], wg[:, cols])

    @pl.loop(0, nb)
    def _(i):
        if scan.steps > 1:
            pl.when(i == nb - 1)(functools.partial(scan.advance, 0))
        causal = iota((Q, Q), 0) >= iota((Q, Q), 1)
        cum = cums[1, block(i), :]
        cum_t = jnp.transpose(cum)
        scores = dot(bc[block(i), n:], bc[block(i), :n], NT)
        stepped = (v.xc[block(i), :] * expand(lay, expm[...], cums[0, block(i), :])).astype(BF)
        for pair in range(lay.heads // 2):
            cols = slice(pair * LANES, (pair + 1) * LANES)
            mixes = [
                (scores * decay_tile(cum, cum_t, lay.off + 2 * pair + e, causal)).astype(BF)
                for e in range(2)
            ]
            xl, xr = halves(stepped[:, cols])
            v.ysd[block(i), cols] = dot(
                jnp.concatenate(mixes, axis=1), jnp.concatenate([xl, xr], axis=0)
            )

    @pl.loop(0, nb)
    def _(i):
        v.nt[:, pl.ds(pl.multiple_of(i * Q, Q), Q)] = jnp.transpose(normed[block(i), :])

    if meanwhile is not None:
        meanwhile()
    for step in range(1 if scan.steps > 1 else 0, scan.steps):
        scan.advance(step)
    scan.hand_over()
    scan.result()
    start = v.enter[...]

    @pl.loop(0, nb)
    def _(i):
        cum = cums[1, block(i), :]
        dec = jnp.exp(v.dpre[pl.ds(pl.multiple_of(8 * i, 8), 8), :])
        full = v.local[i] + expand(lay, expm[...], dec)[:1, :] * start
        v.sin[i] = full
        carried = dot2(bc[block(i), n:], full) * expand(lay, expm[...], jnp.exp(cum))
        y = v.ysd[block(i), :] + carried
        v.ysd[block(i), :] = y
        g = v.gate[block(i), :]
        gated = (y + p["skip"] * v.xc[block(i), :]) * (g * jax.nn.sigmoid(g))
        row = to_row(gated * gated)
        v.sqb[q, pl.ds(pl.multiple_of(8 * i, 8), 8), :] = jnp.broadcast_to(row, (8, Q))
        v.go[block(i), :] = (gated * p["gain_out"]).astype(BF)

    squares = [send(v.sqb.at[q], v.sqb.at[q], target) for _, target in lay.heads_peers()]
    if meanwhile is None:
        ready(3)
    project()
    for copy in squares:
        copy.wait()
    total_sq = v.sqb[0]
    for k in range(1, lay.parts):
        total_sq = total_sq + v.sqb[k]
    v.sqt[...] = total_sq


def run_decays(lay, v, p):
    lower = tri("lower")
    lasts = []
    for i in range(lay.nb):
        rows = pl.ds(i * Q, Q)
        step = softplus(v.sm[16 + i * Q : 16 + (i + 1) * Q, :] + p["step_bias"])
        v.cums[0, rows, :] = step
        cum = sum3(lower, step * p["rate"])
        v.cums[1, rows, :] = cum
        lasts.append(cum[Q - 1 :, :])
    v.table[lay.z] = jnp.broadcast_to(jnp.exp(sum(lasts)), (8, LANES))
    return share_table(lay, v)


def kept_shapes(lay):
    r, w, m, n = lay.rows, lay.width, lay.model, lay.state
    return dict(
        nt=((m, r), BF),
        gate=((r, w), F32),
        xp=((r + 16, w), F32),
        sm=((r + 16, LANES), F32),
        ysd=((r, w), F32),
        sin=((lay.nb, n, w), F32),
        bc=((r, 2 * n), BF),
        sqt=((8 * lay.nb, Q), F32),
    )


def fwd_scratch(lay):
    r, w = lay.rows, lay.width
    dma = pltpu.SemaphoreType.DMA
    n_sem = 2 + 2 * (lay.parts - 1)
    return dict(
        xhs=VM((16, w), BF),
        xhr=VM((16, w), BF),
        shs=VM((16, LANES), BF),
        shr=VM((16, LANES), BF),
        bcg=VM((lay.parts, r // 2, LANES), BF),
        dpre=VM((8 * lay.nb, LANES), F32),
        sqb=VM((lay.parts, 8 * lay.nb, Q), F32),
        fsend=dma((n_sem,)),
        frecv=dma((n_sem,)),
    )


START_SMALL = ["conv_x", "bias_x", "gain_out", "rms", "conv_sm", "bias_sm"]
START_HEADS = ["step_bias", "decay", "skip"]


def start_ins():
    return ["tokens"] + [f"own{k}" for k in range(4)] + START_SMALL + START_HEADS


def start_outs(lay):
    r, w, m = lay.rows, lay.width, lay.model
    sds = jax.ShapeDtypeStruct
    out = {name: sds(*spec) for name, spec in kept_shapes(lay).items()}
    out.update(
        pk=sds((2, 16, w), F32),
        hid=sds((r, lay.share), F32),
        full=sds((r, m), BF),
        other0=sds((m, w), BF),
        other1=sds((m, w), BF),
        other2=sds((m, LANES), BF),
        other3=sds((w, m), BF),
    )
    return out


def start_scratch(lay):
    r, w, m, n = lay.rows, lay.width, lay.model, lay.state
    dma = pltpu.SemaphoreType.DMA
    peers = lay.parts - 1
    out = dict(
        resid=VM((r, m), BF),
        wg=VM((2, m, w), BF),
        wx=VM((2, m, w), BF),
        wsm=VM((2, m, LANES), BF),
        wo=VM((2, w, m), BF),
        expm=VM((LANES, w), BF),
        normed=VM((r, m), BF),
        xc=VM((r, w), F32),
        cums=VM((2, r, LANES), F32),
        go=VM((r, w), BF),
        local=VM((lay.nb, n, w), F32),
        tmp=VM((16, LANES), F32),
        part=VM((peers, r, lay.share), BF),
        own_part=VM((r, lay.share), F32),
        got=VM((peers, r, lay.share), BF),
        wsem=dma((5,)),
        psem=dma((9,)),
        vsem=dma((5,)),
        rs_send=dma((peers, lay.nb)),
        rs_recv=dma((peers, lay.nb)),
        ag_send=dma((peers, lay.nb)),
        ag_recv=dma((peers, lay.nb)),
    )
    out.update(fwd_scratch(lay))
    out.update(scan_scratch(lay, ["f_"]))
    return out


def pack(lay, v):
    c, w, heads, off = lay.c, lay.width, lay.heads, lay.off
    f = lambda ref: ref[...].astype(F32)
    v.tmp[...] = jnp.zeros(v.tmp.shape, F32)
    v.tmp[0:4, :off] = f(v.conv_sm)
    v.tmp[4:5, :off] = f(v.bias_sm)
    v.tmp[8:9, :heads] = v.step_bias[...]
    v.tmp[9:10, :heads] = -jnp.exp(v.decay[...])
    v.tmp[10:11, :heads] = v.skip[...]
    rows = v.tmp[8:16, :]
    groups = rows * 0.0
    for k in range(3):
        groups = groups + pltpu.roll(rows, off + k * GROUP, 1)
    v.pk[c] = jnp.zeros((16, w), F32)
    v.pk[c, 0:4, :] = f(v.conv_x)
    v.pk[c, 4:5, :] = f(v.bias_x)
    v.pk[c, 5:6, :] = f(v.gain_out)
    v.pk[c, 6:7, :] = expand(lay, v.expm[...], groups)[2:3, :]
    rms = f(v.rms)
    for k in range(lay.model // w):
        v.pk[c, 7 + k : 8 + k, :] = rms[:, k * w : (k + 1) * w]
    for k in range(5):
        v.pk[c, 9:10, k * LANES : (k + 1) * LANES] = v.tmp[k : k + 1, :]
    for k in range(2):
        v.pk[c, 10:11, k * LANES : (k + 1) * LANES] = groups[k : k + 1, :]


def start_kernel(lay, *refs):
    v = Names(start_ins() + list(start_outs(lay)) + list(start_scratch(lay)), refs)
    lay.place()
    c, q, nb = lay.c, lay.q, lay.nb
    both, own_w = (v.wg, v.wx, v.wsm, v.wo), (v.own0, v.own1, v.own2, v.own3)
    kept_w = (v.other0, v.other1, v.other2, v.other3)
    order = (2, 1, 0, 3)
    loads = [pltpu.make_async_copy(v.tokens.at[c], v.resid, v.wsem.at[4])]
    loads += [
        pltpu.make_async_copy(own_w[k], both[k].at[c], v.wsem.at[at]) for at, k in enumerate(order)
    ]
    for load in loads:
        load.start()
    v.expm[...] = expander(lay)
    pack(lay, v)
    meet(column_and_heads(lay))
    swaps = [remote(v.pk.at[c], v.pk.at[c], v.psem.at[4], v.vsem.at[4], lay.sibling())]
    swaps += [
        remote(own_w[k], both[k].at[c], v.psem.at[at], v.vsem.at[at], lay.sibling())
        for at, k in enumerate(order)
    ]
    for copy in swaps:
        copy.start()
    keeps = [
        pltpu.make_async_copy(both[k].at[1 - c], kept_w[k], v.psem.at[5 + at])
        for at, k in enumerate(order)
    ]
    wg, wx, wsm, wo = (ref.at[0] for ref in both)
    swaps[0].wait()
    loads[0].wait()

    def ready(at):
        loads[1 + at].wait()
        swaps[1 + at].wait()
        keeps[at].start()

    peers = lay.heads_peers()
    chunks = [[] for _ in range(nb)]

    def project():
        for k, target in peers + [(0, None)]:
            owner = lax.rem(q + k, lay.parts)
            cols = pl.ds(pl.multiple_of(owner * lay.share, LANES), lay.share)
            product = dot(v.go[...], wo[:, cols])
            if k == 0:
                v.own_part[...] = product
                continue
            v.part[k - 1] = product.astype(BF)
            for i in range(nb):
                rows = pl.ds(i * Q, Q)
                copy = remote(
                    v.part.at[k - 1, rows],
                    v.got.at[k - 1, rows],
                    v.rs_send.at[k - 1, i],
                    v.rs_recv.at[k - 1, i],
                    target,
                )
                copy.start()
                chunks[i].append(copy)

    p = params(lay, v.pk, 0)
    forward(lay, v, p, v.resid, (wsm, wx, wg), ready, project)
    cols = pl.ds(pl.multiple_of(q * lay.share, LANES), lay.share)
    given = []
    for i in range(nb):
        rows = pl.ds(i * Q, Q)
        for copy in chunks[i]:
            copy.wait()
        total = v.own_part[rows, :]
        for k, _ in peers:
            total = total + v.got[k - 1, rows, :].astype(F32)
        row = v.sqt[8 * i : 8 * i + 1, :]
        value = v.resid[rows, cols].astype(F32) + to_col(lax.rsqrt(row / lay.inner + EPS)) * total
        v.hid[rows, :] = value
        v.full[rows, cols] = value.astype(BF)
        for k, target in peers:
            copy = remote(
                v.full.at[rows, cols],
                v.full.at[rows, cols],
                v.ag_send.at[k - 1, i],
                v.ag_recv.at[k - 1, i],
                target,
            )
            copy.start()
            given.append(copy)
    for copy in given + keeps:
        copy.wait()


def start_layer(lay, *args):
    outs, scratch = start_outs(lay), start_scratch(lay)
    vmem, hbm = pl.BlockSpec(memory_space=VM), pl.BlockSpec(memory_space=HB)
    got = pl.pallas_call(
        functools.partial(start_kernel, lay),
        out_shape=tuple(outs.values()),
        in_specs=[hbm] * 5 + [vmem] * (len(args) - 5),
        out_specs=tuple([vmem] * (len(outs) - 4) + [hbm] * 4),
        scratch_shapes=list(scratch.values()),
        compiler_params=pltpu.CompilerParams(
            collective_id=1, has_side_effects=True, vmem_limit_bytes=58 << 20
        ),
        name="mixer_start",
    )(*args)
    return Names(list(outs), got)


EARLIER = ["prev_x", "prev_s", "done_o", "done_g", "done_x", "small", "hid0", "hid1", "gt1"]
X_EARLY = 2


def staged(lay):
    r, w, m = lay.rows, lay.width, lay.model
    rest = m // 2 - m // 2 // N_X * X_EARLY
    out = dict(prev_x=((rest, w), BF), prev_s=((m // 2, LANES), BF), pk=((2, 16, w), F32))
    kept = kept_shapes(lay)
    for name in ("sm", "xp", "ysd", "gate", "sqt"):
        out[name] = kept[name]
    out["up"] = ((r, m), BF)
    for name in ("nt", "bc", "sin"):
        out[name] = kept[name]
    out.update(done_o=((w // 2, m), BF), done_g=((m // 2, w), BF))
    out.update(done_x=((m // 2 // N_X * X_EARLY, w), BF), small=((16, w), F32))
    return out


def back_ins(lay, more):
    weights = [f"own{k}" for k in range(4)] + [f"other{k}" for k in range(4)]
    if more:
        return ["from_" + name for name in staged(lay)] + ["tokens"] + weights + EARLIER[-3:]
    return ["cotangent", "resid"] + weights + ["pk"]


def back_outs(lay, late, gather, more):
    r, w, m = lay.rows, lay.width, lay.model
    sds = jax.ShapeDtypeStruct
    out = dict(gt=sds((r, lay.share), F32))
    if more:
        out["total"] = sds((16 + 8 * lay.parts, w), F32)
    else:
        out.update(
            sum_o=sds((w // 2, m), BF),
            sum_g=sds((m // 2, w), BF),
            sum_x=sds((m // 2 // N_X * X_EARLY, w), BF),
            rest_x=sds((m // 2 - m // 2 // N_X * X_EARLY, w), BF),
            own_s=sds((m // 2, LANES), BF),
            psm=sds((16, w), F32),
        )
    if gather:
        out["full"] = sds((r, m), BF)
    if late:
        out["hid"] = sds((r, lay.share), F32)
    if more:
        out.update(
            fin_o=sds((w, m), BF),
            fin_g=sds((m, w), BF),
            fin_x=sds((m, w), BF),
            fin_s=sds((m, LANES), BF),
            got_hid=sds((r, lay.share), F32),
            got_gt=sds((r, lay.share), F32),
        )
    return out


N_OUT = N_GATE = N_X = 4


def back_scratch(lay, late, gather, more):
    r, w, m, n, nb = lay.rows, lay.width, lay.model, lay.state, lay.nb
    dma = pltpu.SemaphoreType.DMA
    peers = lay.parts - 1
    n_sem = 2 * peers + 2 + 4 + peers
    n_seq = N_OUT + N_GATE + (2 * (N_X + 1) - X_EARLY if more else X_EARLY)
    out = dict(
        wg=VM((m, w), BF),
        wx=VM((m, w), BF),
        wsm=VM((m, LANES), BF),
        wo=VM((w, m), BF),
        expm=VM((LANES, w), BF),
        xc=VM((r, w), F32),
        dy=VM((r, w), F32),
        dx=VM((r, w), F32),
        cums=VM((2, r, LANES), F32),
        rcs=VM((r, LANES), F32),
        lowg=VM((r, w), BF),
        lowx=VM((r, w), BF),
        lowsm=VM((r, LANES), BF),
        no=VM((r, w), BF),
        rsb=VM((lay.parts, 8 * nb, Q), F32),
        lamloc=VM((nb, n, w), F32),
        dsuf=VM((8 * nb, LANES), F32),
        dbc=VM((r, 2 * n), F32),
        dbs=VM((lay.parts, r // 2, LANES), BF),
        dbr=VM((peers, r // 2, LANES), BF),
        xdp=VM((r + 16, w), F32),
        smdp=VM((r + 16, LANES), F32),
        hxs=VM((16, w), BF),
        hxr=VM((16, w), BF),
        hss=VM((16, LANES), BF),
        hsr=VM((16, LANES), BF),
        dsp=VM((r, LANES), F32),
        gr_g=VM((m // 2, w), BF),
        gr_x=VM((m // 2, w), BF),
        gs_o=VM((w // 2, m), BF),
        gr_o=VM((w // 2, m), BF),
        gr_s=VM((m // 2, LANES), BF),
        rdacc=VM((r, LANES), F32),
        acch=VM((8, LANES), F32),
        own_o=VM((w // 2, m), BF),
        own_g=VM((m // 2, w), BF),
        in_o=VM((w // 2, m), BF),
        in_g=VM((m // 2, w), BF),
        in_x=VM((m // 2, w), BF),
        dnp=VM((lay.parts, r, lay.share), BF),
        got=VM((peers, r, lay.share), BF),
        rd2=VM((8 * nb, Q), F32),
        got_rows=VM((peers, 8 * nb, Q), F32),
        gains=VM((8, m), F32),
        wsem=dma((5,)),
        ssem=dma((n_sem,)),
        rsem=dma((n_sem,)),
        rs_send=dma((peers, nb)),
        rs_recv=dma((peers, nb)),
        seq1=dma((n_seq,)),
        seq2=dma((n_seq,)),
        seq3=dma((n_seq,)),
        seq4=dma((n_seq,)),
    )
    if gather:
        out.update(ag_send=dma((peers, nb)), ag_recv=dma((peers, nb)))
    out["own_x"] = VM((m // 2, w), BF)
    if more:
        for kind in ("in_s", "in_ps", "own_s", "sum_s", "sum_ps"):
            out[kind] = VM((m // 2, LANES), BF)
        for kind in ("sum_x", "sum_g"):
            out[kind] = VM((m // 2, w), BF)
        for kind in ("in_px", "sum_px"):
            out[kind] = VM((m // 2 - m // 2 // N_X * X_EARLY, w), BF)
        column = 2 * lay.seqs
        out.update(
            sum_o=VM((w // 2, m), BF),
            psm=VM((16, w), F32),
            slots=VM((column, 16, w), F32),
            rest_rows=VM((lay.parts, 8, w), F32),
            fin_sem=dma((3, n_seq + 3)),
            pair_sem=dma((2, 2)),
            slot_sem=dma((2, column - 1)),
            part_sem=dma((2, peers)),
        )
        out["resid"] = VM((r, m), BF)
        out.update({name: VM(*spec) for name, spec in staged(lay).items()})
        out["stage_sem"] = dma((len(staged(lay)),))
    out.update(scan_scratch(lay, ["b_"] if more else ["f_", "b_"]))
    if late:
        out.update(
                late_got=VM((peers, r, lay.share), BF),
            late_send=dma((peers,)),
            late_recv=dma((peers,)),
            up=VM((r, m), BF),
        )
        out.update({name: VM(*spec) for name, spec in kept_shapes(lay).items()})
        out.update(fwd_scratch(lay))
    return out


def bwd_kernel(lay, layer, late, gather, more, *refs):
    outs, scratch = back_outs(lay, late, gather, more), back_scratch(lay, late, gather, more)
    v = Names(back_ins(lay, more) + list(outs) + list(scratch), refs)
    lay.place()
    c, z, q = lay.c, lay.z, lay.q
    nb, w, n, m = lay.nb, lay.width, lay.state, lay.model
    half = lay.rows // 2
    own_w, other_w = (v.own0, v.own1, v.own2, v.own3), (v.other0, v.other1, v.other2, v.other3)
    loads = [
        Load(own_w[k], other_w[k], (v.wg, v.wx, v.wsm, v.wo)[k], v.wsem.at[at], c == layer)
        for at, k in enumerate((3, 0, 1, 2) if more else (2, 1, 0, 3))
    ]
    stages = {}
    if more:
        for k, name in enumerate(staged(lay)):
            src, dst = getattr(v, "from_" + name), getattr(v, name)
            stages[name] = pltpu.make_async_copy(src, dst, v.stage_sem.at[k])
            stages[name].start()
        rows_in = pltpu.make_async_copy(v.tokens.at[c], v.resid, v.wsem.at[4])
    else:
        rows_in = pltpu.make_async_copy(v.cotangent.at[c], v.up, v.wsem.at[4])
    for load in loads + [rows_in]:
        load.start()
    meet(column_and_heads(lay))
    peers = lay.heads_peers()
    counter = iter(range(64))

    def send(src, dst, target):
        at = next(counter)
        copy = remote(src, dst, v.ssem.at[at], v.rsem.at[at], target)
        copy.start()
        return copy

    out_pieces = pieces_of(v.own_o, v.in_o, v.sum_o, N_OUT)
    gate_pieces = pieces_of(v.own_g, v.in_g, v.sum_g, N_GATE)
    finals = []

    def plan_settling(ref, fin, of, rows, skipped=0):
        size = ref.shape[0] if rows is None else rows.size
        offset = skipped + (0 if rows is None else rows.start)
        at = len(finals)
        into = fin.at[pl.ds(pl.multiple_of(c * (fin.shape[0] // 2) + offset, 16), size)]
        src = ref if rows is None else ref.at[rows]
        here = pltpu.make_async_copy(src, into, v.fin_sem.at[0, at])
        there = remote(src, into, v.fin_sem.at[1, at], v.fin_sem.at[2, at], lay.sibling())
        finals.append((of, here, there))

    def settle(at):
        of, here, there = finals[at]
        pl.when(c == of)(here.start)
        pl.when(c != of)(there.start)

    if more:
        kinds = [(pieces_of(v.prev_x, v.in_px, v.sum_px, N_X - X_EARLY), v.fin_x, 1)]
        kinds += [(pieces_of(v.prev_s, v.in_ps, v.sum_ps, 1), v.fin_s, 1)]
        kinds += [(out_pieces, v.fin_o, 0), (gate_pieces, v.fin_g, 0)]
        kinds += [(pieces_of(v.own_x, v.in_x, v.sum_x, N_X), v.fin_x, 0)]
        kinds += [(pieces_of(v.own_s, v.in_s, v.sum_s, 1), v.fin_s, 0)]
        listed = [(piece, fin, of) for pieces, fin, of in kinds for piece in pieces]

        for (_, _, result, rows), fin, of in listed:
            skipped = m // 2 // N_X * X_EARLY if result is v.sum_px else 0
            plan_settling(result, fin, of, rows, skipped)
        done = settle
        plan_settling(v.done_o, v.fin_o, 1, None)
        plan_settling(v.done_g, v.fin_g, 1, None)
        plan_settling(v.done_x, v.fin_x, 1, None)
        pairs = [
            [
                remote(src, dst, v.pair_sem.at[0, k], v.pair_sem.at[1, k], lay.sibling())
                for src in srcs
            ]
            for k, (dst, srcs) in enumerate(
                ((v.got_hid, (v.hid1, v.hid0)), (v.got_gt, (v.gt1, v.gt)))
            )
        ]
        pl.when(c == 0)(pairs[0][0].start)
        pl.when(c == 1)(pairs[0][1].start)
        pl.when(c == 0)(pairs[1][0].start)
    else:
        x_pieces = pieces_of(v.own_x, v.in_x, v.sum_x, N_X)[:X_EARLY]
        listed = [(piece,) for piece in out_pieces + gate_pieces + x_pieces]
        done = None
    pump = Pump(
        SeqSum(lay, [entry[0] for entry in listed], (v.seq1, v.seq2, v.seq3, v.seq4)), done
    )
    tick = pump.tick
    scan = Scan(lay, False, v.expm, scan_refs(v, "b_"))
    if more:
        for name in ("prev_x", "prev_s"):
            stages.pop(name).wait()
        pump.ready += N_X - X_EARLY + 1
        pump.feed()
        for stage in stages.values():
            stage.wait()
        for at in range(len(listed), len(finals)):
            settle(at)

    p = params(lay, v.pk, layer)
    v.expm[...] = expander(lay)
    expm = v.expm
    v.psm[...] = jnp.zeros(v.psm.shape, F32)
    v.acch[...] = jnp.zeros(v.acch.shape, F32)
    lower, upper, strict = tri("lower"), tri("upper"), tri("strict")
    col_n = 256

    def cols_at(j, size=col_n):
        return pl.ds(pl.multiple_of(j * size, LANES), size)

    def tile(i):
        return pl.ds(pl.multiple_of(8 * i, 8), 8)

    def weight_grad(left, low, theirs, got, own):
        width = low.shape[1]
        step_n = min(width, col_n)
        for side, into in ((1 - c, theirs), (c, own)):
            rows = left(side)

            @pl.loop(0, width // step_n)
            def _(j):
                at = cols_at(j, step_n)
                into[:, at] = dot(rows, low[:, at]).astype(BF)

            if into is theirs:
                copy = send(theirs, got, lay.sibling())
        return copy

    def pair_sum(copy, own, got):
        copy.wait()
        own[...] = own[...] + got[...]

    def normed_half(side):
        return v.nt[pl.ds(pl.multiple_of(side * (m // 2), 16), m // 2), :]

    def out_half(side):
        return jnp.transpose(v.no[:, pl.ds(pl.multiple_of(side * (w // 2), LANES), w // 2)])

    late_sums = []

    def project():
        for k in range(lay.parts):
            cols = slice(k * lay.share, (k + 1) * lay.share)
            v.dnp[k] = dot(v.go[...], v.wo[:, cols]).astype(BF)

    def out_grad():
        @pl.loop(0, w // col_n)
        def _(j):
            v.dy[:, cols_at(j)] = dot(v.up[...], v.wo[cols_at(j), :], NT)

    if more:
        tables = run_decays(lay, v, p)
    else:
        v.normed, v.go, v.local = v.full, v.lowx, v.lamloc
        weights = (v.wsm, v.wx, v.wg)

        def meanwhile():
            loads[3].wait()
            rows_in.wait()
            out_grad()

        forward(lay, v, p, v.resid, weights, lambda at: loads[at].wait(), project, meanwhile)
        tables = []

    @pl.loop(0, nb)
    def _(i):
        if more:
            pre = conv_pre(conv_cat(v.xp, i), p["conv_x"], p["bias_x"])
            v.xc[block(i), :] = pre * jax.nn.sigmoid(pre)
        x = v.xc[block(i), :]
        g = v.gate[block(i), :]
        gated = (v.ysd[block(i), :] + p["skip"] * x) * (g * jax.nn.sigmoid(g))
        inv = to_col(lax.rsqrt(v.sqt[tile(i), :][:1, :] / lay.inner + EPS))
        v.no[block(i), :] = (gated * inv * p["gain_out"]).astype(BF)

    if more:
        rows_in.wait()
        tick()
    copy_o = weight_grad(out_half, v.up, v.gs_o, v.gr_o, v.own_o)
    if more:
        loads[0].wait()
        out_grad()

    @pl.loop(0, nb)
    def _(i):
        g = v.gate[block(i), :]
        gated = (v.ysd[block(i), :] + p["skip"] * v.xc[block(i), :]) * (g * jax.nn.sigmoid(g))
        row = to_row(v.dy[block(i), :] * p["gain_out"] * gated)
        v.rsb[q, tile(i), :] = jnp.broadcast_to(row, (8, Q))

    row_sends = [send(v.rsb.at[q], v.rsb.at[q], target) for _, target in peers]
    pair_sum(copy_o, v.own_o, v.gr_o)
    pump.ready += N_OUT
    if more:
        tick()
    pump.feed()
    for copy in row_sends:
        copy.wait()
    if late:
        for k, target in peers:
            copy = remote(
                v.dnp.at[lax.rem(q + k, lay.parts)],
                v.late_got.at[k - 1],
                v.late_send.at[k - 1],
                v.late_recv.at[k - 1],
                target,
            )
            copy.start()
            late_sums.append(copy)
    @pl.loop(0, nb)
    def _(i):
        rd = v.rsb[0, tile(i), :]
        for k in range(1, lay.parts):
            rd = rd + v.rsb[k, tile(i), :]
        inv = to_col(lax.rsqrt(v.sqt[tile(i), :][:1, :] / lay.inner + EPS))
        rdc = to_col(rd[:1, :])
        g, x, d = v.gate[block(i), :], v.xc[block(i), :], v.dy[block(i), :]
        sg = jax.nn.sigmoid(g)
        act = g * sg
        mixed = v.ysd[block(i), :] + p["skip"] * x
        gated = mixed * act
        v.psm[5:6, :] += jnp.sum(d * (gated * inv), axis=0, keepdims=True)
        dgated = inv * p["gain_out"] * d - gated * (inv * inv * inv * rdc / lay.inner)
        dmix = dgated * act
        v.lowg[block(i), :] = (dgated * mixed * (sg * (1.0 + g * (1.0 - sg)))).astype(BF)
        v.psm[8:9, :] += jnp.sum(dmix * x, axis=0, keepdims=True)
        v.dy[block(i), :] = dmix

    lam = jnp.zeros((n, w), F32)
    total = jnp.zeros((1, LANES), F32)
    for i in reversed(range(nb)):
        rows = pl.ds(i * Q, Q)
        cum = v.cums[1, rows, :]
        last = cum[Q - 1 :, :]
        v.lamloc[i] = lam
        v.dsuf[8 * i : 8 * (i + 1), :] = jnp.broadcast_to(total, (8, LANES))
        faded = (expand(lay, expm[...], jnp.exp(cum)) * v.dy[rows, :]).astype(BF)
        dec = expand(lay, expm[...], jnp.broadcast_to(jnp.exp(last), (8, LANES)))[:1, :]
        lam = lam * dec + dot(v.bc[rows, n:], faded, TN)
        total = total + last
    if more:
        tick()
    v.own_state[...] = lam
    for copy in tables:
        copy.wait()
    scan.start()

    copy_g = weight_grad(
        normed_half, v.lowg, v.wo.at[:, :w], v.gr_g, v.own_g
    )
    pair_sum(copy_g, v.own_g, v.gr_g)
    pump.ready += N_GATE
    tick()

    in_loop = pump.later() if more else None

    @pl.loop(0, nb)
    def _(i):
        if scan.steps > 1:
            pl.when(i == 2)(functools.partial(scan.advance, 0))
        if more:
            pl.when(i == 3)(in_loop)
        causal = iota((Q, Q), 0) >= iota((Q, Q), 1)
        cum = v.cums[1, block(i), :]
        cum_t = jnp.transpose(cum)
        b_rows, c_rows = v.bc[block(i), :n], v.bc[block(i), n:]
        scores = dot(c_rows, b_rows, NT)
        stepped = (v.xc[block(i), :] * expand(lay, expm[...], v.cums[0, block(i), :])).astype(BF)
        grad = v.dy[block(i), :]
        low = grad.astype(BF)
        dscores = jnp.zeros((Q, Q), F32)
        for pair in range(lay.heads // 2):
            cols = slice(pair * LANES, (pair + 1) * LANES)
            fades = [decay_tile(cum, cum_t, lay.off + 2 * pair + e, causal) for e in range(2)]
            mixes = [(scores * fade).astype(BF) for fade in fades]
            xl, xr = halves(stepped[:, cols])
            dl, dr = halves(low[:, cols])
            dmix = dot(low[:, cols], jnp.concatenate([xl, xr], axis=0), NT)
            dscores = dscores + dmix[:, :Q] * fades[0] + dmix[:, Q:] * fades[1]
            v.dx[block(i), cols] = dot(
                jnp.concatenate(mixes, axis=0), jnp.concatenate([dl, dr], axis=0), TN
            )
        diff = low.astype(F32) * v.ysd[block(i), :] - stepped.astype(F32) * v.dx[block(i), :]
        v.rcs[block(i), :] = sum3(upper, head_sum(expm[...], diff))
        faded = (expand(lay, expm[...], jnp.exp(cum)) * grad).astype(BF)
        dsc = dscores.astype(BF)
        v.dbc[block(i), :n] = dot(dsc, c_rows, TN)
        v.dbc[block(i), n:] = dot(dsc, b_rows) + dot2(faded, v.sin[i], NT)

    for step in range(1 if scan.steps > 1 else 0, scan.steps):
        scan.advance(step)
    scan.hand_over()
    tick()
    scan.result()
    carry = v.enter[...]
    at = next(counter)
    halo_x = remote(v.hxs, v.hxr, v.ssem.at[at], v.rsem.at[at], lay.prev_run())

    in_loop = pump.later()

    @pl.loop(0, nb)
    def _(i):
        pl.when(i == 2)(in_loop)
        cat = conv_cat(v.xp, i)
        pre = conv_pre(cat, p["conv_x"], p["bias_x"])
        x = v.xc[block(i), :]
        step, cum = v.cums[0, block(i), :], v.cums[1, block(i), :]
        last = cum[Q - 1 :, :]
        fade = expand(lay, expm[...], jnp.exp(last - cum))
        step_w = expand(lay, expm[...], step)
        gone = jnp.exp(v.dsuf[tile(i), :])
        lam_out = v.lamloc[i] + expand(lay, expm[...], gone)[:1, :] * carry
        lam_b = dot2(v.bc[block(i), :n], lam_out)
        xw = x * step_w * fade
        v.dbc[block(i), :n] += dot2(xw.astype(BF), lam_out, NT)
        within = jnp.sum(lam_out * v.sin[i], axis=0, keepdims=True)
        kept = head_sum(expm[...], jnp.broadcast_to(within, (8, w)))[:1, :] * jnp.exp(last)
        dxt = v.dx[block(i), :] + fade * lam_b
        g = v.rcs[block(i), :] + sum3(strict, head_sum(expm[...], xw * lam_b)) + kept
        dstep = head_sum(expm[...], x * dxt) + p["rate"] * g
        v.acch[1:2, :] += jnp.sum(step * g, axis=0, keepdims=True)
        dpre_step = dstep * jax.nn.sigmoid(v.sm[block(i, base=16), :] + p["step_bias"])
        v.acch[0:1, :] += jnp.sum(dpre_step, axis=0, keepdims=True)
        v.dsp[block(i), :] = dpre_step
        d_xin = step_w * dxt + p["skip"] * v.dy[block(i), :]
        dpre = d_xin * silu_grad(pre)
        v.xdp[block(i), :] = dpre
        for k in range(4):
            v.psm[k : k + 1, :] += jnp.sum(dpre * cat[5 + k : 5 + k + Q, :], axis=0, keepdims=True)
        v.psm[4:5, :] += jnp.sum(dpre, axis=0, keepdims=True)

        @pl.when(i == 0)
        def _():
            v.hxs[...] = v.xdp[:16, :].astype(BF)
            halo_x.start()

    sel_top, sel_bottom = selectors(lay)
    pieces = dot(v.dbc[:half, :].astype(BF), sel_top, NT) + dot(
        v.dbc[half:, :].astype(BF), sel_bottom, NT
    )
    for k in range(lay.parts):
        v.dbs[k] = pieces[:, k * LANES : (k + 1) * LANES].astype(BF)
    bc_sends = [
        send(v.dbs.at[lax.rem(q + k, lay.parts)], v.dbr.at[k - 1], target) for k, target in peers
    ]
    inside = jnp.where((c == 1) & (z == lay.seqs - 1), 0.0, 1.0)
    tick()
    if late:
        for copy in late_sums:
            copy.wait()
        cols = pl.ds(pl.multiple_of(q * lay.share, LANES), lay.share)
        for i in range(nb):
            rows = pl.ds(i * Q, Q)
            value = v.dnp[q, rows, :].astype(F32)
            for k, _ in peers:
                value = value + v.late_got[k - 1, rows, :].astype(F32)
            inv = to_col(lax.rsqrt(v.sqt[8 * i : 8 * i + 1, :] / lay.inner + EPS))
            v.hid[rows, :] = v.resid[rows, cols].astype(F32) + inv * value
    halo_x.wait()
    v.xdp[lay.rows :, :] = v.hxr[...].astype(F32) * inside

    @pl.loop(0, nb)
    def _(i):
        cat = v.xdp[pl.ds(pl.multiple_of(i * Q, 8), Q + 8), :]
        grad = jnp.zeros((Q, w), F32)
        for k in range(4):
            grad = grad + p["conv_x"][k : k + 1, :] * cat[3 - k : 3 - k + Q, :]
        v.lowx[block(i), :] = grad.astype(BF)

    for load in loads[1:] if more else []:
        load.wait()
    copy_x = weight_grad(normed_half, v.lowx, v.wo.at[:, w:], v.gr_x, v.own_x)
    tick()

    for copy in bc_sends:
        copy.wait()
    summed = v.dbs[q].astype(F32)
    for k in range(1, lay.parts):
        summed = summed + v.dbr[k - 1].astype(F32)
    for i in range(nb):
        rows = pl.ds(i * Q, Q)
        if i < nb // 2:
            d_conv = summed[i * Q : (i + 1) * Q, :]
        else:
            d_conv = pltpu.roll(summed[i * Q - half : (i + 1) * Q - half, :], LANES // 2, 1)
        cat = conv_cat(v.sm, i)
        pre = conv_pre(cat, p["conv_sm"], p["bias_sm"])
        valid = iota((Q, LANES), 1) < lay.off
        dpre = jnp.where(valid, d_conv * silu_grad(pre), 0.0)
        v.smdp[rows, :] = dpre
        for k in range(4):
            v.psm[7:8, k * LANES : (k + 1) * LANES] += jnp.sum(
                dpre * cat[5 + k : 5 + k + Q, :], axis=0, keepdims=True
            )
        v.psm[7:8, 4 * LANES : 5 * LANES] += jnp.sum(dpre, axis=0, keepdims=True)
    v.hss[...] = v.smdp[:16, :].astype(BF)
    halo_s = send(v.hss, v.hsr, lay.prev_run())
    v.psm[6:7, :LANES] = head_sum(expm[...], v.psm[8:9, :])
    v.psm[6:7, LANES : 2 * LANES] = v.acch[0:1, :]
    v.psm[6:7, 2 * LANES : 3 * LANES] = v.acch[1:2, :] * p["rate"]
    pair_sum(copy_x, v.own_x, v.gr_x)
    halo_s.wait()
    v.smdp[lay.rows :, :] = v.hsr[...].astype(F32) * inside
    for i in range(nb):
        rows = pl.ds(i * Q, Q)
        cat = v.smdp[i * Q : (i + 1) * Q + 8, :]
        grad = jnp.zeros((Q, LANES), F32)
        for k in range(4):
            grad = grad + p["conv_sm"][k : k + 1, :] * cat[3 - k : 3 - k + Q, :]
        lane = iota((Q, LANES), 1)
        first = jnp.where(lane < lay.off + GROUP, v.dsp[rows, :], 0.0)
        v.lowsm[rows, :] = jnp.where(lane < lay.off, grad, first).astype(BF)
    copy_s = weight_grad(normed_half, v.lowsm, v.wo.at[:, :LANES], v.gr_s, v.own_s)
    pump.ready += N_X if more else X_EARLY
    if not more:
        v.rest_x[...] = v.own_x[m // 2 // N_X * X_EARLY :, :]
    tick()

    v.rdacc[...] = jnp.zeros(v.rdacc.shape, F32)
    v.gains[...] = jnp.broadcast_to(p["gain"], (8, m))
    spread = (v.full, v.ag_send, v.ag_recv) if gather else ()
    head_sum_of = HeadSum(lay, v.dnp, v.got, v.rs_send, v.rs_recv, *spread)
    for k in (3, 1, 2, 0):
        cols = head_sum_of.cols(k)
        grad = dot(v.lowg[...], v.wg[cols, :], NT) + dot(v.lowx[...], v.wx[cols, :], NT)
        grad = grad + dot(v.lowsm[...], v.wsm[cols, :], NT)
        v.dnp[k] = grad.astype(BF)
        v.rdacc[...] += fold(grad * v.gains[:1, cols] * v.resid[:, cols].astype(F32))
        for i in range(nb):
            if k == head_sum_of.near(i):
                head_sum_of.first(i)
    for i in range(nb):
        row = to_row(v.rdacc[i * Q : (i + 1) * Q, :])
        v.rd2[8 * i : 8 * (i + 1), :] = jnp.broadcast_to(row, (8, Q))
    rd_sends = [send(v.rd2, v.got_rows.at[k - 1], target) for k, target in peers]
    pair_sum(copy_s, v.own_s, v.gr_s)
    if more:
        pump.ready += 1
    cols = pl.ds(pl.multiple_of(q * lay.share, LANES), lay.share)
    own_gain = v.gains[:1, cols]
    tick()
    for copy in rd_sends:
        copy.wait()
    inner = v.rd2[...]
    for k, _ in peers:
        inner = inner + v.got_rows[k - 1]
    rms_sum = jnp.zeros((1, lay.share), F32)
    for i in range(nb + 2):
        if i < nb:
            head_sum_of.second(i)
        if 1 <= i <= nb:
            at = i - 1
            rows = pl.ds(at * Q, Q)
            total = head_sum_of.total(at)
            start = v.resid[rows, cols].astype(F32)
            x = v.resid[rows, :].astype(F32)
            scale = lax.rsqrt(jnp.mean(x * x, axis=1, keepdims=True) + EPS)
            value = (
                v.up[rows, cols].astype(F32)
                + scale * (own_gain * total)
                - start * (scale * scale * scale * to_col(inner[8 * at : 8 * at + 1, :] / m))
            )
            rms_sum = rms_sum + jnp.sum(total * start * scale, axis=0, keepdims=True)
            v.gt[rows, :] = value
            if gather:
                v.full[rows, cols] = value.astype(BF)
                head_sum_of.give(at)
        if i >= 2 and gather:
            head_sum_of.relay(i - 2)
        tick()
    v.psm[8:9, :] = jnp.zeros((1, w), F32)
    v.psm[8:9, : lay.share] = rms_sum
    if more:
        pl.when(c == 1)(pairs[1][1].start)
        column = [(a, b) for a in range(2) for b in range(lay.seqs) if a or b]
        own_slot = c * lay.seqs + z
        smalls = []
        for at, (a, b) in enumerate(column):
            to_c, to_z = (c + a) % 2, lax.rem(z + b, lay.seqs)
            to = (to_c, to_z, q)
            pair = [
                remote(src, v.slots.at[own_slot], v.slot_sem.at[0, at], v.slot_sem.at[1, at], to)
                for src in (v.psm, v.small)
            ]
            pl.when(to_c == 0)(pair[0].start)
            pl.when(to_c == 1)(pair[1].start)
            smalls.append(pair[0])
        v.slots[own_slot] = jnp.where(c == 0, v.psm[...], v.small[...])
        tick()
        for copy in smalls:
            copy.wait()
        value = v.slots[0]
        for k in range(1, 2 * lay.seqs):
            value = value + v.slots[k]
        v.total[:16, :] = value
        v.rest_rows[q] = value[8:16, :]
        parts = []
        for k, target in peers:
            copy = remote(
                v.rest_rows.at[q],
                v.rest_rows.at[q],
                v.part_sem.at[0, k - 1],
                v.part_sem.at[1, k - 1],
                target,
            )
            copy.start()
            parts.append(copy)
        tick()
        for copy in parts:
            copy.wait()
        for k in range(lay.parts):
            v.total[16 + 8 * k : 24 + 8 * k, :] = v.rest_rows[k]
    pump.finish()
    if gather:
        head_sum_of.finish()
    if more:
        for of, here, there in finals:
            pl.when(c == of)(here.wait)
            pl.when(c == of)(there.wait_recv)
            pl.when(c != of)(there.wait_send)
        for pair in pairs:
            pair[0].wait()


def bwd_layer(lay, layer, args, more):
    late = gather = not more
    outs, scratch = back_outs(lay, late, gather, more), back_scratch(lay, late, gather, more)
    vmem, hbm = pl.BlockSpec(memory_space=VM), pl.BlockSpec(memory_space=HB)
    names = back_ins(lay, more)
    specs = [vmem if name in ("resid", "pk") else hbm for name in names]
    out_specs = [vmem] * len(outs)
    if more:
        out_specs[-6:] = [hbm] * 6
    got = pl.pallas_call(
        functools.partial(bwd_kernel, lay, layer, late, gather, more),
        out_shape=tuple(outs.values()),
        in_specs=specs,
        out_specs=tuple(out_specs),
        scratch_shapes=list(scratch.values()),
        compiler_params=pltpu.CompilerParams(
            collective_id=5 + layer, has_side_effects=True, vmem_limit_bytes=63 << 20
        ),
        name=f"mixer_backward_{layer}",
    )(*(args[name.removeprefix("from_")] for name in names))
    return Names(list(outs), got)


def on_device(
    mesh_shape, tokens, cotangent, rms_gain, proj_gate, proj_x, proj_bc, proj_step, conv_x, conv_x_bias,
    conv_bc, conv_bc_bias, step_bias, decay_log, skip_gain, norm_gain, proj_out,
):
    pieces, rows, model = tokens.shape
    width, heads, local_state = proj_x.shape[2], proj_step.shape[2], proj_bc.shape[3]
    lay = Lay(mesh_shape, rows, width, model, heads, local_state)
    section = lax.axis_index("section")
    group = jnp.pad(proj_step[0], ((0, 0), (0, GROUP - heads)))
    w_small = jnp.concatenate(
        [
            proj_bc[0].reshape(model, lay.off),
            group,
            group,
            group,
            jnp.zeros((model, LANES - lay.off - 3 * GROUP), BF),
        ],
        axis=1,
    )
    taps = conv_x.shape[1]
    own = (proj_gate[0], proj_x[0], w_small, proj_out[0])
    first = start_layer(
        lay,
        tokens,
        *own,
        conv_x[0],
        conv_x_bias,
        norm_gain,
        rms_gain,
        conv_bc.reshape(taps, lay.off),
        conv_bc_bias.reshape(1, lay.off),
        step_bias,
        decay_log,
        skip_gain,
    )
    args = dict(vars(first), tokens=tokens, cotangent=cotangent, resid=first.full)
    args.update({f"own{k}": weight for k, weight in enumerate(own)})
    one = bwd_layer(lay, 1, args, False)
    args.update(up=one.full, prev_x=one.rest_x, prev_s=one.own_s, done_o=one.sum_o, done_g=one.sum_g)
    args.update(done_x=one.sum_x, small=one.psm, hid0=first.hid, hid1=one.hid, gt1=one.gt)
    zero = bwd_layer(lay, 0, args, True)
    at_zero = section == 0

    def both_pieces(ours0, ours1, theirs):
        ours = jnp.where(at_zero, ours0, ours1)
        return jnp.stack([jnp.where(at_zero, ours, theirs), jnp.where(at_zero, theirs, ours)])[None]

    hid = both_pieces(first.hid, one.hid, zero.got_hid)
    gt = both_pieces(zero.gt, one.gt, zero.got_gt)
    g_gate, g_x, g_out, g_sm = (
        a.astype(F32)[None] for a in (zero.fin_g, zero.fin_x, zero.fin_o, zero.fin_s)
    )
    total = zero.total
    lane = lay.off
    rms_all = total[16:].reshape(lay.parts, 8, width)[:, 0, : lay.share].reshape(1, model)
    conv_small = total[7].reshape(-1, LANES)[:5, : lay.off]

    def head_row(k):
        return total[6, k * LANES + lane : k * LANES + lane + heads][None]

    return (
        hid,
        gt,
        rms_all,
        g_gate,
        g_x,
        g_sm[:, :, : lay.off].reshape(1, model, 2, local_state),
        g_sm[:, :, lane : lane + heads],
        total[None, 0:4],
        total[4:5],
        conv_small[:4].reshape(1, 4, 2, local_state),
        conv_small[4].reshape(1, 2, local_state),
        head_row(1),
        head_row(2),
        head_row(0),
        total[5:6],
        g_out,
    )


def solution(mesh):
    placed = (
        P(None, "seq", None),
        P(None, "seq", None),
        P("section", None),
        P("section", None, "head"),
        P("section", None, "head"),
        P("section", None, None, "head"),
        P("section", None, "head"),
        P("section", None, "head"),
        P("section", "head"),
        P("section", None, None, "head"),
        P("section", None, "head"),
        P("section", "head"),
        P("section", "head"),
        P("section", "head"),
        P("section", "head"),
        P("section", "head", None),
    )
    back = (P("section", None, "seq", "head"),) * 2 + placed[2:]
    shape = tuple(mesh.shape[name] for name in ("section", "seq", "head"))
    return jax.shard_map(
        functools.partial(on_device, shape),
        mesh=mesh,
        in_specs=placed,
        out_specs=back,
        check_vma=False,
    )
```
